128 devices in a mesh: slab: 32 (over y, z, core), col: 4 (over x).
Axes of the slice: x: 4, y: 4, z: 4, core: 2. Of those that a mesh axis runs over, the one named last changes fastest.
Arguments:
- classes: int32 [256, 512], P(('slab', 'col')), may hold values from 0 to 15
- across_coeff: float32 [16], replicated, may hold values from 0.5 to 5
- along_coeff: float32 [16], replicated, may hold values from 0.05 to 0.5
Outputs:
- piece_maps: float32 [131072, 1024], P(('slab', 'col'))
- root_map: float32 [1024, 1024], P(('slab', 'col'))
The draws below stay inside these ranges and needn't reach their ends.
All inputs are finite; a program needn't handle non-finite values.
Results may differ from the reference program's by a relative error of at most 0.0003.
Values sent between devices are 32-bit elements; how exact they have to be, the bound alone decides.
No kernel may reach another device: no remote copies, remote signals or barrier semaphores. Data moves between devices by JAX's collectives and lax.ppermute only.
A program may use at most 128 MiB of HBM per device.

```python
import math
from functools import partial
import jax
import jax.numpy as jnp
from jax import lax

E = 512
C = 2
CLASSES = 16
PIECES = 128
COLS = 256


def plant(array, rng, low, high):
    spot = [jax.random.randint(jax.random.fold_in(rng, axis), (), 0, length) for axis, length in enumerate(array.shape)]
    widest = array.shape.index(max(array.shape))
    neighbour = spot[:widest] + [(spot[widest] + 1) % array.shape[widest]] + spot[widest + 1:]
    return array.at[tuple(spot)].set(low).at[tuple(neighbour)].set(high)


def setup_inputs(seed: int = 0) -> dict:
    key_of = jax.random.split(jax.random.key(seed), 4)
    classes = plant(jax.random.randint(key_of[0], (COLS, E), 0, CLASSES), jax.random.fold_in(key_of[0], 1), 0, CLASSES - 1).astype(jnp.int32)
    across_coeff = jnp.clip(jnp.exp(jax.random.uniform(key_of[1], (CLASSES,), jnp.float32, math.log(0.5), math.log(5.0))), 0.5, 5.0)
    along_coeff = jnp.clip(jnp.exp(jax.random.uniform(key_of[2], (CLASSES,), jnp.float32, math.log(0.05), math.log(0.5))), 0.05, 0.5)
    return {"classes": classes, "across_coeff": across_coeff, "along_coeff": along_coeff}


def lookup(classes, values_table):
    levels = jnp.arange(values_table.shape[0], dtype=jnp.int32)
    matches = classes[:, None, :] == levels[None, :, None]
    return jnp.sum(jnp.where(matches, values_table[None, :, None], 0.0), axis=1)

def strip_map(along_col, across_col):
    half_size = along_col.shape[0]
    row_index = lax.broadcasted_iota(jnp.int32, (half_size, half_size), 0)
    col_index = lax.broadcasted_iota(jnp.int32, (half_size, half_size), 1)
    shifted = jnp.roll(along_col, 1)
    vertical = jnp.where(row_index == col_index, (along_col + shifted)[None, :], 0.0)
    vertical = vertical - jnp.where(col_index == (row_index + 1) % half_size, along_col[:, None], 0.0)
    vertical = vertical - jnp.where(row_index == (col_index + 1) % half_size, along_col[None, :], 0.0)
    across_diag = jnp.where(row_index == col_index, across_col[None, :], 0.0)
    upper_rows = jnp.concatenate([vertical + across_diag, -across_diag], axis=1)
    lower_rows = jnp.concatenate([-across_diag, across_diag], axis=1)
    return jnp.concatenate([upper_rows, lower_rows], axis=0)

def quarters(full_map):
    half_size = full_map.shape[0] // 2
    return (full_map[:half_size, :half_size], full_map[:half_size, half_size:], full_map[half_size:, :half_size], full_map[half_size:, half_size:])

def merge_blocks(left_upper, left_lower_left, left_lower, right_upper, right_upper_right, right_lower):
    half_size = left_upper.shape[0]
    factor = jnp.linalg.cholesky(left_lower + right_upper)
    coupled = jnp.concatenate([left_lower_left, right_upper_right], axis=1)
    scaled = lax.linalg.triangular_solve(factor, coupled, left_side=True, lower=True)
    product = lax.dot_general(scaled, scaled, (((0,), (0,)), ((), ())), precision=lax.Precision.HIGHEST)
    zero_block = jnp.zeros((half_size, half_size), left_upper.dtype)
    diagonal_part = jnp.concatenate([jnp.concatenate([left_upper, zero_block], axis=1), jnp.concatenate([zero_block, right_lower], axis=1)], axis=0)
    return diagonal_part - product

def merge_maps(left_map, right_map):
    left_upper, left_upper_right, left_lower_left, left_lower = quarters(left_map)
    right_upper, right_upper_right, right_lower_left, right_lower = quarters(right_map)
    return merge_blocks(left_upper, left_lower_left, left_lower, right_upper, right_upper_right, right_lower)

def build_piece(piece_classes, across_coeff, along_coeff):
    across = lookup(piece_classes, across_coeff)
    along = lookup(piece_classes, along_coeff)
    own_map = strip_map(along[0], across[0])
    for column in range(1, piece_classes.shape[0]):
        own_map = merge_maps(own_map, strip_map(along[column], across[column]))
    return own_map

def advance(running, own_map):
    return (merge_maps(running, own_map), None)

def reference(classes, across_coeff, along_coeff):
    grouped = classes.reshape(PIECES, C, E)
    pieces = lax.map(partial(build_piece, across_coeff=across_coeff, along_coeff=along_coeff), grouped)
    root_map, unused = lax.scan(advance, pieces[0], pieces[1:])
    return (pieces.reshape(PIECES * 2 * E, 2 * E), root_map)
```

```python
import functools
import jax
import jax.numpy as jnp
from jax import lax
from jax.experimental import pallas as pl
from jax.experimental.pallas import tpu as pltpu
from jax.sharding import PartitionSpec as P

F32 = jnp.float32
BF16 = jnp.bfloat16
VMEM_BYTES = 56 * 1024 * 1024
PLAIN = (((1,), (0,)), ((), ()))
LEFT_T = (((0,), (0,)), ((), ()))


def split(x):
    high = x.astype(BF16)
    return high, (x - high.astype(F32)).astype(BF16)


def dot3(left, right, dims=PLAIN):
    lh, ll = split(left)
    rh, rl = split(right)
    dot = functools.partial(lax.dot_general, dimension_numbers=dims, preferred_element_type=F32)
    return dot(lh, rh) + (dot(lh, rl) + dot(ll, rh))


def inverse_small(A, start=0):
    n = A.shape[0]
    lane = lax.broadcasted_iota(jnp.int32, (1, n), 1)
    sub = lax.broadcasted_iota(jnp.int32, (n, 1), 0)
    for k in range(start, n):
        row = A[k : k + 1, :]
        col = A[:, k : k + 1]
        inv = 1.0 / A[k : k + 1, k : k + 1]
        hit = lane == k
        r = jnp.where(hit, -inv, row * inv)
        A = jnp.where(sub == k, r, jnp.where(hit, 0.0, A) - col * r)
    if start:
        keep = (lane < start) | (sub < start)
        return jnp.where(keep, A, -A)
    return -A


def inverse_blocks(A_ref, n):
    lane = lax.broadcasted_iota(jnp.int32, (1, n), 1)

    def step(b, carry):
        at = pl.ds(pl.multiple_of(b * 128, 128), 128)
        row = A_ref[at, :]
        col = A_ref[:, at]
        pivot = inverse_small(A_ref[at, at])
        inside = (lane >= b * 128) & (lane < b * 128 + 128)
        scaled = dot3(pivot, row)
        wide = jnp.concatenate([pivot] * (n // 128), axis=1)
        scaled = jnp.where(inside, wide, scaled)
        A_ref[...] = jnp.where(inside, 0.0, A_ref[...]) - dot3(col, scaled)
        A_ref[at, :] = scaled
        return carry

    lax.fori_loop(0, n // 128, step, 0)


def pick(levels, table_ref):
    values = jnp.zeros(levels.shape, F32)
    for k in range(table_ref.shape[0]):
        values = jnp.where(levels == k, table_ref[k], values)
    return values


def piece_kernel(cls_ref, across_ref, along_ref, out_ref, cols_ref):
    E = cls_ref.shape[1]
    across = pick(cls_ref[...], across_ref)
    along = pick(cls_ref[...], along_ref)
    d0, d1 = across[0:1], across[1:2]
    v0, a = along[0:1], along[1:2]
    v0_prev, a_prev = jnp.roll(v0, 1, axis=1), jnp.roll(a, 1, axis=1)
    diag = d0 + d1 + a + a_prev
    down, up = diag, diag
    for _ in range(16):
        down = diag - a_prev * a_prev / jnp.roll(down, 1, axis=1)
        up = diag - a * a / jnp.roll(up, -1, axis=1)
    g = 1.0 / (down + up - diag)
    step_p = jnp.log(down / a)
    step_q = jnp.log(up / a_prev)
    ph = jnp.floor(step_p * 256.0 + 0.5) * (1.0 / 256.0)
    qh = jnp.floor(step_q * 256.0 + 0.5) * (1.0 / 256.0)
    steps = jnp.concatenate([ph, step_p - ph, qh, step_q - qh, d0, d1, d0, d1], axis=0)
    lane8 = lax.broadcasted_iota(jnp.int32, (8, E), 1)
    sums = steps
    width = 1
    while width < E:
        sums = sums + jnp.where(lane8 >= width, jnp.roll(sums, width, axis=1), 0.0)
        width *= 2
    total = sums[:, E - 1 : E]
    ph_before, pl_before = sums[0:1] - steps[0:1], sums[1:2] - steps[1:2]
    rows = jnp.concatenate([ph_before, pl_before, sums[2:4], d0, d1, d0, d1], axis=0)
    tall = jnp.concatenate([rows, jnp.zeros((120, E), F32)], axis=0)
    cols_ref[...] = tall.T
    pt_h, pt_l, qt_h, qt_l = total[0:1], total[1:2], total[2:3], total[3:4]
    wrap_p = 1.0 / (1.0 - jnp.exp(-(pt_h + pt_l)))
    wrap_q = 1.0 / (1.0 - jnp.exp(-(qt_h + qt_l)))
    R = 64
    lane = lax.broadcasted_iota(jnp.int32, (R, E), 1)
    sub = lax.broadcasted_iota(jnp.int32, (R, E), 0)

    def chunk(i, carry):
        at = pl.ds(pl.multiple_of(i * R, R), R)
        c = cols_ref[at, :]
        index = sub + i * R
        later, earlier = lane < index, index < lane
        p = (rows[0:1] - c[:, 0:1]) + jnp.where(later, pt_h, 0.0)
        p = p + ((rows[1:2] - c[:, 1:2]) + jnp.where(later, pt_l, 0.0))
        q = (c[:, 2:3] - rows[2:3]) + jnp.where(earlier, qt_h, 0.0)
        q = q + ((c[:, 3:4] - rows[3:4]) + jnp.where(earlier, qt_l, 0.0))
        same = lane == index
        G = g * (jnp.exp(-p) * wrap_p + jnp.exp(-q) * wrap_q - jnp.where(same, 1.0, 0.0))
        c0, c1 = c[:, 4:5], c[:, 5:6]
        G0, G1 = G * d0, G * d1
        after = lane == jnp.where(index == E - 1, 0, index + 1)
        before = lane == jnp.where(index == 0, E - 1, index - 1)
        top = jnp.where(same, d0 + v0 + v0_prev, 0.0)
        top = top - jnp.where(after, v0_prev, 0.0) - jnp.where(before, v0, 0.0)
        out_ref[at, 0:E] = top - c0 * G0
        out_ref[at, E : 2 * E] = -(c0 * G1)
        low = pl.ds(pl.multiple_of(i * R + E, R), R)
        out_ref[low, 0:E] = -(c1 * G0)
        out_ref[low, E : 2 * E] = jnp.where(same, d1, 0.0) - c1 * G1
        return carry

    lax.fori_loop(0, E // R, chunk, 0)


def piece_map(classes, across_coeff, along_coeff):
    E = classes.shape[1]
    return pl.pallas_call(
        piece_kernel,
        out_shape=jax.ShapeDtypeStruct((2 * E, 2 * E), F32),
        in_specs=[
            pl.BlockSpec(memory_space=pltpu.VMEM),
            pl.BlockSpec(memory_space=pltpu.SMEM),
            pl.BlockSpec(memory_space=pltpu.SMEM),
        ],
        out_specs=pl.BlockSpec(memory_space=pltpu.VMEM),
        scratch_shapes=[pltpu.VMEM((E, 128), F32)],
        compiler_params=pltpu.CompilerParams(vmem_limit_bytes=VMEM_BYTES),
        cost_estimate=pl.CostEstimate(flops=20_000_000, bytes_accessed=16 << 20, transcendentals=0),
        name="piece_map",
    )(classes, across_coeff, along_coeff)


N = 32


def block_kernel(cls_ref, across_ref, along_ref, out_ref, maps, vals, packs):
    lane1 = lax.broadcasted_iota(jnp.int32, (1, 128), 1)
    lane = lax.broadcasted_iota(jnp.int32, (128, 128), 1)
    sub = lax.broadcasted_iota(jnp.int32, (128, 128), 0)
    across = pick(cls_ref[...], across_ref)
    along = pick(cls_ref[...], along_ref)
    vals[0:32, :] = across
    vals[32:64, :] = along
    vals[64:96, :] = jnp.where(lane1 % N == 0, 0.0, jnp.roll(along, 1, axis=1))
    vals[96:128, :] = jnp.broadcast_to(along[:, N - 1 : N], (N, 128))
    low = jnp.where(sub < N, sub, -1000)
    is_diag = low == lane
    is_after = (low + 1 == lane) & (lane < N)
    is_before = (low == lane + 1)
    mid_diag = (sub == lane) & (sub >= N) & (sub < 2 * N)
    cross = ((low + N == lane) & (lane < 2 * N)) | ((lane < N) & (sub == lane + N))

    def first(c, carry):
        ac = vals[pl.ds(c, 1), :]
        al = vals[pl.ds(c + 32, 1), :]
        al_prev = vals[pl.ds(c + 64, 1), :]
        al_last = vals[pl.ds(c + 96, 1), :]
        m = jnp.where(is_diag, ac + al + al_prev, 0.0)
        m = m - jnp.where(is_after, al_prev, 0.0) - jnp.where(is_before, al, 0.0)
        m = m + jnp.where(mid_diag, ac, 0.0) - jnp.where(cross, ac, 0.0)
        slot = 3 * N + c
        ends = ((sub == N - 1) & (lane == slot)) | ((sub == slot) & (lane == N - 1))
        m = m - jnp.where(ends, al_last, 0.0)
        m = m + jnp.where((sub == slot) & (lane == slot), al_last, 0.0)
        maps[c] = m
        return carry

    lax.fori_loop(0, N, first, 0)

    seg1 = lane1 // N
    seg = lane // N
    subN = lax.broadcasted_iota(jnp.int32, (N, 128), 0)
    laneN = lax.broadcasted_iota(jnp.int32, (N, 128), 1)
    row_R = (sub >= N) & (sub < 2 * N)
    row_L = sub < N
    col_R = (lane >= N) & (lane < 2 * N)
    col_L = lane < N
    colR1 = (lane1 >= N) & (lane1 < 2 * N)
    colL1 = lane1 < N
    drop_a = row_R | col_R
    drop_b = row_L | col_L
    edge = (subN == 0) | (laneN % N == 0)
    corner = (subN == 0) & (laneN % N == 0)
    blockdiag = (sub // N) == seg

    count = N // 2
    span = 1
    while count >= 1:
        quads = max(count // 4, 1)
        live = min(count, 4)

        def gather(q, carry, live=live):
            packed = jnp.zeros((N, 128), F32)
            for i in range(live):
                a_rows = maps[q * 8 + 2 * i, N : 2 * N, :]
                b_rows = maps[q * 8 + 2 * i + 1, 0:N, :]
                piece = jnp.where(colR1, a_rows, 0.0)
                piece = jnp.roll(piece, N * (i - 1), axis=1) if i != 1 else piece
                other = jnp.where(colL1, b_rows, 0.0)
                other = jnp.roll(other, N * i, axis=1) if i else other
                packed = packed + piece + other
            packs[q] = jnp.where(corner, 1.0, jnp.where(edge, 0.0, packed))
            return carry

        lax.fori_loop(0, quads, gather, 0)

        def pivots(k, carry, quads=quads):
            index = seg1 * N + k
            wide = jnp.broadcast_to(index, (N, 128))
            out = []
            for A in carry:
                row = jnp.sum(jnp.where(subN == k, A, 0.0), axis=0, keepdims=True)
                row = jnp.broadcast_to(row, (8, 128))
                d = jnp.take_along_axis(row, wide[:8], axis=1)[:1]
                col = jnp.take_along_axis(A, wide, axis=1)
                inv = 1.0 / d
                hit = (lane1 % N) == k
                r = jnp.where(hit, -inv, row[:1] * inv)
                out.append(jnp.where(subN == k, r, jnp.where(hit, 0.0, A) - col * r))
            return tuple(out)

        done = lax.fori_loop(1, N, pivots, tuple(packs[q] for q in range(quads)))
        for q in range(quads):
            packs[q] = jnp.where(edge, 0.0, -done[q])

        def merge(q, carry, live=live, span=span):
            G = packs[q]
            G4 = jnp.where(blockdiag, jnp.concatenate([G] * 4, axis=0), 0.0)
            sides = []
            fronts = []
            for i in range(4):
                if i >= live:
                    sides.append(jnp.zeros((N, 128), F32))
                    continue
                a = maps[q * 8 + 2 * i]
                b = maps[q * 8 + 2 * i + 1]
                t = 2 * N + (q * 8 + 2 * i + 1) * span
                a_rows, b_rows = a[N : 2 * N], b[0:N]
                W = jnp.where(colR1, 0.0, a_rows) + jnp.where(colL1, 0.0, b_rows)
                a_col, b_col = a[:, N : N + 1], b[:, 0:1]
                at_lane = lane1 == t
                into = a_col[N : 2 * N] + b_col[0:N]
                w_row = W[0:1]
                W = W + jnp.where(at_lane, into, 0.0)
                W = jnp.where(subN == 0, 0.0, W)
                F = jnp.where(drop_a, 0.0, a) + jnp.where(drop_b, 0.0, b)
                kept_col = jnp.where(row_R[:, :1], 0.0, a_col) + jnp.where(row_L[:, :1], 0.0, b_col)
                F = F + jnp.where(at_lane, kept_col, 0.0)
                F = F + jnp.where(sub == t, w_row + jnp.where(at_lane, into[0:1], 0.0), 0.0)
                sides.append(W)
                fronts.append(F)
            stack = jnp.concatenate(sides, axis=0)
            X = dot3(G4, stack)
            for i in range(live):
                part = dot3(sides[i], X[i * N : (i + 1) * N], LEFT_T)
                maps[q * 4 + i] = fronts[i] - part
            return carry

        lax.fori_loop(0, quads, merge, 0)
        count //= 2
        span *= 2
    out_ref[...] = maps[0]


def block_map(cells, across_coeff, along_coeff):
    return pl.pallas_call(
        block_kernel,
        out_shape=jax.ShapeDtypeStruct((128, 128), F32),
        in_specs=[
            pl.BlockSpec(memory_space=pltpu.VMEM),
            pl.BlockSpec(memory_space=pltpu.SMEM),
            pl.BlockSpec(memory_space=pltpu.SMEM),
        ],
        out_specs=pl.BlockSpec(memory_space=pltpu.VMEM),
        scratch_shapes=[
            pltpu.VMEM((N, 128, 128), F32),
            pltpu.VMEM((128, 128), F32),
            pltpu.VMEM((4, N, 128), F32),
        ],
        compiler_params=pltpu.CompilerParams(vmem_limit_bytes=VMEM_BYTES),
        name="block_map",
    )(cells, across_coeff, along_coeff)


def merge_kernel(s, x, flip, closing, second_ref, own_ref, recv_ref, out_ref, W_ref, A_ref, X_ref):
    second = second_ref[0] == 1
    offsets = {"S1": (0, s), "S2": (s, s), "X": (2 * s, x), "Y": (2 * s + x, x)}

    def block(which, rows, cols):
        (r, nr), (c, nc) = offsets[rows], offsets[cols]
        own = own_ref[r : r + nr, c : c + nc]
        recv = recv_ref[r : r + nr, c : c + nc]
        if which == "a":
            return jnp.where(second, recv, own)
        return jnp.where(second, own, recv)

    K = out_ref.shape[0]
    E = A_ref.shape[0]
    if closing:
        place = {"S1": 0, "S2": 2 * s}
        kept = {"a": {"S1": 0, "S2": 2 * s}, "b": {"S1": s, "S2": 3 * s}}
        gone = {"a": {"Y": 0, "X": x}, "b": {"X": 0, "Y": x}}
    else:
        sides, ends = (2 * x, 0) if flip else (0, 4 * s)
        kept = {
            "a": {"S1": sides, "S2": sides + 2 * s, "X": ends},
            "b": {"S1": sides + s, "S2": sides + 3 * s, "Y": ends + x},
        }
        gone = {"a": {"Y": 0}, "b": {"X": 0}}

    out_ref[...] = jnp.zeros_like(out_ref)
    for which in "ab":
        for rows, r in kept[which].items():
            for cols, c in kept[which].items():
                nr, nc = offsets[rows][1], offsets[cols][1]
                out_ref[r : r + nr, c : c + nc] += block(which, rows, cols)
    A_ref[...] = jnp.zeros_like(A_ref)
    W_ref[...] = jnp.zeros_like(W_ref)
    for which in "ab":
        for rows, r in gone[which].items():
            for cols, c in gone[which].items():
                A_ref[r : r + x, c : c + x] += block(which, rows, cols)
            for cols, c in kept[which].items():
                W_ref[r : r + x, c : c + offsets[cols][1]] += block(which, rows, cols)
    folds = [(0, kept["b"]["S1"])]
    if closing:
        folds.append((x, kept["a"]["S1"]))
    rowE = lax.broadcasted_iota(jnp.int32, (E, 1), 0)
    for e, t in folds:
        tb = t // 128 * 128
        tw = min(128, K - tb)
        lane = lax.broadcasted_iota(jnp.int32, (1, tw), 1)
        hit = lane == t - tb
        for which in "ab":
            for cols, c in gone[which].items():
                if c == e:
                    for rows, r in kept[which].items():
                        nr = offsets[rows][1]
                        vec = block(which, rows, cols)[:, 0:1]
                        out_ref[r : r + nr, tb : tb + tw] += jnp.where(hit, vec, 0.0)
        out_ref[t : t + 1, :] += W_ref[e : e + 1, :]
        into = A_ref[:, e : e + 1]
        out_ref[t : t + 1, tb : tb + tw] += jnp.where(hit, into[e : e + 1], 0.0)
        W_ref[:, tb : tb + tw] += jnp.where(hit, into, 0.0)
    laneE = lax.broadcasted_iota(jnp.int32, (1, E), 1)
    for e, t in folds:
        W_ref[e : e + 1, :] = jnp.zeros((1, K), F32)
        corner = (rowE == e) & (laneE == e)
        A_ref[...] = jnp.where(corner, 1.0, jnp.where((rowE == e) | (laneE == e), 0.0, A_ref[...]))
    if E <= 128:
        G = inverse_small(A_ref[...], start=1)
    else:
        inverse_blocks(A_ref, E)
        G = A_ref[...]
    X_ref[...] = dot3(G, W_ref[...])
    R = min(K, 256) if K % 256 == 0 else min(K, 128) if K % 128 == 0 else K
    if R == K:
        out_ref[...] = out_ref[...] - dot3(W_ref[...], X_ref[...], LEFT_T)
    else:

        def rows(i, carry):
            at = pl.ds(pl.multiple_of(i * R, R), R)
            out_ref[at, :] = out_ref[at, :] - dot3(W_ref[:, at], X_ref[...], LEFT_T)
            return carry

        lax.fori_loop(0, K // R, rows, 0)


def merged(own, recv, second, s, x, flip=False, closing=False):
    K = 4 * s if closing else 4 * s + 2 * x
    E = 2 * x if closing else x
    return pl.pallas_call(
        functools.partial(merge_kernel, s, x, flip, closing),
        out_shape=jax.ShapeDtypeStruct((K, K), F32),
        in_specs=[
            pl.BlockSpec(memory_space=pltpu.SMEM),
            pl.BlockSpec(memory_space=pltpu.VMEM),
            pl.BlockSpec(memory_space=pltpu.VMEM),
        ],
        out_specs=pl.BlockSpec(memory_space=pltpu.VMEM),
        scratch_shapes=[pltpu.VMEM((E, K), F32), pltpu.VMEM((E, E), F32), pltpu.VMEM((E, K), F32)],
        compiler_params=pltpu.CompilerParams(vmem_limit_bytes=VMEM_BYTES),
        name=f"merge_{E}_{K}",
    )(second, own, recv)


def interface_kernel(own_ref, recv_ref, pick_ref, out_ref, A_ref):
    A_ref[...] = own_ref[...] + recv_ref[...]
    inverse_blocks(A_ref, A_ref.shape[0])
    out_ref[...] = dot3(pick_ref[...], A_ref[...])


def interface(own, recv, picked):
    E = own.shape[0]
    vmem = pl.BlockSpec(memory_space=pltpu.VMEM)
    return pl.pallas_call(
        interface_kernel,
        out_shape=jax.ShapeDtypeStruct(picked.shape, F32),
        in_specs=[vmem] * 3,
        out_specs=vmem,
        scratch_shapes=[pltpu.VMEM((E, E), F32)],
        compiler_params=pltpu.CompilerParams(vmem_limit_bytes=VMEM_BYTES),
        cost_estimate=pl.CostEstimate(flops=20_000_000_000, bytes_accessed=64 << 20, transcendentals=0),
        name="interface",
    )(own, recv, picked)


def last_kernel(base_ref, Y_ref, own_ref, recv_ref, out_ref):
    E = own_ref.shape[0]
    out_ref[:, 0:E] = base_ref[...] - dot3(Y_ref[...], own_ref[...])
    out_ref[:, E : 2 * E] = -dot3(Y_ref[...], recv_ref[...])


def last_rows(base, Y, own, recv):
    vmem = pl.BlockSpec(memory_space=pltpu.VMEM)
    return pl.pallas_call(
        last_kernel,
        out_shape=jax.ShapeDtypeStruct((Y.shape[0], 2 * own.shape[0]), F32),
        in_specs=[vmem] * 4,
        out_specs=vmem,
        compiler_params=pltpu.CompilerParams(vmem_limit_bytes=VMEM_BYTES),
        name="last_rows",
    )(base, Y, own, recv)


def flipped(block, axis, mask):
    return lax.ppermute(block, axis, [(i, i ^ mask) for i in range(lax.axis_size(axis))])


def ordered(parts, index):
    low = (index & 1) == 1
    p0, p1 = jnp.where(low, parts[1], parts[0]), jnp.where(low, parts[0], parts[1])
    p2, p3 = jnp.where(low, parts[3], parts[2]), jnp.where(low, parts[2], parts[3])
    high = (index & 2) == 2
    return [jnp.where(high, p2, p0), jnp.where(high, p3, p1), jnp.where(high, p0, p2), jnp.where(high, p1, p3)]


def gathered_cells(classes):
    x = lax.axis_index("col")
    g = lax.axis_index("slab") & 3
    parts = [classes] + [flipped(classes, "col", k) for k in (1, 2, 3)]
    strip = jnp.concatenate(ordered(parts, x), axis=0)

    def share(k):
        to = g ^ k
        start = ((to & 1) * 8 + (to >> 1) * 4 + x) * N
        return lax.dynamic_slice_in_dim(strip, start, N, axis=1)

    parts = [share(0)] + [flipped(share(k), "slab", k) for k in (1, 2, 3)]
    return jnp.concatenate(ordered(parts, g), axis=0)


def local(classes, across_coeff, along_coeff):
    E = classes.shape[1]
    slab, col = lax.axis_index("slab"), lax.axis_index("col")
    core = slab & 1

    def bit(index, mask):
        return jnp.where((index & mask) != 0, 1, 0).astype(jnp.int32).reshape(1)

    cells = gathered_cells(classes)
    m = block_map(jnp.concatenate([cells] * 4, axis=1), across_coeff, along_coeff)
    pieces = piece_map(classes, across_coeff, along_coeff)
    m = merged(m, flipped(m, "col", 1), bit(col, 1), 32, 32, flip=True)
    m = merged(m, flipped(m, "slab", 4), bit(slab, 4), 32, 64, flip=True)
    m = merged(m, flipped(m, "col", 2), bit(col, 2), 64, 64, flip=True)
    m = merged(m, flipped(m, "slab", 8), bit(slab, 8), 64, 128, flip=True)
    m = merged(m, flipped(m, "slab", 2), bit(slab, 2), 128, 128)
    m = merged(m, flipped(m, "slab", 1), bit(slab, 1), 256, 128, closing=True)
    right = (slab & 16) != 0
    h = E // 2

    def swapped(block):
        mine = lax.dynamic_slice_in_dim(block, core * h, h, 0)
        came = flipped(mine, "slab", 16)
        other = flipped(came, "slab", 1)
        return jnp.where(core == 0, jnp.concatenate([came, other]), jnp.concatenate([other, came]))

    inner = jnp.where(right, m[:E, :E], m[E:, E:])
    reach = jnp.where(right, m[:E, E:], m[E:, :E])
    far = jnp.where(right, m[E:, E:], m[:E, :E])
    back = jnp.where(right, m[E:, :E], m[:E, E:])
    share = 2 * E // (lax.axis_size("slab") * lax.axis_size("col"))
    at = ((slab & 15) * lax.axis_size("col") + col) * share
    picked = lax.dynamic_slice_in_dim(back, at, share, 0)
    base = lax.dynamic_slice_in_dim(far, at, share, 0)
    inner_recv = swapped(inner)
    Y = interface(inner, inner_recv, picked)
    rows = last_rows(base, Y, reach, swapped(reach))
    halves = jnp.where(right, jnp.concatenate([rows[:, E:], rows[:, :E]], axis=1), rows)
    return (pieces, halves)


def solution(mesh):
    placed = P(("slab", "col"), None)
    return jax.shard_map(
        local,
        mesh=mesh,
        in_specs=(placed, P(), P()),
        out_specs=(placed, placed),
        check_vma=False,
    )
```

```python
import functools
import jax
import jax.numpy as jnp
from jax import lax
from jax.experimental import pallas as pl
from jax.experimental.pallas import tpu as pltpu
from jax.sharding import PartitionSpec as P

F32 = jnp.float32
BF16 = jnp.bfloat16
PLAIN = (((1,), (0,)), ((), ()))
LEFT_T = (((0,), (0,)), ((), ()))


def split(x):
    high = x.astype(BF16)
    return high, (x - high.astype(F32)).astype(BF16)


def dot3(left, right, dims=PLAIN):
    lh, ll = split(left)
    rh, rl = split(right)
    dot = functools.partial(lax.dot_general, dimension_numbers=dims, preferred_element_type=F32)
    return dot(lh, rh) + (dot(lh, rl) + dot(ll, rh))


def small_inverse(s):
    size = max(i for i, _ in s) + 1
    if size == 1:
        return {(0, 0): 1.0 / s[0, 0]}
    if size == 2:
        a, b, d = s[0, 0], s[0, 1], s[1, 1]
        r = 1.0 / (a * d - b * b)
        return {(0, 0): d * r, (0, 1): -(b * r), (1, 1): a * r}
    h = size // 2
    both = range(h)

    def at(m, i, j):
        return m[min(i, j), max(i, j)]

    def total(terms):
        terms = list(terms)
        out = terms[0]
        for term in terms[1:]:
            out = out + term
        return out

    A = small_inverse({(i, j): s[i, j] for i in both for j in range(i, h)})
    X = {(i, j): total(at(A, i, k) * s[k, h + j] for k in both) for i in both for j in both}
    S = {(i, j): s[h + i, h + j] - total(s[k, h + i] * X[k, j] for k in both) for i in both for j in range(i, h)}
    S = small_inverse(S)
    Y = {(i, j): -total(X[i, k] * at(S, k, j) for k in both) for i in both for j in both}
    out = {}
    for i in both:
        for j in range(i, h):
            out[i, j] = A[i, j] - total(Y[i, k] * X[j, k] for k in both)
            out[h + i, h + j] = S[i, j]
        for j in both:
            out[i, h + j] = Y[i, j]
    return out


def panel_sweep(tiles, n, size, spread, lane):
    shape = tiles[0].shape
    sub = lax.broadcasted_iota(jnp.int32, shape, 0)
    tiles = list(tiles)
    groups = len(tiles) // (n // 8)
    per = n // 8
    for k in range(0, n, size):
        pt, ps = k // 8, k % 8
        inside = (lane >= k) & (lane < k + size)
        units = [jnp.where(lane == k + j, 1.0, 0.0) for j in range(size)]
        for q in range(groups):
            mine = tiles[q * per : (q + 1) * per]
            C = [[spread(t, k + j) for t in mine] for j in range(size)]
            R = [jnp.broadcast_to(mine[pt][ps + j : ps + j + 1, :], shape) for j in range(size)]
            s = {}
            for i in range(size):
                for j in range(i, size):
                    s[i, j] = jnp.broadcast_to(C[j][pt][ps + i : ps + i + 1, :], shape)
            G = small_inverse(s)
            R = [jnp.where(inside, units[j], R[j]) for j in range(size)]
            scaled = []
            for i in range(size):
                row = G[0, i] * R[0]
                for j in range(1, size):
                    row = row + G[min(i, j), max(i, j)] * R[j]
                scaled.append(row)
            for t in range(per):
                change = C[0][t] * scaled[0]
                for j in range(1, size):
                    change = change + C[j][t] * scaled[j]
                new = jnp.where(inside, 0.0, mine[t]) - change
                if t == pt:
                    for j in range(size):
                        new = jnp.where(sub == ps + j, scaled[j], new)
                tiles[q * per + t] = new
    return tiles


def inverse_small(A, size):
    n = A.shape[0]
    lane = lax.broadcasted_iota(jnp.int32, (8, n), 1)
    tiles = [A[i : i + 8, :] for i in range(0, n, 8)]

    def spread(tile, k):
        return jnp.broadcast_to(tile[:, k : k + 1], (8, n))

    return jnp.concatenate(panel_sweep(tiles, n, size, spread, lane), axis=0)


def inverse_blocks(A_ref, n):
    lane = lax.broadcasted_iota(jnp.int32, (1, n), 1)

    def step(b, carry):
        at = pl.ds(pl.multiple_of(b * 128, 128), 128)
        row = A_ref[at, :]
        col = A_ref[:, at]
        pivot = inverse_small(A_ref[at, at], 8)
        inside = (lane >= b * 128) & (lane < b * 128 + 128)
        scaled = dot3(pivot, row)
        wide = jnp.concatenate([pivot] * (n // 128), axis=1)
        scaled = jnp.where(inside, wide, scaled)
        A_ref[...] = jnp.where(inside, 0.0, A_ref[...]) - dot3(col, scaled)
        A_ref[at, :] = scaled
        return carry

    lax.fori_loop(0, n // 128, step, 0)


def pick(levels, table_ref):
    values = jnp.zeros(levels.shape, F32)
    for k in range(table_ref.shape[0]):
        values = jnp.where(levels == k, table_ref[k], values)
    return values


def piece_kernel(cls_ref, across_ref, along_ref, out_ref, cols_ref):
    E = cls_ref.shape[1]
    across = pick(cls_ref[...], across_ref)
    along = pick(cls_ref[...], along_ref)
    d0, d1 = across[0:1], across[1:2]
    v0, a = along[0:1], along[1:2]
    v0_prev, a_prev = jnp.roll(v0, 1, axis=1), jnp.roll(a, 1, axis=1)
    diag = d0 + d1 + a + a_prev
    down, up = diag, diag
    for _ in range(16):
        down = diag - a_prev * a_prev / jnp.roll(down, 1, axis=1)
        up = diag - a * a / jnp.roll(up, -1, axis=1)
    g = 1.0 / (down + up - diag)
    step_p = jnp.log(down / a)
    step_q = jnp.log(up / a_prev)
    ph = jnp.floor(step_p * 256.0 + 0.5) * (1.0 / 256.0)
    qh = jnp.floor(step_q * 256.0 + 0.5) * (1.0 / 256.0)
    steps = jnp.concatenate([ph, step_p - ph, qh, step_q - qh, d0, d1, d0, d1], axis=0)
    lane8 = lax.broadcasted_iota(jnp.int32, (8, E), 1)
    sums = steps
    width = 1
    while width < E:
        sums = sums + jnp.where(lane8 >= width, jnp.roll(sums, width, axis=1), 0.0)
        width *= 2
    total = sums[:, E - 1 : E]
    ph_before, pl_before = sums[0:1] - steps[0:1], sums[1:2] - steps[1:2]
    rows = jnp.concatenate([ph_before, pl_before, sums[2:4], d0, d1, d0, d1], axis=0)
    tall = jnp.concatenate([rows, jnp.zeros((120, E), F32)], axis=0)
    cols_ref[...] = tall.T
    pt_h, pt_l, qt_h, qt_l = total[0:1], total[1:2], total[2:3], total[3:4]
    wrap_p = 1.0 / (1.0 - jnp.exp(-(pt_h + pt_l)))
    wrap_q = 1.0 / (1.0 - jnp.exp(-(qt_h + qt_l)))
    R = 64
    lane = lax.broadcasted_iota(jnp.int32, (R, E), 1)
    sub = lax.broadcasted_iota(jnp.int32, (R, E), 0)

    def chunk(i, carry):
        at = pl.ds(pl.multiple_of(i * R, R), R)
        c = cols_ref[at, :]
        index = sub + i * R
        later, earlier = lane < index, index < lane
        p = (rows[0:1] - c[:, 0:1]) + jnp.where(later, pt_h, 0.0)
        p = p + ((rows[1:2] - c[:, 1:2]) + jnp.where(later, pt_l, 0.0))
        q = (c[:, 2:3] - rows[2:3]) + jnp.where(earlier, qt_h, 0.0)
        q = q + ((c[:, 3:4] - rows[3:4]) + jnp.where(earlier, qt_l, 0.0))
        same = lane == index
        G = g * (jnp.exp(-p) * wrap_p + jnp.exp(-q) * wrap_q - jnp.where(same, 1.0, 0.0))
        c0, c1 = c[:, 4:5], c[:, 5:6]
        G0, G1 = G * d0, G * d1
        after = lane == jnp.where(index == E - 1, 0, index + 1)
        before = lane == jnp.where(index == 0, E - 1, index - 1)
        top = jnp.where(same, d0 + v0 + v0_prev, 0.0)
        top = top - jnp.where(after, v0_prev, 0.0) - jnp.where(before, v0, 0.0)
        out_ref[at, 0:E] = top - c0 * G0
        out_ref[at, E : 2 * E] = -(c0 * G1)
        low = pl.ds(pl.multiple_of(i * R + E, R), R)
        out_ref[low, 0:E] = -(c1 * G0)
        out_ref[low, E : 2 * E] = jnp.where(same, d1, 0.0) - c1 * G1
        return carry

    lax.fori_loop(0, E // R, chunk, 0)


def piece_map(classes, across_coeff, along_coeff):
    E = classes.shape[1]
    return pl.pallas_call(
        piece_kernel,
        out_shape=jax.ShapeDtypeStruct((2 * E, 2 * E), F32),
        in_specs=[
            pl.BlockSpec(memory_space=pltpu.VMEM),
            pl.BlockSpec(memory_space=pltpu.SMEM),
            pl.BlockSpec(memory_space=pltpu.SMEM),
        ],
        out_specs=pl.BlockSpec(memory_space=pltpu.VMEM),
        scratch_shapes=[pltpu.VMEM((E, 128), F32)],
        compiler_params=pltpu.CompilerParams(vmem_limit_bytes=12 << 20),
        cost_estimate=pl.CostEstimate(flops=20_000_000, bytes_accessed=16 << 20, transcendentals=0),
        name="piece_map",
    )(classes, across_coeff, along_coeff)


N = 32


def block_kernel(cls_ref, across_ref, along_ref, out_ref, maps, vals, packs):
    lane1 = lax.broadcasted_iota(jnp.int32, (1, 128), 1)
    lane = lax.broadcasted_iota(jnp.int32, (128, 128), 1)
    sub = lax.broadcasted_iota(jnp.int32, (128, 128), 0)
    across = pick(cls_ref[...], across_ref)
    along = pick(cls_ref[...], along_ref)
    vals[0:32, :] = across
    vals[32:64, :] = along
    vals[64:96, :] = jnp.where(lane1 % N == 0, 0.0, jnp.roll(along, 1, axis=1))
    vals[96:128, :] = jnp.broadcast_to(along[:, N - 1 : N], (N, 128))
    low = jnp.where(sub < N, sub, -1000)
    is_diag = low == lane
    is_after = (low + 1 == lane) & (lane < N)
    is_before = (low == lane + 1)
    mid_diag = (sub == lane) & (sub >= N) & (sub < 2 * N)
    cross = ((low + N == lane) & (lane < 2 * N)) | ((lane < N) & (sub == lane + N))

    def first(c, carry):
        ac = vals[pl.ds(c, 1), :]
        al = vals[pl.ds(c + 32, 1), :]
        al_prev = vals[pl.ds(c + 64, 1), :]
        al_last = vals[pl.ds(c + 96, 1), :]
        m = jnp.where(is_diag, ac + al + al_prev, 0.0)
        m = m - jnp.where(is_after, al_prev, 0.0) - jnp.where(is_before, al, 0.0)
        m = m + jnp.where(mid_diag, ac, 0.0) - jnp.where(cross, ac, 0.0)
        slot = 3 * N + c
        ends = ((sub == N - 1) & (lane == slot)) | ((sub == slot) & (lane == N - 1))
        m = m - jnp.where(ends, al_last, 0.0)
        m = m + jnp.where((sub == slot) & (lane == slot), al_last, 0.0)
        maps[c] = m
        return carry

    lax.fori_loop(0, N, first, 0)

    seg1 = lane1 // N
    seg = lane // N
    subN = lax.broadcasted_iota(jnp.int32, (N, 128), 0)
    laneN = lax.broadcasted_iota(jnp.int32, (N, 128), 1)
    row_R = (sub >= N) & (sub < 2 * N)
    row_L = sub < N
    col_R = (lane >= N) & (lane < 2 * N)
    col_L = lane < N
    colR1 = (lane1 >= N) & (lane1 < 2 * N)
    colL1 = lane1 < N
    drop_a = row_R | col_R
    drop_b = row_L | col_L
    edge = (subN == 0) | (laneN % N == 0)
    corner = (subN == 0) & (laneN % N == 0)
    blockdiag = (sub // N) == seg

    lane8 = lax.broadcasted_iota(jnp.int32, (8, 128), 1)
    base8 = lane8 // N * N

    def spread(tile, k):
        return jnp.take_along_axis(tile, base8 + k, axis=1)

    count = N // 2
    span = 1
    while count >= 1:
        quads = max(count // 4, 1)
        live = min(count, 4)

        def gather(q, carry, live=live):
            packed = jnp.zeros((N, 128), F32)
            for i in range(live):
                a_rows = maps[q * 8 + 2 * i, N : 2 * N, :]
                b_rows = maps[q * 8 + 2 * i + 1, 0:N, :]
                piece = jnp.where(colR1, a_rows, 0.0)
                piece = jnp.roll(piece, N * (i - 1), axis=1) if i != 1 else piece
                other = jnp.where(colL1, b_rows, 0.0)
                other = jnp.roll(other, N * i, axis=1) if i else other
                packed = packed + piece + other
            packs[q] = jnp.where(corner, 1.0, jnp.where(edge, 0.0, packed))
            return carry

        lax.fori_loop(0, quads, gather, 0)

        done = panel_sweep(
            [packs[q, 8 * i : 8 * i + 8, :] for q in range(quads) for i in range(N // 8)], N, 4, spread, lane8 % N
        )
        for q in range(quads):
            for i in range(N // 8):
                packs[q, 8 * i : 8 * i + 8, :] = done[q * (N // 8) + i]

        def merge(q, carry, live=live, span=span):
            G = packs[q]
            G4 = jnp.where(blockdiag, jnp.concatenate([G] * 4, axis=0), 0.0)
            sides = []
            fronts = []
            for i in range(4):
                if i >= live:
                    sides.append(jnp.zeros((N, 128), F32))
                    continue
                a = maps[q * 8 + 2 * i]
                b = maps[q * 8 + 2 * i + 1]
                t = 2 * N + (q * 8 + 2 * i + 1) * span
                a_rows, b_rows = a[N : 2 * N], b[0:N]
                W = jnp.where(colR1, 0.0, a_rows) + jnp.where(colL1, 0.0, b_rows)
                a_col, b_col = a[:, N : N + 1], b[:, 0:1]
                at_lane = lane1 == t
                into = a_col[N : 2 * N] + b_col[0:N]
                w_row = W[0:1]
                W = W + jnp.where(at_lane, into, 0.0)
                W = jnp.where(subN == 0, 0.0, W)
                F = jnp.where(drop_a, 0.0, a) + jnp.where(drop_b, 0.0, b)
                kept_col = jnp.where(row_R[:, :1], 0.0, a_col) + jnp.where(row_L[:, :1], 0.0, b_col)
                F = F + jnp.where(at_lane, kept_col, 0.0)
                F = F + jnp.where(sub == t, w_row + jnp.where(at_lane, into[0:1], 0.0), 0.0)
                sides.append(W)
                fronts.append(F)
            stack = jnp.concatenate(sides, axis=0)
            X = dot3(G4, stack)
            for i in range(live):
                part = dot3(sides[i], X[i * N : (i + 1) * N], LEFT_T)
                maps[q * 4 + i] = fronts[i] - part
            return carry

        lax.fori_loop(0, quads, merge, 0)
        count //= 2
        span *= 2
    out_ref[...] = maps[0]


def block_map(cells, across_coeff, along_coeff):
    return pl.pallas_call(
        block_kernel,
        out_shape=jax.ShapeDtypeStruct((128, 128), F32),
        in_specs=[
            pl.BlockSpec(memory_space=pltpu.VMEM),
            pl.BlockSpec(memory_space=pltpu.SMEM),
            pl.BlockSpec(memory_space=pltpu.SMEM),
        ],
        out_specs=pl.BlockSpec(memory_space=pltpu.VMEM),
        scratch_shapes=[
            pltpu.VMEM((N, 128, 128), F32),
            pltpu.VMEM((128, 128), F32),
            pltpu.VMEM((4, N, 128), F32),
        ],
        compiler_params=pltpu.CompilerParams(vmem_limit_bytes=8 << 20),
        name="block_map",
    )(cells, across_coeff, along_coeff)


def pairs(n):
    return [(i, j) for i in range(n // 128) for j in range(i, n // 128)]


def pack(full_ref, packed_ref):
    for k, (i, j) in enumerate(pairs(full_ref.shape[0])):
        packed_ref[128 * k : 128 * k + 128, :] = full_ref[128 * i : 128 * i + 128, 128 * j : 128 * j + 128]


def unpack(packed_ref, full_ref):
    for k, (i, j) in enumerate(pairs(full_ref.shape[0])):
        block = packed_ref[128 * k : 128 * k + 128, :]
        full_ref[128 * i : 128 * i + 128, 128 * j : 128 * j + 128] = block
        if i != j:
            full_ref[128 * j : 128 * j + 128, 128 * i : 128 * i + 128] = block.T


def merge_kernel(s, x, flip, closing, packed_in, packed_out, order, *refs):
    flags_ref, own_ref, recv_ref = refs[:3]
    refs = list(refs[3:])
    if closing:
        inner_ref, reach_ref, edge_ref, send_ref = refs[:4]
        W_ref, A_ref, X_ref, out_ref = refs[4:8]
        rest = refs[8:]
    else:
        out_ref = refs.pop(0)
        packed_ref = refs.pop(0) if packed_out else None
        W_ref, A_ref, X_ref = refs[:3]
        rest = refs[3:]
    if packed_in:
        full_ref = rest[0]
        unpack(recv_ref, full_ref)
        recv_ref = full_ref
    second = flags_ref[0] == 1
    offsets = {"S1": (0, s), "S2": (s, s), "X": (2 * s, x), "Y": (2 * s + x, x)}

    def block(which, rows, cols):
        (r, nr), (c, nc) = offsets[rows], offsets[cols]
        own = own_ref[r : r + nr, c : c + nc]
        recv = recv_ref[r : r + nr, c : c + nc]
        if which == "a":
            return jnp.where(second, recv, own)
        return jnp.where(second, own, recv)

    K = out_ref.shape[0]
    E = A_ref.shape[0]
    if closing:
        kept = {"a": {"S1": 0, "S2": 2 * s}, "b": {"S1": s, "S2": 3 * s}}
        gone = {"a": {"Y": 0, "X": x}, "b": {"X": 0, "Y": x}}
    else:
        sides, ends = (2 * x, 0) if flip else (0, 4 * s)
        kept = {
            "a": {"S1": sides, "S2": sides + 2 * s, "X": ends},
            "b": {"S1": sides + s, "S2": sides + 3 * s, "Y": ends + x},
        }
        gone = {"a": {"Y": 0}, "b": {"X": 0}}

    out_ref[...] = jnp.zeros_like(out_ref)
    for which in "ab":
        for rows, r in kept[which].items():
            for cols, c in kept[which].items():
                nr, nc = offsets[rows][1], offsets[cols][1]
                out_ref[r : r + nr, c : c + nc] = block(which, rows, cols)
    if closing:
        A_ref[...] = jnp.zeros_like(A_ref)
        for which in "ab":
            for rows, r in gone[which].items():
                for cols, c in gone[which].items():
                    A_ref[r : r + x, c : c + x] += block(which, rows, cols)
    else:
        A_ref[...] = block("a", "Y", "Y") + block("b", "X", "X")
    W_ref[...] = jnp.zeros_like(W_ref)
    for which in "ab":
        for rows, r in gone[which].items():
            for cols, c in kept[which].items():
                W_ref[r : r + x, c : c + offsets[cols][1]] += block(which, rows, cols)
    rowE = lax.broadcasted_iota(jnp.int32, (E, 1), 0)
    laneE = lax.broadcasted_iota(jnp.int32, (1, E), 1)

    def fold(side):
        targets = [(0, kept["b"][side])]
        if closing:
            targets.append((x, kept["a"][side]))
        for e, t in targets:
            tb = t // 128 * 128
            tw = min(128, K - tb)
            lane = lax.broadcasted_iota(jnp.int32, (1, tw), 1)
            hit = lane == t - tb
            for which in "ab":
                for cols, c in gone[which].items():
                    if c == e:
                        for rows, r in kept[which].items():
                            nr = offsets[rows][1]
                            vec = block(which, rows, cols)[:, 0:1]
                            out_ref[r : r + nr, tb : tb + tw] += jnp.where(hit, vec, 0.0)
            out_ref[t : t + 1, :] += W_ref[e : e + 1, :]
            into = A_ref[:, e : e + 1]
            out_ref[t : t + 1, tb : tb + tw] += jnp.where(hit, into[e : e + 1], 0.0)
            W_ref[:, tb : tb + tw] += jnp.where(hit, into, 0.0)

    if order == "swapped":
        swapped = flags_ref[1] == 1
        pl.when(swapped)(lambda: fold("S2"))
        pl.when(jnp.logical_not(swapped))(lambda: fold("S1"))
    else:
        fold("S1")
    for e in (0, x) if closing else (0,):
        W_ref[e : e + 1, :] = jnp.zeros((1, K), F32)
        corner = (rowE == e) & (laneE == e)
        A_ref[...] = jnp.where(corner, 1.0, jnp.where((rowE == e) | (laneE == e), 0.0, A_ref[...]))
    if E <= 128:
        G = inverse_small(A_ref[...], 8 if E == 128 else 4)
    else:
        inverse_blocks(A_ref, E)
        G = A_ref[...]
    X_ref[...] = dot3(G, W_ref[...])
    if closing:
        h = K // 2
        q = h // 2
        core = flags_ref[0]
        for i in range(0, h, 256):
            new = out_ref[i : i + 256, :] - dot3(W_ref[:, i : i + 256], X_ref[...], LEFT_T)
            inner_ref[i : i + 256, :] = new[:, 0:h]
            reach_ref[i : i + 256, :] = new[:, h:K]
        row = flags_ref[2]
        at = pl.ds(pl.multiple_of(h + row // 128 * 128, 128), 128)
        out_ref[at, :] = out_ref[at, :] - dot3(W_ref[:, at], X_ref[...], LEFT_T)
        edge_ref[...] = out_ref[pl.ds(pl.multiple_of(h + row, 8), 8), :]
        half = pl.ds(pl.multiple_of(core * q, q), q)
        send_ref[0:q, :] = inner_ref[half, half]
        send_ref[q : q + q // 2, :] = inner_ref[pl.ds(pl.multiple_of(core * (q // 2), q // 2), q // 2), q:h]
        return
    R = min(K, 256) if K % 256 == 0 else min(K, 128) if K % 128 == 0 else K
    if R == K:
        out_ref[...] = out_ref[...] - dot3(W_ref[...], X_ref[...], LEFT_T)
    else:
        for i in range(0, K, R):
            out_ref[i : i + R, :] = out_ref[i : i + R, :] - dot3(W_ref[:, i : i + R], X_ref[...], LEFT_T)
    if order == "swap":

        @pl.when(flags_ref[1] == 1)
        def _():
            first, other = out_ref[0:x, :], out_ref[x : 2 * x, :]
            out_ref[0:x, :] = other
            out_ref[x : 2 * x, :] = first
            first, other = out_ref[:, 0:x], out_ref[:, x : 2 * x]
            out_ref[:, 0:x] = other
            out_ref[:, x : 2 * x] = first

    if packed_out:
        pack(out_ref, packed_ref)


SCALAR = pl.BlockSpec(memory_space=pltpu.SMEM)
WHOLE = pl.BlockSpec(memory_space=pltpu.VMEM)


def limit(mib):
    return pltpu.CompilerParams(vmem_limit_bytes=mib << 20)


def merged(flags, own, recv, s, x, flip=False, closing=False, packed_out=False, order="", mib=16):
    n = 2 * s + 2 * x
    K = 4 * s if closing else 4 * s + 2 * x
    E = 2 * x if closing else x
    packed_in = recv.shape != (n, n)
    scratch = [pltpu.VMEM((E, K), F32), pltpu.VMEM((E, E), F32), pltpu.VMEM((E, K), F32)]
    if closing:
        h = K // 2
        shapes = [(h, h), (h, h), (8, K), (h * 3 // 4, h // 2)]
        scratch.append(pltpu.VMEM((K, K), F32))
    else:
        shapes = [(K, K)]
        if packed_out:
            shapes.append((128 * len(pairs(K)), 128))
    if packed_in:
        scratch.append(pltpu.VMEM((n, n), F32))
    out = pl.pallas_call(
        functools.partial(merge_kernel, s, x, flip, closing, packed_in, packed_out, order),
        out_shape=[jax.ShapeDtypeStruct(shape, F32) for shape in shapes],
        in_specs=[SCALAR, WHOLE, WHOLE],
        out_specs=[WHOLE] * len(shapes),
        scratch_shapes=scratch,
        compiler_params=limit(mib),
        name=f"merge_{E}_{K}",
    )(flags, own, recv)
    return out if len(shapes) > 1 else out[0]


def interface_kernel(flags_ref, own_ref, near_ref, cross_ref, edge_ref, out_ref, A_ref):
    n = own_ref.shape[0]
    h = n // 2
    q = h // 2
    first = flags_ref[0] == 0
    near, cross = near_ref[...], cross_ref[...]
    low, high = jnp.where(first, near, cross), jnp.where(first, cross, near)
    off = jnp.concatenate([low[h:], high[h:]], axis=0)
    A_ref[0:h, 0:h] = own_ref[0:h, 0:h] + low[0:h]
    A_ref[h:n, h:n] = own_ref[h:n, h:n] + high[0:h]
    A_ref[0:h, h:n] = own_ref[0:h, h:n] + off
    A_ref[h:n, 0:h] = own_ref[h:n, 0:h] + off.T
    inverse_blocks(A_ref, n)
    out_ref[...] = dot3(edge_ref[:, 0:n], A_ref[...])


def interface(flags, own, near, cross, edge):
    E = own.shape[0]
    return pl.pallas_call(
        interface_kernel,
        out_shape=jax.ShapeDtypeStruct((8, E), F32),
        in_specs=[SCALAR] + [WHOLE] * 4,
        out_specs=WHOLE,
        scratch_shapes=[pltpu.VMEM((E, E), F32)],
        compiler_params=limit(16),
        cost_estimate=pl.CostEstimate(flops=30_000_000_000, bytes_accessed=64 << 20, transcendentals=0),
        name="interface",
    )(flags, own, near, cross, edge)


def last_kernel(flags_ref, edge_ref, Y_ref, own_ref, near_ref, cross_ref, out_ref):
    E = own_ref.shape[0]
    h = E // 2
    Y = Y_ref[...]
    mine = edge_ref[:, E : 2 * E] - dot3(Y, own_ref[...])
    first = flags_ref[0] == 0
    near, cross = near_ref[...], cross_ref[...]
    low, high = jnp.where(first, near, cross), jnp.where(first, cross, near)
    other = -(dot3(Y[:, 0:h], low) + dot3(Y[:, h:E], high))
    left = flags_ref[1] == 1
    out_ref[:, 0:E] = jnp.where(left, mine, other)
    out_ref[:, E : 2 * E] = jnp.where(left, other, mine)


def last_rows(flags, edge, Y, own, near, cross):
    return pl.pallas_call(
        last_kernel,
        out_shape=jax.ShapeDtypeStruct((Y.shape[0], 2 * own.shape[0]), F32),
        in_specs=[SCALAR] + [WHOLE] * 5,
        out_specs=WHOLE,
        compiler_params=limit(16),
        name="last_rows",
    )(flags, edge, Y, own, near, cross)


def flipped(block, axis, mask):
    return lax.ppermute(block, axis, [(i, i ^ mask) for i in range(lax.axis_size(axis))])


def ordered(parts, index):
    low = (index & 1) == 1
    p0, p1 = jnp.where(low, parts[1], parts[0]), jnp.where(low, parts[0], parts[1])
    p2, p3 = jnp.where(low, parts[3], parts[2]), jnp.where(low, parts[2], parts[3])
    high = (index & 2) == 2
    return [jnp.where(high, p2, p0), jnp.where(high, p3, p1), jnp.where(high, p0, p2), jnp.where(high, p1, p3)]


def gathered_cells(classes):
    x = lax.axis_index("col")
    g = lax.axis_index("slab") & 3
    parts = [classes] + [flipped(classes, "col", k) for k in (1, 2, 3)]
    strip = jnp.concatenate(ordered(parts, x), axis=0)

    def share(k):
        to = g ^ k
        start = ((to & 1) * 8 + (to >> 1) * 4 + x) * N
        return lax.dynamic_slice_in_dim(strip, start, N, axis=1)

    parts = [share(0)] + [flipped(share(k), "slab", k) for k in (1, 2, 3)]
    return jnp.concatenate(ordered(parts, g), axis=0)


def local(classes, across_coeff, along_coeff):
    E = classes.shape[1]
    slab, col = lax.axis_index("slab"), lax.axis_index("col")
    core = slab & 1

    def bit(index, mask):
        return jnp.where((index & mask) != 0, 1, 0).astype(jnp.int32).reshape(1)

    left = jnp.where((slab & 16) == 0, 1, 0).astype(jnp.int32).reshape(1)
    share = 2 * E // (lax.axis_size("slab") * lax.axis_size("col"))
    row = (((slab & 15) * lax.axis_size("col") + col) * share).astype(jnp.int32).reshape(1)

    def flags(index, mask):
        return jnp.concatenate([bit(index, mask), left, row])

    cells = gathered_cells(classes)
    m = block_map(jnp.concatenate([cells] * 4, axis=1), across_coeff, along_coeff)
    m = merged(flags(col, 1), m, flipped(m, "col", 1), 32, 32, flip=True)
    m, sent = merged(flags(slab, 4), m, flipped(m, "slab", 4), 32, 64, flip=True, packed_out=True)
    m, sent = merged(flags(col, 2), m, flipped(sent, "col", 2), 64, 64, flip=True, packed_out=True)
    m, sent = merged(flags(slab, 8), m, flipped(sent, "slab", 8), 64, 128, flip=True, packed_out=True, order="swap")
    held, sent = lax.optimization_barrier((classes, sent))
    recv = flipped(sent, "slab", 2)
    pieces = piece_map(held, across_coeff, along_coeff)
    recv, pieces = lax.optimization_barrier((recv, pieces))
    m, sent = merged(flags(slab, 2), m, recv, 128, 128, packed_out=True, order="swapped", mib=16)
    inner, reach, edge, sent = merged(
        flags(slab, 1), m, flipped(sent, "slab", 1), 256, 128, closing=True, order="swapped", mib=40
    )
    near = flipped(sent, "slab", 16)
    both = flags(slab, 1)
    half = E // 2
    part = lax.dynamic_slice_in_dim(reach, core * half, half, 0)
    Y = interface(both, inner, near, flipped(near, "slab", 1), edge)
    part, Y = lax.optimization_barrier((flipped(part, "slab", 16), Y))
    rows = last_rows(both, edge, Y, reach, part, flipped(part, "slab", 1))
    return (pieces, rows)


def solution(mesh):
    placed = P(("slab", "col"), None)
    return jax.shard_map(
        local,
        mesh=mesh,
        in_specs=(placed, P(), P()),
        out_specs=(placed, placed),
        check_vma=False,
    )
```

```python
import functools
import jax
import jax.numpy as jnp
from jax import lax
from jax.experimental import pallas as pl
from jax.experimental.pallas import tpu as pltpu
from jax.sharding import PartitionSpec as P

F32 = jnp.float32
BF16 = jnp.bfloat16
PLAIN = (((1,), (0,)), ((), ()))
LEFT_T = (((0,), (0,)), ((), ()))


def split(x):
    high = x.astype(BF16)
    return high, (x - high.astype(F32)).astype(BF16)


def dot3(left, right, dims=PLAIN):
    lh, ll = split(left)
    rh, rl = split(right)
    dot = functools.partial(lax.dot_general, dimension_numbers=dims, preferred_element_type=F32)
    return dot(lh, rh) + (dot(lh, rl) + dot(ll, rh))


def total(terms):
    terms = list(terms)
    out = terms[0]
    for term in terms[1:]:
        out = out + term
    return out


def small_inverse(s):
    size = max(i for i, _ in s) + 1
    if size == 1:
        return {(0, 0): 1.0 / s[0, 0]}
    if size == 2:
        a, b, d = s[0, 0], s[0, 1], s[1, 1]
        r = 1.0 / (a * d - b * b)
        return {(0, 0): d * r, (0, 1): -(b * r), (1, 1): a * r}
    h = size // 2
    both = range(h)

    def at(m, i, j):
        return m[min(i, j), max(i, j)]

    A = small_inverse({(i, j): s[i, j] for i in both for j in range(i, h)})
    X = {(i, j): total(at(A, i, k) * s[k, h + j] for k in both) for i in both for j in both}
    S = {(i, j): s[h + i, h + j] - total(s[k, h + i] * X[k, j] for k in both) for i in both for j in range(i, h)}
    S = small_inverse(S)
    Y = {(i, j): -total(X[i, k] * at(S, k, j) for k in both) for i in both for j in both}
    out = {}
    for i in both:
        for j in range(i, h):
            out[i, j] = A[i, j] - total(Y[i, k] * X[j, k] for k in both)
            out[h + i, h + j] = S[i, j]
        for j in both:
            out[i, h + j] = Y[i, j]
    return out


def panel_sweep(tiles, n, spread, lane, size=4):
    shape = tiles[0].shape
    sub = lax.broadcasted_iota(jnp.int32, shape, 0)
    tiles = list(tiles)
    per = n // 8
    groups = len(tiles) // per
    each = range(size)
    upper = [(i, j) for i in each for j in range(i, size)]

    def at(m, i, j):
        return m[min(i, j), max(i, j)]

    def row_of(tile, r):
        return jnp.broadcast_to(tile[r % 8 : r % 8 + 1, :], shape)

    blocks = [None] * groups
    for k in range(0, n, size):
        inside = (lane >= k) & (lane < k + size)
        units = [jnp.where(lane == k + j, 1.0, 0.0) for j in each]
        here, later = k // 8, (k + size) // 8
        for q in range(groups):
            mine = tiles[q * per : (q + 1) * per]
            C = [[spread(t, k + j) for t in mine] for j in each]
            R = [row_of(mine[here], k + j) for j in each]
            if k == 0:
                blocks[q] = {(i, j): row_of(C[j][here], i) for i, j in upper}
            G = small_inverse(blocks[q])
            if k + size < n:
                near = [spread(mine[here], k + size + j) for j in each]
                far = near if here == later else [spread(mine[later], k + size + j) for j in each]
                u = {(i, j): row_of(near[j], k + i) for i in each for j in each}
                v = {(i, j): row_of(far[j], k + size + i) for i, j in upper}
                T = {(i, j): total(at(G, i, m) * u[m, j] for m in each) for i in each for j in each}
                blocks[q] = {(i, j): v[i, j] - total(u[m, i] * T[m, j] for m in each) for i, j in upper}
            R = [jnp.where(inside, units[j], R[j]) for j in each]
            scaled = [total(at(G, i, j) * R[j] for j in each) for i in each]
            for t in range(per):
                new = jnp.where(inside, 0.0, mine[t]) - total(C[j][t] * scaled[j] for j in each)
                if t == here:
                    for j in each:
                        new = jnp.where(sub == (k + j) % 8, scaled[j], new)
                tiles[q * per + t] = new
    return tiles


def inverse_small(A):
    n = A.shape[0]
    lane = lax.broadcasted_iota(jnp.int32, (8, n), 1)
    tiles = [A[i : i + 8, :] for i in range(0, n, 8)]

    def spread(tile, k):
        return jnp.broadcast_to(tile[:, k : k + 1], (8, n))

    return jnp.concatenate(panel_sweep(tiles, n, spread, lane), axis=0)


def inverse_blocks(A_ref, n):
    lane = lax.broadcasted_iota(jnp.int32, (1, n), 1)

    def step(b, carry):
        at = pl.ds(pl.multiple_of(b * 128, 128), 128)
        row = A_ref[at, :]
        col = A_ref[:, at]
        pivot = inverse_small(A_ref[at, at])
        inside = (lane >= b * 128) & (lane < b * 128 + 128)
        scaled = dot3(pivot, row)
        wide = jnp.concatenate([pivot] * (n // 128), axis=1)
        scaled = jnp.where(inside, wide, scaled)
        A_ref[...] = jnp.where(inside, 0.0, A_ref[...]) - dot3(col, scaled)
        A_ref[at, :] = scaled
        return carry

    lax.fori_loop(0, n // 128, step, 0)


def pick(levels, table_ref, which):
    values = jnp.zeros(levels.shape, F32)
    for k in range(table_ref.shape[1]):
        values = jnp.where(levels == k, table_ref[which, k], values)
    return values


def piece_kernel(cls_ref, coeff_ref, out_ref, cols_ref):
    E = cls_ref.shape[1]
    across = pick(cls_ref[...], coeff_ref, 0)
    along = pick(cls_ref[...], coeff_ref, 1)
    d0, d1 = across[0:1], across[1:2]
    v0, a = along[0:1], along[1:2]
    v0_prev, a_prev = jnp.roll(v0, 1, axis=1), jnp.roll(a, 1, axis=1)
    diag = d0 + d1 + a + a_prev
    down, up = diag, diag
    for _ in range(16):
        down = diag - a_prev * a_prev / jnp.roll(down, 1, axis=1)
        up = diag - a * a / jnp.roll(up, -1, axis=1)
    g = 1.0 / (down + up - diag)
    step_p = jnp.log(down / a)
    step_q = jnp.log(up / a_prev)
    ph = jnp.floor(step_p * 256.0 + 0.5) * (1.0 / 256.0)
    qh = jnp.floor(step_q * 256.0 + 0.5) * (1.0 / 256.0)
    steps = jnp.concatenate([ph, step_p - ph, qh, step_q - qh, d0, d1, d0, d1], axis=0)
    lane8 = lax.broadcasted_iota(jnp.int32, (8, E), 1)
    sums = steps
    width = 1
    while width < E:
        sums = sums + jnp.where(lane8 >= width, jnp.roll(sums, width, axis=1), 0.0)
        width *= 2
    total = sums[:, E - 1 : E]
    ph_before, pl_before = sums[0:1] - steps[0:1], sums[1:2] - steps[1:2]
    rows = jnp.concatenate([ph_before, pl_before, sums[2:4], d0, d1, d0, d1], axis=0)
    tall = jnp.concatenate([rows, jnp.zeros((120, E), F32)], axis=0)
    cols_ref[...] = tall.T
    pt_h, pt_l, qt_h, qt_l = total[0:1], total[1:2], total[2:3], total[3:4]
    wrap_p = 1.0 / (1.0 - jnp.exp(-(pt_h + pt_l)))
    wrap_q = 1.0 / (1.0 - jnp.exp(-(qt_h + qt_l)))
    R = 64
    lane = lax.broadcasted_iota(jnp.int32, (R, E), 1)
    sub = lax.broadcasted_iota(jnp.int32, (R, E), 0)

    def chunk(i, carry):
        at = pl.ds(pl.multiple_of(i * R, R), R)
        c = cols_ref[at, :]
        index = sub + i * R
        later, earlier = lane < index, index < lane
        p = (rows[0:1] - c[:, 0:1]) + jnp.where(later, pt_h, 0.0)
        p = p + ((rows[1:2] - c[:, 1:2]) + jnp.where(later, pt_l, 0.0))
        q = (c[:, 2:3] - rows[2:3]) + jnp.where(earlier, qt_h, 0.0)
        q = q + ((c[:, 3:4] - rows[3:4]) + jnp.where(earlier, qt_l, 0.0))
        same = lane == index
        G = g * (jnp.exp(-p) * wrap_p + jnp.exp(-q) * wrap_q - jnp.where(same, 1.0, 0.0))
        c0, c1 = c[:, 4:5], c[:, 5:6]
        G0, G1 = G * d0, G * d1
        after = lane == jnp.where(index == E - 1, 0, index + 1)
        before = lane == jnp.where(index == 0, E - 1, index - 1)
        top = jnp.where(same, d0 + v0 + v0_prev, 0.0)
        top = top - jnp.where(after, v0_prev, 0.0) - jnp.where(before, v0, 0.0)
        out_ref[at, 0:E] = top - c0 * G0
        out_ref[at, E : 2 * E] = -(c0 * G1)
        low = pl.ds(pl.multiple_of(i * R + E, R), R)
        out_ref[low, 0:E] = -(c1 * G0)
        out_ref[low, E : 2 * E] = jnp.where(same, d1, 0.0) - c1 * G1
        return carry

    lax.fori_loop(0, E // R, chunk, 0)


def piece_map(classes, coeffs):
    E = classes.shape[1]
    return pl.pallas_call(
        piece_kernel,
        out_shape=jax.ShapeDtypeStruct((2 * E, 2 * E), F32),
        in_specs=[
            pl.BlockSpec(memory_space=pltpu.VMEM),
            pl.BlockSpec(memory_space=pltpu.SMEM),
        ],
        out_specs=pl.BlockSpec(memory_space=pltpu.VMEM),
        scratch_shapes=[pltpu.VMEM((E, 128), F32)],
        compiler_params=pltpu.CompilerParams(vmem_limit_bytes=12 << 20),
        cost_estimate=pl.CostEstimate(flops=20_000_000, bytes_accessed=16 << 20, transcendentals=0),
        name="piece_map",
    )(classes, coeffs)


N = 32


def block_kernel(second_ref, cls_ref, coeff_ref, out_ref, seam_ref, maps, vals, packs):
    lane1 = lax.broadcasted_iota(jnp.int32, (1, 128), 1)
    lane = lax.broadcasted_iota(jnp.int32, (128, 128), 1)
    sub = lax.broadcasted_iota(jnp.int32, (128, 128), 0)
    across = pick(cls_ref[...], coeff_ref, 0)
    along = pick(cls_ref[...], coeff_ref, 1)
    vals[0:32, :] = across
    vals[32:64, :] = along
    vals[64:96, :] = jnp.where(lane1 % N == 0, 0.0, jnp.roll(along, 1, axis=1))
    vals[96:128, :] = jnp.broadcast_to(along[:, N - 1 : N], (N, 128))
    low = jnp.where(sub < N, sub, -1000)
    is_diag = low == lane
    is_after = (low + 1 == lane) & (lane < N)
    is_before = (low == lane + 1)
    mid_diag = (sub == lane) & (sub >= N) & (sub < 2 * N)
    cross = ((low + N == lane) & (lane < 2 * N)) | ((lane < N) & (sub == lane + N))

    def first(c, carry):
        ac = vals[pl.ds(c, 1), :]
        al = vals[pl.ds(c + 32, 1), :]
        al_prev = vals[pl.ds(c + 64, 1), :]
        al_last = vals[pl.ds(c + 96, 1), :]
        m = jnp.where(is_diag, ac + al + al_prev, 0.0)
        m = m - jnp.where(is_after, al_prev, 0.0) - jnp.where(is_before, al, 0.0)
        m = m + jnp.where(mid_diag, ac, 0.0) - jnp.where(cross, ac, 0.0)
        slot = 3 * N + c
        ends = ((sub == N - 1) & (lane == slot)) | ((sub == slot) & (lane == N - 1))
        m = m - jnp.where(ends, al_last, 0.0)
        m = m + jnp.where((sub == slot) & (lane == slot), al_last, 0.0)
        maps[c] = m
        return carry

    lax.fori_loop(0, N, first, 0)

    seg1 = lane1 // N
    seg = lane // N
    subN = lax.broadcasted_iota(jnp.int32, (N, 128), 0)
    laneN = lax.broadcasted_iota(jnp.int32, (N, 128), 1)
    row_R = (sub >= N) & (sub < 2 * N)
    row_L = sub < N
    col_R = (lane >= N) & (lane < 2 * N)
    col_L = lane < N
    colR1 = (lane1 >= N) & (lane1 < 2 * N)
    colL1 = lane1 < N
    drop_a = row_R | col_R
    drop_b = row_L | col_L
    edge = (subN == 0) | (laneN % N == 0)
    corner = (subN == 0) & (laneN % N == 0)
    blockdiag = (sub // N) == seg

    lane8 = lax.broadcasted_iota(jnp.int32, (8, 128), 1)
    base8 = lane8 // N * N

    def spread(tile, k):
        return jnp.take_along_axis(tile, base8 + k, axis=1)

    count = N // 2
    span = 1
    while count >= 1:
        quads = max(count // 4, 1)
        live = min(count, 4)

        def gather(q, carry, live=live):
            packed = jnp.zeros((N, 128), F32)
            for i in range(live):
                a_rows = maps[q * 8 + 2 * i, N : 2 * N, :]
                b_rows = maps[q * 8 + 2 * i + 1, 0:N, :]
                piece = jnp.where(colR1, a_rows, 0.0)
                piece = jnp.roll(piece, N * (i - 1), axis=1) if i != 1 else piece
                other = jnp.where(colL1, b_rows, 0.0)
                other = jnp.roll(other, N * i, axis=1) if i else other
                packed = packed + piece + other
            packs[q] = jnp.where(corner, 1.0, jnp.where(edge, 0.0, packed))
            return carry

        lax.fori_loop(0, quads, gather, 0)

        done = panel_sweep(
            [packs[q, 8 * i : 8 * i + 8, :] for q in range(quads) for i in range(N // 8)], N, spread, lane8 % N
        )
        for q in range(quads):
            for i in range(N // 8):
                packs[q, 8 * i : 8 * i + 8, :] = done[q * (N // 8) + i]

        def merge(q, carry, live=live, span=span):
            G = packs[q]
            G4 = jnp.where(blockdiag, jnp.concatenate([G] * 4, axis=0), 0.0)
            sides = []
            fronts = []
            for i in range(4):
                if i >= live:
                    sides.append(jnp.zeros((N, 128), F32))
                    continue
                a = maps[q * 8 + 2 * i]
                b = maps[q * 8 + 2 * i + 1]
                t = 2 * N + (q * 8 + 2 * i + 1) * span
                a_rows, b_rows = a[N : 2 * N], b[0:N]
                W = jnp.where(colR1, 0.0, a_rows) + jnp.where(colL1, 0.0, b_rows)
                a_col, b_col = a[:, N : N + 1], b[:, 0:1]
                at_lane = lane1 == t
                into = a_col[N : 2 * N] + b_col[0:N]
                w_row = W[0:1]
                W = W + jnp.where(at_lane, into, 0.0)
                W = jnp.where(subN == 0, 0.0, W)
                F = jnp.where(drop_a, 0.0, a) + jnp.where(drop_b, 0.0, b)
                kept_col = jnp.where(row_R[:, :1], 0.0, a_col) + jnp.where(row_L[:, :1], 0.0, b_col)
                F = F + jnp.where(at_lane, kept_col, 0.0)
                F = F + jnp.where(sub == t, w_row + jnp.where(at_lane, into[0:1], 0.0), 0.0)
                sides.append(W)
                fronts.append(F)
            stack = jnp.concatenate(sides, axis=0)
            X = dot3(G4, stack)
            for i in range(live):
                part = dot3(sides[i], X[i * N : (i + 1) * N], LEFT_T)
                maps[q * 4 + i] = fronts[i] - part
            return carry

        lax.fori_loop(0, quads, merge, 0)
        count //= 2
        span *= 2
    out_ref[...] = maps[0]
    hand_on(out_ref, seam_ref, second_ref[0] == 1, N, False)


def block_map(second, cells, coeffs):
    return pl.pallas_call(
        block_kernel,
        out_shape=[jax.ShapeDtypeStruct((128, 128), F32), jax.ShapeDtypeStruct((N, N), F32)],
        in_specs=[SCALAR, WHOLE, SCALAR],
        out_specs=[WHOLE, WHOLE],
        scratch_shapes=[
            pltpu.VMEM((N, 128, 128), F32),
            pltpu.VMEM((128, 128), F32),
            pltpu.VMEM((4, N, 128), F32),
        ],
        compiler_params=pltpu.CompilerParams(vmem_limit_bytes=8 << 20),
        name="block_map",
    )(second, cells, coeffs)


def packing(n):
    count = n // 128
    above = [(i, j) for i in range(count) for j in range(i + 1, count)]
    return above, [(i, i + 1 if i + 1 < count else None) for i in range(0, count, 2)]


def packed_rows(n):
    above, twos = packing(n)
    return 128 * (len(above) + len(twos)) + 8


def diagonal_masks():
    row = lax.broadcasted_iota(jnp.int32, (128, 128), 0)
    lane = lax.broadcasted_iota(jnp.int32, (128, 128), 1)
    return row < lane, row == lane


def pack(full_ref, packed_ref):
    above, twos = packing(full_ref.shape[0])
    upper, diagonal = diagonal_masks()

    def block(i, j):
        return full_ref[128 * i : 128 * i + 128, 128 * j : 128 * j + 128]

    for k, (i, j) in enumerate(above):
        packed_ref[128 * k : 128 * k + 128, :] = block(i, j)
    last = 128 * (len(above) + len(twos))
    packed_ref[last : last + 8, :] = jnp.zeros((8, 128), F32)
    for m, (i, j) in enumerate(twos):
        at = 128 * (len(above) + m)
        if j is None:
            packed_ref[at : at + 128, :] = block(i, i)
        else:
            lower = block(j, j)
            packed_ref[at : at + 128, :] = jnp.where(upper | diagonal, block(i, i), lower)
            packed_ref[last + m : last + m + 1, :] = jnp.sum(jnp.where(diagonal, lower, 0.0), axis=0, keepdims=True)


def unpack(packed_ref, full_ref):
    above, twos = packing(full_ref.shape[0])
    upper, diagonal = diagonal_masks()

    def put(i, j, value):
        full_ref[128 * i : 128 * i + 128, 128 * j : 128 * j + 128] = value

    for k, (i, j) in enumerate(above):
        block = packed_ref[128 * k : 128 * k + 128, :]
        put(i, j, block)
        put(j, i, block.T)
    last = 128 * (len(above) + len(twos))
    for m, (i, j) in enumerate(twos):
        at = 128 * (len(above) + m)
        block = packed_ref[at : at + 128, :]
        if j is None:
            put(i, i, block)
        else:
            turned = block.T
            put(i, i, jnp.where(upper | diagonal, block, turned))
            entries = packed_ref[last + m : last + m + 1, :]
            put(j, j, jnp.where(upper, turned, jnp.where(diagonal, entries, block)))


def hand_on(map_ref, seam_ref, second, x, closing):
    n = map_ref.shape[0]
    X, Y = (n - 2 * x, n - x), (n - x, n)
    if not closing:
        first, other = map_ref[Y[0] : Y[1], Y[0] : Y[1]], map_ref[X[0] : X[1], X[0] : X[1]]
        seam_ref[...] = jnp.where(second, other, first)
        return
    for i, rows in enumerate((Y, X)):
        for j, cols in enumerate((Y, X)):
            flip_rows, flip_cols = (X, Y)[i], (X, Y)[j]
            first = map_ref[rows[0] : rows[1], cols[0] : cols[1]]
            other = map_ref[flip_rows[0] : flip_rows[1], flip_cols[0] : flip_cols[1]]
            seam_ref[i * x : i * x + x, j * x : j * x + x] = jnp.where(second, other, first)


def seam_matrix(A, x):
    E = A.shape[0]
    row = lax.broadcasted_iota(jnp.int32, (E, 1), 0)
    lane = lax.broadcasted_iota(jnp.int32, (1, E), 1)
    return jnp.where((row % x == 0) | (lane % x == 0), jnp.where(row == lane, 1.0, 0.0), A)


def seam_inverse(A, x):
    return inverse_small(seam_matrix(A, x))


def inverse_kernel(x, own_ref, recv_ref, out_ref):
    A = own_ref[...] + recv_ref[...]
    if A.shape[0] <= 128:
        out_ref[...] = seam_inverse(A, x)
    else:
        out_ref[...] = seam_matrix(A, x)
        inverse_blocks(out_ref, A.shape[0])


def inverse(own, recv, x):
    E = own.shape[0]
    return pl.pallas_call(
        functools.partial(inverse_kernel, x),
        out_shape=jax.ShapeDtypeStruct((E, E), F32),
        in_specs=[WHOLE, WHOLE],
        out_specs=WHOLE,
        compiler_params=limit(8),
        cost_estimate=pl.CostEstimate(flops=40_000_000 * E, bytes_accessed=E * E * 12, transcendentals=0),
        name=f"inverse_{E}",
    )(own, recv)


def merge_kernel(s, x, flip, closing, fused, packed_in, packed_out, order, onward, *refs):
    flags_ref, own_ref, recv_ref = refs[:3]
    refs = list(refs[3:])
    G_ref = None if fused else refs.pop(0)
    if closing:
        inner_ref, send_ref, coupling_ref, edge_ref, W_ref, X_ref, out_ref = refs[:7]
        rest = refs[7:]
    else:
        out_ref = refs.pop(0)
        seam_ref = refs.pop(0)
        packed_ref = refs.pop(0) if packed_out else None
        W_ref, X_ref = refs[:2]
        rest = refs[2:]
    if packed_in:
        full_ref = rest[0]
        unpack(recv_ref, full_ref)
        recv_ref = full_ref
    second = flags_ref[0] == 1
    offsets = {"S1": (0, s), "S2": (s, s), "X": (2 * s, x), "Y": (2 * s + x, x)}

    def block(which, rows, cols, width=0):
        (r, nr), (c, nc) = offsets[rows], offsets[cols]
        nc = width or nc
        own = own_ref[r : r + nr, c : c + nc]
        recv = recv_ref[r : r + nr, c : c + nc]
        if which == "a":
            return jnp.where(second, recv, own)
        return jnp.where(second, own, recv)

    K = out_ref.shape[0]
    if closing:
        kept = {"a": {"S1": 0, "S2": 2 * s}, "b": {"S1": s, "S2": 3 * s}}
        gone = {"a": {"Y": 0, "X": x}, "b": {"X": 0, "Y": x}}
    else:
        sides, ends = (2 * x, 0) if flip else (0, 4 * s)
        kept = {
            "a": {"S1": sides, "S2": sides + 2 * s, "X": ends},
            "b": {"S1": sides + s, "S2": sides + 3 * s, "Y": ends + x},
        }
        gone = {"a": {"Y": 0}, "b": {"X": 0}}

    for which in "ab":
        for rows, r in kept[which].items():
            nr = offsets[rows][1]
            for cols, c in kept[which].items():
                out_ref[r : r + nr, c : c + offsets[cols][1]] = block(which, rows, cols)
            for cols, c in kept["b" if which == "a" else "a"].items():
                nc = offsets[cols][1]
                out_ref[r : r + nr, c : c + nc] = jnp.zeros((nr, nc), F32)
        for rows, r in gone[which].items():
            for cols, c in kept[which].items():
                W_ref[r : r + x, c : c + offsets[cols][1]] = block(which, rows, cols)

    def fold(side):
        targets = [(0, kept["b"][side])]
        if closing:
            targets.append((x, kept["a"][side]))
        for e, t in targets:
            tb = t // 128 * 128
            tw = min(128, K - tb)
            lane = lax.broadcasted_iota(jnp.int32, (1, tw), 1)
            hit = lane == t - tb
            out_ref[t : t + 1, :] += W_ref[e : e + 1, :]
            for which in "ab":
                for cols, c in gone[which].items():
                    if c != e:
                        continue
                    for rows, r in kept[which].items():
                        nr = offsets[rows][1]
                        vec = block(which, rows, cols, 1)
                        out_ref[r : r + nr, tb : tb + tw] += jnp.where(hit, vec, 0.0)
                    for rows, r in gone[which].items():
                        vec = block(which, rows, cols, 1)
                        W_ref[r : r + x, tb : tb + tw] += jnp.where(hit, vec, 0.0)
                        if r == e:
                            out_ref[t : t + 1, tb : tb + tw] += jnp.where(hit, vec[0:1], 0.0)

    if order == "swapped":
        swapped = flags_ref[1] == 1
        pl.when(swapped)(lambda: fold("S2"))
        pl.when(jnp.logical_not(swapped))(lambda: fold("S1"))
    else:
        fold("S1")
    for e in (0, x) if closing else (0,):
        W_ref[e : e + 1, :] = jnp.zeros((1, K), F32)
    G = seam_inverse(block("a", "Y", "Y") + block("b", "X", "X"), x) if fused else G_ref[...]
    X_ref[...] = dot3(G, W_ref[...])
    if closing:
        h = K // 2
        core = flags_ref[0]
        for i in range(0, h, 256):
            inner_ref[i : i + 256, :] = out_ref[i : i + 256, 0:h] - dot3(W_ref[:, i : i + 256], X_ref[:, 0:h], LEFT_T)
        packed_ref = rest.pop()
        pack(inner_ref, packed_ref)
        half = send_ref.shape[0] - 8
        send_ref[0:half, :] = packed_ref[pl.ds(pl.multiple_of(core * half, half), half), :]
        send_ref[half : half + 8, :] = packed_ref[2 * half : 2 * half + 8, :]
        coupling_ref[...] = out_ref[0:h, h:K]
        edge_ref[...] = out_ref[pl.ds(pl.multiple_of(h + flags_ref[2], 8), 8), :]
        return
    R = min(K, 256) if K % 256 == 0 else min(K, 128) if K % 128 == 0 else K
    for i in range(0, K, R):
        out_ref[i : i + R, :] = out_ref[i : i + R, :] - dot3(W_ref[:, i : i + R], X_ref[...], LEFT_T)
    if order == "swap":

        @pl.when(flags_ref[1] == 1)
        def _():
            first, other = out_ref[0:x, :], out_ref[x : 2 * x, :]
            out_ref[0:x, :] = other
            out_ref[x : 2 * x, :] = first
            first, other = out_ref[:, 0:x], out_ref[:, x : 2 * x]
            out_ref[:, 0:x] = other
            out_ref[:, x : 2 * x] = first

    if packed_out:
        pack(out_ref, packed_ref)
    hand_on(out_ref, seam_ref, flags_ref[3] == 1, *onward)


SCALAR = pl.BlockSpec(memory_space=pltpu.SMEM)
WHOLE = pl.BlockSpec(memory_space=pltpu.VMEM)


def limit(mib):
    return pltpu.CompilerParams(vmem_limit_bytes=mib << 20)


def merged(flags, own, recv, G, s, x, onward=None, flip=False, packed_out=False, order="", mib=16):
    n = 2 * s + 2 * x
    closing = onward is None
    fused = G is None
    E = 2 * x if closing else x
    K = 4 * s if closing else 4 * s + 2 * x
    packed_in = recv.shape != (n, n)
    if closing:
        h = K // 2
        shapes = [(h, h), ((packed_rows(h) + 8) // 2, 128), (h, h), (8, K), (E, K), (E, K)]
        scratch = [pltpu.VMEM((K, K), F32)]
    else:
        seam = onward[0] * (2 if onward[1] else 1)
        shapes = [(K, K), (seam, seam)]
        if packed_out:
            shapes.append((packed_rows(K), 128))
        scratch = [pltpu.VMEM((E, K), F32), pltpu.VMEM((E, K), F32)]
    if packed_in:
        scratch.append(pltpu.VMEM((n, n), F32))
    if closing:
        scratch.append(pltpu.VMEM((packed_rows(h), 128), F32))
    return pl.pallas_call(
        functools.partial(merge_kernel, s, x, flip, closing, fused, packed_in, packed_out, order, onward),
        out_shape=[jax.ShapeDtypeStruct(shape, F32) for shape in shapes],
        in_specs=[SCALAR] + [WHOLE] * (2 if fused else 3),
        out_specs=[WHOLE] * len(shapes),
        scratch_shapes=scratch,
        compiler_params=limit(mib),
        name=f"merge_{E}_{K}",
    )(*((flags, own, recv) if fused else (flags, own, recv, G)))


def coupling_kernel(flags_ref, reach_ref, edge_ref, W_ref, X_ref, reach_out, edge_out, wide_ref):
    h = reach_ref.shape[0]
    for i in range(0, h, 256):
        reach_out[i : i + 256, :] = reach_ref[i : i + 256, :] - dot3(W_ref[:, i : i + 256], X_ref[:, h : 2 * h], LEFT_T)
    row = flags_ref[2]
    at = pl.ds(pl.multiple_of(h + row // 128 * 128, 128), 128)
    wide_ref[...] = dot3(W_ref[:, at], X_ref[...], LEFT_T)
    edge_out[...] = edge_ref[...] - wide_ref[pl.ds(pl.multiple_of(row % 128, 8), 8), :]


def coupling(flags, reach, edge, W, X):
    return pl.pallas_call(
        coupling_kernel,
        out_shape=[jax.ShapeDtypeStruct(reach.shape, F32), jax.ShapeDtypeStruct(edge.shape, F32)],
        in_specs=[SCALAR] + [WHOLE] * 4,
        out_specs=[WHOLE] * 2,
        scratch_shapes=[pltpu.VMEM((128, edge.shape[1]), F32)],
        compiler_params=limit(16),
        cost_estimate=pl.CostEstimate(flops=3_000_000_000, bytes_accessed=8 << 20, transcendentals=0),
        name="coupling",
    )(flags, reach, edge, W, X)


def interface_kernel(flags_ref, own_ref, near_ref, cross_ref, edge_ref, out_ref, A_ref, packed_ref):
    n = own_ref.shape[0]
    half = near_ref.shape[0] - 8
    first = flags_ref[0] == 0
    near, cross = near_ref[...], cross_ref[...]
    packed_ref[0:half, :] = jnp.where(first, near, cross)[0:half]
    packed_ref[half : 2 * half, :] = jnp.where(first, cross, near)[0:half]
    packed_ref[2 * half : 2 * half + 8, :] = near[half : half + 8]
    unpack(packed_ref, A_ref)
    A_ref[...] += own_ref[...]
    inverse_blocks(A_ref, n)
    out_ref[...] = dot3(edge_ref[:, 0:n], A_ref[...])


def interface(flags, own, near, cross, edge):
    E = own.shape[0]
    return pl.pallas_call(
        interface_kernel,
        out_shape=jax.ShapeDtypeStruct((8, E), F32),
        in_specs=[SCALAR] + [WHOLE] * 4,
        out_specs=WHOLE,
        scratch_shapes=[pltpu.VMEM((E, E), F32), pltpu.VMEM((packed_rows(E), 128), F32)],
        compiler_params=limit(16),
        cost_estimate=pl.CostEstimate(flops=30_000_000_000, bytes_accessed=64 << 20, transcendentals=0),
        name="interface",
    )(flags, own, near, cross, edge)


def last_kernel(flags_ref, edge_ref, Y_ref, own_ref, near_ref, cross_ref, out_ref):
    E = own_ref.shape[0]
    h = E // 2
    Y = Y_ref[...]
    mine = edge_ref[:, E : 2 * E] - dot3(Y, own_ref[...])
    first = flags_ref[0] == 0
    near, cross = near_ref[...], cross_ref[...]
    low, high = jnp.where(first, near, cross), jnp.where(first, cross, near)
    other = -(dot3(Y[:, 0:h], low) + dot3(Y[:, h:E], high))
    left = flags_ref[1] == 1
    out_ref[:, 0:E] = jnp.where(left, mine, other)
    out_ref[:, E : 2 * E] = jnp.where(left, other, mine)


def last_rows(flags, edge, Y, own, near, cross):
    return pl.pallas_call(
        last_kernel,
        out_shape=jax.ShapeDtypeStruct((Y.shape[0], 2 * own.shape[0]), F32),
        in_specs=[SCALAR] + [WHOLE] * 5,
        out_specs=WHOLE,
        compiler_params=limit(16),
        name="last_rows",
    )(flags, edge, Y, own, near, cross)


def flipped(block, axis, mask):
    return lax.ppermute(block, axis, [(i, i ^ mask) for i in range(lax.axis_size(axis))])


def ordered(parts, index):
    low = (index & 1) == 1
    p0, p1 = jnp.where(low, parts[1], parts[0]), jnp.where(low, parts[0], parts[1])
    p2, p3 = jnp.where(low, parts[3], parts[2]), jnp.where(low, parts[2], parts[3])
    high = (index & 2) == 2
    return [jnp.where(high, p2, p0), jnp.where(high, p3, p1), jnp.where(high, p0, p2), jnp.where(high, p1, p3)]


def gathered_cells(classes):
    E = classes.shape[1]
    x = lax.axis_index("col")
    slab = lax.axis_index("slab")
    core, z = slab & 1, slab >> 1 & 3
    parts = [classes] + [flipped(classes, "col", k) for k in (1, 2, 3)]
    strip = jnp.concatenate(ordered(parts, x), axis=0)

    def pair(low, high, second):
        return jnp.concatenate([jnp.where(second, high, low), jnp.where(second, low, high)], axis=0)

    def share(block, index, length):
        return lax.dynamic_slice_in_dim(block, index * length, length, axis=1)

    upper = core == 1
    strip = pair(share(strip, core, E // 2), flipped(share(strip, 1 - core, E // 2), "slab", 1), upper)
    quarter = (z ^ (z >> 1)) & 1
    place = 2 * (x >> 1) + ((x ^ (x >> 1)) & 1)
    strip = jnp.stack([share(strip, k * 4 + place, N) for k in (0, 1)])
    mine = lax.dynamic_index_in_dim(strip, quarter, 0, keepdims=False)
    other = lax.dynamic_index_in_dim(strip, 1 - quarter, 0, keepdims=False)
    return pair(mine, flipped(other, "slab", 2), z & 1 == 1)


def local(classes, across_coeff, along_coeff):
    E = classes.shape[1]
    slab, col = lax.axis_index("slab"), lax.axis_index("col")
    core = slab & 1

    def bit(index, mask):
        return jnp.where((index & mask) != 0, 1, 0).astype(jnp.int32).reshape(1)

    left = bit(slab ^ 16, 16)
    share = 2 * E // (lax.axis_size("slab") * lax.axis_size("col"))
    row = (((slab & 15) * lax.axis_size("col") + col) * share).astype(jnp.int32).reshape(1)
    seconds = [bit(col ^ (col >> 1), 1), bit(slab, 4), bit(col, 2), bit(slab, 8), bit(slab ^ (slab >> 1), 2), bit(slab, 1)]

    def flags(k):
        return jnp.concatenate([seconds[k], left, row, seconds[min(k + 1, 5)]])

    swaps = [("col", 1), ("slab", 6), ("col", 3), ("slab", 8), ("slab", 2), ("slab", 1)]
    coeffs = jnp.stack([across_coeff, along_coeff])
    cells = gathered_cells(classes)
    m, seam = block_map(seconds[0], jnp.concatenate([cells] * 4, axis=1), coeffs)
    sent = m
    sizes = [(32, 32), (32, 64), (64, 64), (64, 128), (128, 128)]
    for k, (s, x) in enumerate(sizes):
        G = None
        if k >= 2:
            other = flipped(seam, *swaps[k])
            if k == 4:
                sent, other = lax.optimization_barrier((sent, other))
            G = inverse(seam, other, x)
        recv = flipped(sent, *swaps[k])
        now = flags(k)
        if k == 4:
            held, G = lax.optimization_barrier((classes, G))
            pieces = piece_map(held, coeffs)
            now, pieces = lax.optimization_barrier((now, pieces))
        onward = (s * 2, False) if k < 4 else (x, True)
        if k == 3:
            onward = (x, False)
        order = {3: "swap", 4: "swapped"}.get(k, "")
        out = merged(now, m, recv, G, s, x, onward, flip=k < 4, packed_out=k > 0, order=order)
        m, seam, sent = out if k > 0 else (out[0], out[1], out[0])
    other = flipped(seam, *swaps[5])
    recv = flipped(sent, *swaps[5])
    G = inverse(seam, other, 128)
    inner, sent, reach, edge, W, X = merged(flags(5), m, recv, G, 256, 128, order="swapped", mib=32)
    both = flags(5)
    near = flipped(sent, "slab", 24)
    reach, edge = coupling(both, reach, edge, W, X)
    half = E // 2
    part = lax.dynamic_slice_in_dim(reach, core * half, half, 0)
    part_recv = flipped(part, "slab", 24)
    near, edge = lax.optimization_barrier((near, edge))
    Y = interface(both, inner, near, flipped(near, "slab", 1), edge)
    part, Y = lax.optimization_barrier((part_recv, Y))
    rows = last_rows(both, edge, Y, reach, part, flipped(part, "slab", 1))
    return (pieces, rows)


def solution(mesh):
    placed = P(("slab", "col"), None)
    return jax.shard_map(
        local,
        mesh=mesh,
        in_specs=(placed, P(), P()),
        out_specs=(placed, placed),
        check_vma=False,
    )
```

```python
import functools
import jax
import jax.numpy as jnp
from jax import lax
from jax.experimental import pallas as pl
from jax.experimental.pallas import tpu as pltpu
from jax.sharding import PartitionSpec as P

F32 = jnp.float32
BF16 = jnp.bfloat16
PLAIN = (((1,), (0,)), ((), ()))
LEFT_T = (((0,), (0,)), ((), ()))


SCALAR = pl.BlockSpec(memory_space=pltpu.SMEM)
WHOLE = pl.BlockSpec(memory_space=pltpu.VMEM)


def limit(mib):
    return pltpu.CompilerParams(vmem_limit_bytes=mib << 20)


def split(x):
    high = x.astype(BF16)
    return high, (x - high.astype(F32)).astype(BF16)


def dot3(left, right, dims=PLAIN):
    lh, ll = split(left)
    rh, rl = split(right)
    dot = functools.partial(lax.dot_general, dimension_numbers=dims, preferred_element_type=F32)
    return dot(lh, rh) + (dot(lh, rl) + dot(ll, rh))


def total(terms):
    terms = list(terms)
    out = terms[0]
    for term in terms[1:]:
        out = out + term
    return out


def small_inverse(s):
    size = max(i for i, _ in s) + 1
    if size == 1:
        return {(0, 0): 1.0 / s[0, 0]}
    if size == 2:
        a, b, d = s[0, 0], s[0, 1], s[1, 1]
        r = 1.0 / (a * d - b * b)
        return {(0, 0): d * r, (0, 1): -(b * r), (1, 1): a * r}
    h = size // 2
    both = range(h)

    def at(m, i, j):
        return m[min(i, j), max(i, j)]

    A = small_inverse({(i, j): s[i, j] for i in both for j in range(i, h)})
    X = {(i, j): total(at(A, i, k) * s[k, h + j] for k in both) for i in both for j in both}
    S = {(i, j): s[h + i, h + j] - total(s[k, h + i] * X[k, j] for k in both) for i in both for j in range(i, h)}
    S = small_inverse(S)
    Y = {(i, j): -total(X[i, k] * at(S, k, j) for k in both) for i in both for j in both}
    out = {}
    for i in both:
        for j in range(i, h):
            out[i, j] = A[i, j] - total(Y[i, k] * X[j, k] for k in both)
            out[h + i, h + j] = S[i, j]
        for j in both:
            out[i, h + j] = Y[i, j]
    return out


def panel_sweep(tiles, n, spread, lane, size=4):
    shape = tiles[0].shape
    sub = lax.broadcasted_iota(jnp.int32, shape, 0)
    tiles = list(tiles)
    per = n // 8
    groups = len(tiles) // per
    each = range(size)
    upper = [(i, j) for i in each for j in range(i, size)]

    def at(m, i, j):
        return m[min(i, j), max(i, j)]

    def row_of(tile, r):
        return jnp.broadcast_to(tile[r % 8 : r % 8 + 1, :], shape)

    blocks = [None] * groups
    for k in range(0, n, size):
        inside = (lane >= k) & (lane < k + size)
        units = [jnp.where(lane == k + j, 1.0, 0.0) for j in each]
        here, later = k // 8, (k + size) // 8
        for q in range(groups):
            mine = tiles[q * per : (q + 1) * per]
            C = [[spread(t, k + j) for t in mine] for j in each]
            R = [row_of(mine[here], k + j) for j in each]
            if k == 0:
                blocks[q] = {(i, j): row_of(C[j][here], i) for i, j in upper}
            G = small_inverse(blocks[q])
            if k + size < n:
                near = [spread(mine[here], k + size + j) for j in each]
                far = near if here == later else [spread(mine[later], k + size + j) for j in each]
                u = {(i, j): row_of(near[j], k + i) for i in each for j in each}
                v = {(i, j): row_of(far[j], k + size + i) for i, j in upper}
                T = {(i, j): total(at(G, i, m) * u[m, j] for m in each) for i in each for j in each}
                blocks[q] = {(i, j): v[i, j] - total(u[m, i] * T[m, j] for m in each) for i, j in upper}
            R = [jnp.where(inside, units[j], R[j]) for j in each]
            scaled = [total(at(G, i, j) * R[j] for j in each) for i in each]
            for t in range(per):
                new = jnp.where(inside, 0.0, mine[t]) - total(C[j][t] * scaled[j] for j in each)
                if t == here:
                    for j in each:
                        new = jnp.where(sub == (k + j) % 8, scaled[j], new)
                tiles[q * per + t] = new
    return tiles


def inverse_small(A):
    n = A.shape[0]
    lane = lax.broadcasted_iota(jnp.int32, (8, n), 1)
    tiles = [A[i : i + 8, :] for i in range(0, n, 8)]

    def spread(tile, k):
        return jnp.broadcast_to(tile[:, k : k + 1], (8, n))

    return jnp.concatenate(panel_sweep(tiles, n, spread, lane), axis=0)


def inverse_blocks(A_ref, n):
    lane = lax.broadcasted_iota(jnp.int32, (1, n), 1)

    def step(b, carry):
        at = pl.ds(pl.multiple_of(b * 128, 128), 128)
        row = A_ref[at, :]
        col = A_ref[:, at]
        pivot = inverse_small(A_ref[at, at])
        inside = (lane >= b * 128) & (lane < b * 128 + 128)
        scaled = dot3(pivot, row)
        wide = jnp.concatenate([pivot] * (n // 128), axis=1)
        scaled = jnp.where(inside, wide, scaled)
        A_ref[...] = jnp.where(inside, 0.0, A_ref[...]) - dot3(col, scaled)
        A_ref[at, :] = scaled
        return carry

    lax.fori_loop(0, n // 128, step, 0)


def pick(levels, table_ref, which):
    values = jnp.zeros(levels.shape, F32)
    for k in range(table_ref.shape[1]):
        values = jnp.where(levels == k, table_ref[which, k], values)
    return values


def piece_prelude(cls_ref, coeff_ref, rows_ref, cols_ref):
    E = cls_ref.shape[1]
    across = pick(cls_ref[...], coeff_ref, 0)
    along = pick(cls_ref[...], coeff_ref, 1)
    d0, d1 = across[0:1], across[1:2]
    v0, a = along[0:1], along[1:2]
    v0_prev, a_prev = jnp.roll(v0, 1, axis=1), jnp.roll(a, 1, axis=1)
    diag = d0 + d1 + a + a_prev
    down, up = diag, diag
    for _ in range(14):
        down = diag - a_prev * a_prev / jnp.roll(down, 1, axis=1)
        up = diag - a * a / jnp.roll(up, -1, axis=1)
    g = 1.0 / (down + up - diag)
    step_p = jnp.log(down / a)
    step_q = jnp.log(up / a_prev)
    ph = jnp.floor(step_p * 256.0 + 0.5) * (1.0 / 256.0)
    qh = jnp.floor(step_q * 256.0 + 0.5) * (1.0 / 256.0)
    steps = jnp.concatenate([ph, step_p - ph, qh, step_q - qh, d0, d1, d0, d1], axis=0)
    lane8 = lax.broadcasted_iota(jnp.int32, (8, E), 1)
    sums = steps
    width = 1
    while width < E:
        sums = sums + jnp.where(lane8 >= width, jnp.roll(sums, width, axis=1), 0.0)
        width *= 2
    total = sums[:, E - 1 : E]
    ph_before, pl_before = sums[0:1] - steps[0:1], sums[1:2] - steps[1:2]
    rows = jnp.concatenate([ph_before, pl_before, sums[2:4], d0, d1, d0 + v0 + v0_prev, v0], axis=0)
    tall = jnp.concatenate([rows, jnp.zeros((120, E), F32)], axis=0)
    cols_ref[...] = tall.T
    pt_h, pt_l, qt_h, qt_l = total[0:1], total[1:2], total[2:3], total[3:4]
    wrap_p = 1.0 / (1.0 - jnp.exp(-(pt_h + pt_l)))
    wrap_q = 1.0 / (1.0 - jnp.exp(-(qt_h + qt_l)))
    more = [g * wrap_p, g * wrap_q, g, v0_prev]
    more += [jnp.broadcast_to(t, (1, E)) for t in (pt_h, pt_l, qt_h, qt_l)]
    rows_ref[0:8, :] = rows
    rows_ref[8:16, :] = jnp.concatenate(more, axis=0)


def piece_kernel(cls_ref, coeff_ref, out_ref, rows_ref, cols_ref):
    step = pl.program_id(0)
    pl.when(step == 0)(lambda: piece_prelude(cls_ref, coeff_ref, rows_ref, cols_ref))
    R, E = out_ref.shape[1], cls_ref.shape[1]
    row = [rows_ref[k : k + 1, :] for k in range(16)]
    c = cols_ref[pl.ds(pl.multiple_of(step * R, R), R), :]
    lane = lax.broadcasted_iota(jnp.int32, (R, E), 1)
    index = lax.broadcasted_iota(jnp.int32, (R, E), 0) + step * R
    later, earlier = lane < index, index < lane
    p = (row[0] - c[:, 0:1]) + jnp.where(later, row[12], 0.0)
    p = p + ((row[1] - c[:, 1:2]) + jnp.where(later, row[13], 0.0))
    q = (c[:, 2:3] - row[2]) + jnp.where(earlier, row[14], 0.0)
    q = q + ((c[:, 3:4] - row[3]) + jnp.where(earlier, row[15], 0.0))
    same = lane == index
    G = row[8] * jnp.exp(-p) + row[9] * jnp.exp(-q) - jnp.where(same, row[10], 0.0)
    d0, d1 = row[4], row[5]
    G0, G1 = G * d0, G * d1
    c0, c1 = c[:, 4:5], c[:, 5:6]
    after = lane == jnp.where(index == E - 1, 0, index + 1)
    before = lane == jnp.where(index == 0, E - 1, index - 1)
    top = jnp.where(same, row[6], 0.0) - jnp.where(after, row[11], 0.0) - jnp.where(before, row[7], 0.0)
    out_ref[0, :, 0:E] = top - c0 * G0
    out_ref[0, :, E : 2 * E] = -(c0 * G1)
    out_ref[1, :, 0:E] = -(c1 * G0)
    out_ref[1, :, E : 2 * E] = jnp.where(same, d1, 0.0) - c1 * G1


def piece_map(classes, coeffs):
    E = classes.shape[1]
    R = 64
    out = pl.pallas_call(
        piece_kernel,
        grid=(E // R,),
        out_shape=jax.ShapeDtypeStruct((2, E, 2 * E), F32),
        in_specs=[WHOLE, SCALAR],
        out_specs=pl.BlockSpec((2, R, 2 * E), lambda i: (0, i, 0)),
        scratch_shapes=[pltpu.VMEM((16, E), F32), pltpu.VMEM((E, 128), F32)],
        compiler_params=limit(12),
        cost_estimate=pl.CostEstimate(flops=20_000_000, bytes_accessed=16 << 20, transcendentals=0),
        name="piece_map",
    )(classes, coeffs)
    return out.reshape(2 * E, 2 * E)


N = 32


def block_kernel(second_ref, cls_ref, coeff_ref, out_ref, seam_ref, maps, vals, packs):
    lane1 = lax.broadcasted_iota(jnp.int32, (1, 128), 1)
    lane = lax.broadcasted_iota(jnp.int32, (128, 128), 1)
    sub = lax.broadcasted_iota(jnp.int32, (128, 128), 0)
    across = pick(cls_ref[...], coeff_ref, 0)
    along = pick(cls_ref[...], coeff_ref, 1)
    vals[0:32, :] = across
    vals[32:64, :] = along
    vals[64:96, :] = jnp.where(lane1 % N == 0, 0.0, jnp.roll(along, 1, axis=1))
    vals[96:128, :] = jnp.broadcast_to(along[:, N - 1 : N], (N, 128))
    low = jnp.where(sub < N, sub, -1000)
    is_diag = low == lane
    is_after = (low + 1 == lane) & (lane < N)
    is_before = (low == lane + 1)
    mid_diag = (sub == lane) & (sub >= N) & (sub < 2 * N)
    cross = ((low + N == lane) & (lane < 2 * N)) | ((lane < N) & (sub == lane + N))

    def first(c, carry):
        ac = vals[pl.ds(c, 1), :]
        al = vals[pl.ds(c + 32, 1), :]
        al_prev = vals[pl.ds(c + 64, 1), :]
        al_last = vals[pl.ds(c + 96, 1), :]
        m = jnp.where(is_diag, ac + al + al_prev, 0.0)
        m = m - jnp.where(is_after, al_prev, 0.0) - jnp.where(is_before, al, 0.0)
        m = m + jnp.where(mid_diag, ac, 0.0) - jnp.where(cross, ac, 0.0)
        slot = 3 * N + c
        ends = ((sub == N - 1) & (lane == slot)) | ((sub == slot) & (lane == N - 1))
        m = m - jnp.where(ends, al_last, 0.0)
        m = m + jnp.where((sub == slot) & (lane == slot), al_last, 0.0)
        maps[c] = m
        return carry

    lax.fori_loop(0, N, first, 0)

    seg1 = lane1 // N
    seg = lane // N
    subN = lax.broadcasted_iota(jnp.int32, (N, 128), 0)
    laneN = lax.broadcasted_iota(jnp.int32, (N, 128), 1)
    row_R = (sub >= N) & (sub < 2 * N)
    row_L = sub < N
    col_R = (lane >= N) & (lane < 2 * N)
    col_L = lane < N
    colR1 = (lane1 >= N) & (lane1 < 2 * N)
    colL1 = lane1 < N
    drop_a = row_R | col_R
    drop_b = row_L | col_L
    edge = (subN == 0) | (laneN % N == 0)
    corner = (subN == 0) & (laneN % N == 0)
    blockdiag = (sub // N) == seg

    lane8 = lax.broadcasted_iota(jnp.int32, (8, 128), 1)
    base8 = lane8 // N * N

    def spread(tile, k):
        return jnp.take_along_axis(tile, base8 + k, axis=1)

    count = N // 2
    span = 1
    while count >= 1:
        quads = max(count // 4, 1)
        live = min(count, 4)

        def gather(q, carry, live=live):
            packed = jnp.zeros((N, 128), F32)
            for i in range(live):
                a_rows = maps[q * 8 + 2 * i, N : 2 * N, :]
                b_rows = maps[q * 8 + 2 * i + 1, 0:N, :]
                piece = jnp.where(colR1, a_rows, 0.0)
                piece = jnp.roll(piece, N * (i - 1), axis=1) if i != 1 else piece
                other = jnp.where(colL1, b_rows, 0.0)
                other = jnp.roll(other, N * i, axis=1) if i else other
                packed = packed + piece + other
            packs[q] = jnp.where(corner, 1.0, jnp.where(edge, 0.0, packed))
            return carry

        lax.fori_loop(0, quads, gather, 0)

        done = panel_sweep(
            [packs[q, 8 * i : 8 * i + 8, :] for q in range(quads) for i in range(N // 8)], N, spread, lane8 % N
        )
        for q in range(quads):
            for i in range(N // 8):
                packs[q, 8 * i : 8 * i + 8, :] = done[q * (N // 8) + i]

        def merge(q, carry, live=live, span=span):
            G = packs[q]
            G4 = jnp.where(blockdiag, jnp.concatenate([G] * 4, axis=0), 0.0)
            sides = []
            fronts = []
            for i in range(4):
                if i >= live:
                    sides.append(jnp.zeros((N, 128), F32))
                    continue
                a = maps[q * 8 + 2 * i]
                b = maps[q * 8 + 2 * i + 1]
                t = 2 * N + (q * 8 + 2 * i + 1) * span
                a_rows, b_rows = a[N : 2 * N], b[0:N]
                W = jnp.where(colR1, 0.0, a_rows) + jnp.where(colL1, 0.0, b_rows)
                a_col, b_col = a[:, N : N + 1], b[:, 0:1]
                at_lane = lane1 == t
                into = a_col[N : 2 * N] + b_col[0:N]
                w_row = W[0:1]
                W = W + jnp.where(at_lane, into, 0.0)
                W = jnp.where(subN == 0, 0.0, W)
                F = jnp.where(drop_a, 0.0, a) + jnp.where(drop_b, 0.0, b)
                kept_col = jnp.where(row_R[:, :1], 0.0, a_col) + jnp.where(row_L[:, :1], 0.0, b_col)
                F = F + jnp.where(at_lane, kept_col, 0.0)
                F = F + jnp.where(sub == t, w_row + jnp.where(at_lane, into[0:1], 0.0), 0.0)
                sides.append(W)
                fronts.append(F)
            stack = jnp.concatenate(sides, axis=0)
            X = dot3(G4, stack)
            for i in range(live):
                part = dot3(sides[i], X[i * N : (i + 1) * N], LEFT_T)
                maps[q * 4 + i] = fronts[i] - part
            return carry

        lax.fori_loop(0, quads, merge, 0)
        count //= 2
        span *= 2
    out_ref[...] = maps[0]
    hand_on(out_ref, seam_ref, second_ref[0] == 1, N, False)


def block_map(second, cells, coeffs):
    return pl.pallas_call(
        block_kernel,
        out_shape=[jax.ShapeDtypeStruct((128, 128), F32), jax.ShapeDtypeStruct((N, N), F32)],
        in_specs=[SCALAR, WHOLE, SCALAR],
        out_specs=[WHOLE, WHOLE],
        scratch_shapes=[
            pltpu.VMEM((N, 128, 128), F32),
            pltpu.VMEM((128, 128), F32),
            pltpu.VMEM((4, N, 128), F32),
        ],
        compiler_params=pltpu.CompilerParams(vmem_limit_bytes=8 << 20),
        name="block_map",
    )(second, cells, coeffs)


def packing(n):
    count = n // 128
    above = [(i, j) for i in range(count) for j in range(i + 1, count)]
    return above, [(i, i + 1 if i + 1 < count else None) for i in range(0, count, 2)]


def packed_rows(n):
    above, twos = packing(n)
    return 128 * (len(above) + len(twos)) + 8


def diagonal_masks():
    row = lax.broadcasted_iota(jnp.int32, (128, 128), 0)
    lane = lax.broadcasted_iota(jnp.int32, (128, 128), 1)
    return row < lane, row == lane


def pack(full_ref, packed_ref):
    above, twos = packing(full_ref.shape[0])
    upper, diagonal = diagonal_masks()

    def block(i, j):
        return full_ref[128 * i : 128 * i + 128, 128 * j : 128 * j + 128]

    for k, (i, j) in enumerate(above):
        packed_ref[128 * k : 128 * k + 128, :] = block(i, j)
    last = 128 * (len(above) + len(twos))
    packed_ref[last : last + 8, :] = jnp.zeros((8, 128), F32)
    for m, (i, j) in enumerate(twos):
        at = 128 * (len(above) + m)
        if j is None:
            packed_ref[at : at + 128, :] = block(i, i)
        else:
            lower = block(j, j)
            packed_ref[at : at + 128, :] = jnp.where(upper | diagonal, block(i, i), lower)
            packed_ref[last + m : last + m + 1, :] = jnp.sum(jnp.where(diagonal, lower, 0.0), axis=0, keepdims=True)


def unpack(packed_ref, full_ref):
    above, twos = packing(full_ref.shape[0])
    upper, diagonal = diagonal_masks()

    def put(i, j, value):
        full_ref[128 * i : 128 * i + 128, 128 * j : 128 * j + 128] = value

    for k, (i, j) in enumerate(above):
        block = packed_ref[128 * k : 128 * k + 128, :]
        put(i, j, block)
        put(j, i, block.T)
    last = 128 * (len(above) + len(twos))
    for m, (i, j) in enumerate(twos):
        at = 128 * (len(above) + m)
        block = packed_ref[at : at + 128, :]
        if j is None:
            put(i, i, block)
        else:
            turned = block.T
            put(i, i, jnp.where(upper | diagonal, block, turned))
            entries = packed_ref[last + m : last + m + 1, :]
            put(j, j, jnp.where(upper, turned, jnp.where(diagonal, entries, block)))


def hand_on(map_ref, seam_ref, second, x, closing):
    n = map_ref.shape[0]
    X, Y = (n - 2 * x, n - x), (n - x, n)
    if not closing:
        first, other = map_ref[Y[0] : Y[1], Y[0] : Y[1]], map_ref[X[0] : X[1], X[0] : X[1]]
        seam_ref[...] = jnp.where(second, other, first)
        return
    for i, rows in enumerate((Y, X)):
        for j, cols in enumerate((Y, X)):
            flip_rows, flip_cols = (X, Y)[i], (X, Y)[j]
            first = map_ref[rows[0] : rows[1], cols[0] : cols[1]]
            other = map_ref[flip_rows[0] : flip_rows[1], flip_cols[0] : flip_cols[1]]
            seam_ref[i * x : i * x + x, j * x : j * x + x] = jnp.where(second, other, first)


def seam_matrix(A, x):
    E = A.shape[0]
    row = lax.broadcasted_iota(jnp.int32, (E, 1), 0)
    lane = lax.broadcasted_iota(jnp.int32, (1, E), 1)
    return jnp.where((row % x == 0) | (lane % x == 0), jnp.where(row == lane, 1.0, 0.0), A)


def seam_inverse(A, x):
    return inverse_small(seam_matrix(A, x))


def inverse_kernel(x, own_ref, recv_ref, out_ref):
    A = own_ref[...] + recv_ref[...]
    if A.shape[0] <= 128:
        out_ref[...] = seam_inverse(A, x) if x else inverse_small(A)
    else:
        out_ref[...] = seam_matrix(A, x)
        inverse_blocks(out_ref, A.shape[0])


def inverse(own, recv, x):
    E = own.shape[0]
    return pl.pallas_call(
        functools.partial(inverse_kernel, x),
        out_shape=jax.ShapeDtypeStruct((E, E), F32),
        in_specs=[WHOLE, WHOLE],
        out_specs=WHOLE,
        compiler_params=limit(8),
        cost_estimate=pl.CostEstimate(flops=40_000_000 * E, bytes_accessed=E * E * 12, transcendentals=0),
        name=f"inverse_{E}",
    )(own, recv)


def merge_kernel(s, x, flip, closing, fused, packed_in, packed_out, order, onward, *refs):
    flags_ref, own_ref, recv_ref = refs[:3]
    refs = list(refs[3:])
    G_ref = None if fused else refs.pop(0)
    if closing:
        inner_ref, first_ref, coupling_ref, edge_ref, W_ref, X_ref, out_ref = refs[:7]
        rest = refs[7:]
    else:
        out_ref = refs.pop(0)
        seam_ref = refs.pop(0)
        packed_ref = refs.pop(0) if packed_out else None
        W_ref, X_ref = refs[:2]
        rest = refs[2:]
    if packed_in:
        full_ref = rest[0]
        unpack(recv_ref, full_ref)
        recv_ref = full_ref
    second = flags_ref[0] == 1
    offsets = {"S1": (0, s), "S2": (s, s), "X": (2 * s, x), "Y": (2 * s + x, x)}

    def block(which, rows, cols, width=0):
        (r, nr), (c, nc) = offsets[rows], offsets[cols]
        nc = width or nc
        own = own_ref[r : r + nr, c : c + nc]
        recv = recv_ref[r : r + nr, c : c + nc]
        if which == "a":
            return jnp.where(second, recv, own)
        return jnp.where(second, own, recv)

    K = out_ref.shape[0]
    if closing:
        kept = {"a": {"S1": 0, "S2": 2 * s}, "b": {"S1": s, "S2": 3 * s}}
        gone = {"a": {"Y": 0, "X": x}, "b": {"X": 0, "Y": x}}
    else:
        sides, ends = (2 * x, 0) if flip else (0, 4 * s)
        kept = {
            "a": {"S1": sides, "S2": sides + 2 * s, "X": ends},
            "b": {"S1": sides + s, "S2": sides + 3 * s, "Y": ends + x},
        }
        gone = {"a": {"Y": 0}, "b": {"X": 0}}

    for which in "ab":
        for rows, r in kept[which].items():
            nr = offsets[rows][1]
            for cols, c in kept[which].items():
                out_ref[r : r + nr, c : c + offsets[cols][1]] = block(which, rows, cols)
            for cols, c in kept["b" if which == "a" else "a"].items():
                nc = offsets[cols][1]
                out_ref[r : r + nr, c : c + nc] = jnp.zeros((nr, nc), F32)
        for rows, r in gone[which].items():
            for cols, c in kept[which].items():
                W_ref[r : r + x, c : c + offsets[cols][1]] = block(which, rows, cols)

    def fold(side):
        targets = [(0, kept["b"][side])]
        if closing:
            targets.append((x, kept["a"][side]))
        for e, t in targets:
            tb = t // 128 * 128
            tw = min(128, K - tb)
            lane = lax.broadcasted_iota(jnp.int32, (1, tw), 1)
            hit = lane == t - tb
            out_ref[t : t + 1, :] += W_ref[e : e + 1, :]
            for which in "ab":
                for cols, c in gone[which].items():
                    if c != e:
                        continue
                    for rows, r in kept[which].items():
                        nr = offsets[rows][1]
                        vec = block(which, rows, cols, 1)
                        out_ref[r : r + nr, tb : tb + tw] += jnp.where(hit, vec, 0.0)
                    for rows, r in gone[which].items():
                        vec = block(which, rows, cols, 1)
                        W_ref[r : r + x, tb : tb + tw] += jnp.where(hit, vec, 0.0)
                        if r == e:
                            out_ref[t : t + 1, tb : tb + tw] += jnp.where(hit, vec[0:1], 0.0)

    if order == "swapped":
        swapped = flags_ref[1] == 1
        pl.when(swapped)(lambda: fold("S2"))
        pl.when(jnp.logical_not(swapped))(lambda: fold("S1"))
    else:
        fold("S1")
    for e in (0, x) if closing else (0,):
        W_ref[e : e + 1, :] = jnp.zeros((1, K), F32)
    G = seam_inverse(block("a", "Y", "Y") + block("b", "X", "X"), x) if fused else G_ref[...]
    X_ref[...] = dot3(G, W_ref[...])
    if closing:
        h = K // 2
        first_ref[...] = out_ref[0:128, 0:128] - dot3(W_ref[:, 0:128], X_ref[:, 0:128], LEFT_T)
        inner_ref[...] = out_ref[0:h, 0:h]
        coupling_ref[...] = out_ref[0:h, h:K]
        edge_ref[...] = out_ref[pl.ds(pl.multiple_of(h + flags_ref[2], 8), 8), :]
        return
    R = min(K, 256) if K % 256 == 0 else min(K, 128) if K % 128 == 0 else K
    for i in range(0, K, R):
        out_ref[i : i + R, :] = out_ref[i : i + R, :] - dot3(W_ref[:, i : i + R], X_ref[...], LEFT_T)
    if order == "swap":

        @pl.when(flags_ref[1] == 1)
        def _():
            first, other = out_ref[0:x, :], out_ref[x : 2 * x, :]
            out_ref[0:x, :] = other
            out_ref[x : 2 * x, :] = first
            first, other = out_ref[:, 0:x], out_ref[:, x : 2 * x]
            out_ref[:, 0:x] = other
            out_ref[:, x : 2 * x] = first

    if packed_out:
        pack(out_ref, packed_ref)
    hand_on(out_ref, seam_ref, flags_ref[3] == 1, *onward)


def merged(flags, own, recv, G, s, x, onward=None, flip=False, packed_out=False, order="", mib=16):
    n = 2 * s + 2 * x
    closing = onward is None
    fused = G is None
    E = 2 * x if closing else x
    K = 4 * s if closing else 4 * s + 2 * x
    packed_in = recv.shape != (n, n)
    if closing:
        h = K // 2
        shapes = [(h, h), (128, 128), (h, h), (8, K), (E, K), (E, K)]
        scratch = [pltpu.VMEM((K, K), F32)]
    else:
        seam = onward[0] * (2 if onward[1] else 1)
        shapes = [(K, K), (seam, seam)]
        if packed_out:
            shapes.append((packed_rows(K), 128))
        scratch = [pltpu.VMEM((E, K), F32), pltpu.VMEM((E, K), F32)]
    if packed_in:
        scratch.append(pltpu.VMEM((n, n), F32))
    return pl.pallas_call(
        functools.partial(merge_kernel, s, x, flip, closing, fused, packed_in, packed_out, order, onward),
        out_shape=[jax.ShapeDtypeStruct(shape, F32) for shape in shapes],
        in_specs=[SCALAR] + [WHOLE] * (2 if fused else 3),
        out_specs=[WHOLE] * len(shapes),
        scratch_shapes=scratch,
        compiler_params=limit(mib),
        name=f"merge_{E}_{K}",
    )(*((flags, own, recv) if fused else (flags, own, recv, G)))


def inner_kernel(flags_ref, map_ref, W_ref, X_ref, inner_ref, send_ref, packed_ref):
    h = map_ref.shape[0]
    for i in range(0, h, 256):
        inner_ref[i : i + 256, :] = map_ref[i : i + 256, :] - dot3(W_ref[:, i : i + 256], X_ref[:, 0:h], LEFT_T)
    pack(inner_ref, packed_ref)
    half = send_ref.shape[0] - 8
    send_ref[0:half, :] = packed_ref[pl.ds(pl.multiple_of(flags_ref[0] * half, half), half), :]
    send_ref[half : half + 8, :] = packed_ref[2 * half : 2 * half + 8, :]


def inner_map(flags, half_map, W, X):
    rows = packed_rows(half_map.shape[0])
    return pl.pallas_call(
        inner_kernel,
        out_shape=[jax.ShapeDtypeStruct(half_map.shape, F32), jax.ShapeDtypeStruct(((rows + 8) // 2, 128), F32)],
        in_specs=[SCALAR] + [WHOLE] * 3,
        out_specs=[WHOLE] * 2,
        scratch_shapes=[pltpu.VMEM((rows, 128), F32)],
        compiler_params=limit(16),
        cost_estimate=pl.CostEstimate(flops=2_000_000_000, bytes_accessed=6 << 20, transcendentals=0),
        name="inner",
    )(flags, half_map, W, X)


def coupling_kernel(flags_ref, reach_ref, edge_ref, W_ref, X_ref, reach_out, edge_out, wide_ref):
    h = reach_ref.shape[0]
    for i in range(0, h, 256):
        reach_out[i : i + 256, :] = reach_ref[i : i + 256, :] - dot3(W_ref[:, i : i + 256], X_ref[:, h : 2 * h], LEFT_T)
    row = flags_ref[2]
    at = pl.ds(pl.multiple_of(h + row // 128 * 128, 128), 128)
    wide_ref[...] = dot3(W_ref[:, at], X_ref[...], LEFT_T)
    edge_out[...] = edge_ref[...] - wide_ref[pl.ds(pl.multiple_of(row % 128, 8), 8), :]


def coupling(flags, reach, edge, W, X):
    return pl.pallas_call(
        coupling_kernel,
        out_shape=[jax.ShapeDtypeStruct(reach.shape, F32), jax.ShapeDtypeStruct(edge.shape, F32)],
        in_specs=[SCALAR] + [WHOLE] * 4,
        out_specs=[WHOLE] * 2,
        scratch_shapes=[pltpu.VMEM((128, edge.shape[1]), F32)],
        compiler_params=limit(16),
        cost_estimate=pl.CostEstimate(flops=3_000_000_000, bytes_accessed=8 << 20, transcendentals=0),
        name="coupling",
    )(flags, reach, edge, W, X)


RIGHT_T = (((1,), (1,)), ((), ()))


def eliminate(S_ref, R_ref, Q_ref, b, pivot):
    n = S_ref.shape[0]
    at, rest = slice(128 * b, 128 * b + 128), slice(128 * b + 128, n)
    Z = dot3(Q_ref[:, at], pivot)
    Q_ref[:, at] = Z
    if rest.start < n:
        row = S_ref[at, rest]
        R = dot3(pivot, row)
        R_ref[at, rest] = R
        S_ref[rest, rest] = S_ref[rest, rest] - dot3(row, R, LEFT_T)
        Q_ref[:, rest] = Q_ref[:, rest] - dot3(Z, row)


def interface_kernel(flags_ref, own_ref, near_ref, cross_ref, edge_ref, pivot_ref, S_out, R_out, Q_out, S_ref, packed_ref):
    n = own_ref.shape[0]
    half = near_ref.shape[0] - 8
    first = flags_ref[0] == 0
    near, cross = near_ref[...], cross_ref[...]
    packed_ref[0:half, :] = jnp.where(first, near, cross)[0:half]
    packed_ref[half : 2 * half, :] = jnp.where(first, cross, near)[0:half]
    packed_ref[2 * half : 2 * half + 8, :] = near[half : half + 8]
    unpack(packed_ref, S_ref)
    S_ref[...] += own_ref[...]
    Q_out[...] = edge_ref[:, 0:n]
    eliminate(S_ref, R_out, Q_out, 0, pivot_ref[...])
    for b in range(1, n // 128 - 1):
        at = slice(128 * b, 128 * b + 128)
        eliminate(S_ref, R_out, Q_out, b, inverse_small(S_ref[at, at]))
    S_out[...] = S_ref[n - 128 : n, n - 128 : n]


def interface(flags, own, near, cross, edge, pivot):
    E = own.shape[0]
    return pl.pallas_call(
        interface_kernel,
        out_shape=[jax.ShapeDtypeStruct(shape, F32) for shape in ((128, 128), (E - 128, E), (8, E))],
        in_specs=[SCALAR] + [WHOLE] * 5,
        out_specs=[WHOLE] * 3,
        scratch_shapes=[pltpu.VMEM((E, E), F32), pltpu.VMEM((packed_rows(E), 128), F32)],
        compiler_params=limit(16),
        cost_estimate=pl.CostEstimate(flops=1_000_000_000, bytes_accessed=4 << 20, transcendentals=0),
        name="interface",
    )(flags, own, near, cross, edge, pivot)


def solve_kernel(S_ref, R_ref, Q_ref, Y_ref):
    n = Q_ref.shape[1]
    last = slice(n - 128, n)
    Y_ref[:, last] = dot3(Q_ref[:, last], inverse_small(S_ref[...]))
    for b in range(n // 128 - 2, -1, -1):
        at, rest = slice(128 * b, 128 * b + 128), slice(128 * b + 128, n)
        Y_ref[:, at] = Q_ref[:, at] - dot3(Y_ref[:, rest], R_ref[at, rest], RIGHT_T)


def solve(S, R, Q):
    return pl.pallas_call(
        solve_kernel,
        out_shape=jax.ShapeDtypeStruct(Q.shape, F32),
        in_specs=[WHOLE] * 3,
        out_specs=WHOLE,
        compiler_params=limit(16),
        cost_estimate=pl.CostEstimate(flops=5_000_000_000, bytes_accessed=4 << 20, transcendentals=0),
        name="solve",
    )(S, R, Q)


def last_kernel(flags_ref, edge_ref, Y_ref, own_ref, near_ref, cross_ref, out_ref):
    E = own_ref.shape[0]
    h = E // 2
    Y = Y_ref[...]
    mine = edge_ref[:, E : 2 * E] - dot3(Y, own_ref[...])
    first = flags_ref[0] == 0
    near, cross = near_ref[...], cross_ref[...]
    low, high = jnp.where(first, near, cross), jnp.where(first, cross, near)
    other = -(dot3(Y[:, 0:h], low) + dot3(Y[:, h:E], high))
    left = flags_ref[1] == 1
    out_ref[:, 0:E] = jnp.where(left, mine, other)
    out_ref[:, E : 2 * E] = jnp.where(left, other, mine)


def last_rows(flags, edge, Y, own, near, cross):
    return pl.pallas_call(
        last_kernel,
        out_shape=jax.ShapeDtypeStruct((Y.shape[0], 2 * own.shape[0]), F32),
        in_specs=[SCALAR] + [WHOLE] * 5,
        out_specs=WHOLE,
        compiler_params=limit(16),
        name="last_rows",
    )(flags, edge, Y, own, near, cross)


def flipped(block, axis, mask):
    return lax.ppermute(block, axis, [(i, i ^ mask) for i in range(lax.axis_size(axis))])


def ordered(parts, index):
    low = (index & 1) == 1
    p0, p1 = jnp.where(low, parts[1], parts[0]), jnp.where(low, parts[0], parts[1])
    p2, p3 = jnp.where(low, parts[3], parts[2]), jnp.where(low, parts[2], parts[3])
    high = (index & 2) == 2
    return [jnp.where(high, p2, p0), jnp.where(high, p3, p1), jnp.where(high, p0, p2), jnp.where(high, p1, p3)]


def gathered_cells(classes):
    E = classes.shape[1]
    x = lax.axis_index("col")
    slab = lax.axis_index("slab")
    core, quarter = slab & 1, slab >> 1 & 1
    parts = [classes] + [flipped(classes, "col", k) for k in (1, 2, 3)]
    strip = jnp.concatenate(ordered(parts, x), axis=0)

    def pair(low, high, second):
        return jnp.concatenate([jnp.where(second, high, low), jnp.where(second, low, high)], axis=0)

    def share(block, index, length):
        return lax.dynamic_slice_in_dim(block, index * length, length, axis=1)

    upper = core == 1
    strip = pair(share(strip, core, E // 2), flipped(share(strip, 1 - core, E // 2), "slab", 1), upper)
    place = 2 * (x >> 1) + ((x ^ (x >> 1)) & 1)
    strip = jnp.stack([share(strip, k * 4 + place, N) for k in (0, 1)])
    mine = lax.dynamic_index_in_dim(strip, quarter, 0, keepdims=False)
    other = lax.dynamic_index_in_dim(strip, 1 - quarter, 0, keepdims=False)
    return pair(mine, flipped(other, "slab", 2), quarter == 1)


def local(classes, across_coeff, along_coeff):
    E = classes.shape[1]
    slab, col = lax.axis_index("slab"), lax.axis_index("col")
    core = slab & 1

    def bit(index, mask):
        return jnp.where((index & mask) != 0, 1, 0).astype(jnp.int32).reshape(1)

    left = bit(slab ^ 16, 16)
    share = 2 * E // (lax.axis_size("slab") * lax.axis_size("col"))
    row = (((slab & 15) * lax.axis_size("col") + col) * share).astype(jnp.int32).reshape(1)
    seconds = [bit(col ^ (col >> 1), 1), bit(slab, 4), bit(col, 2), bit(slab, 8), bit(slab, 2), bit(slab, 1)]

    def flags(k):
        return jnp.concatenate([seconds[k], left, row, seconds[min(k + 1, 5)]])

    swaps = [("col", 1), ("slab", 4), ("col", 3), ("slab", 8), ("slab", 2), ("slab", 1)]
    coeffs = jnp.stack([across_coeff, along_coeff])
    cells = gathered_cells(classes)
    m, seam = block_map(seconds[0], jnp.concatenate([cells] * 4, axis=1), coeffs)
    sent = m
    sizes = [(32, 32), (32, 64), (64, 64), (64, 128), (128, 128)]
    for k, (s, x) in enumerate(sizes):
        G = None
        if k >= 2:
            other = flipped(seam, *swaps[k])
            if k == 4:
                sent, other = lax.optimization_barrier((sent, other))
            G = inverse(seam, other, x)
        recv = flipped(sent, *swaps[k])
        now = flags(k)
        if k == 4:
            held, G = lax.optimization_barrier((classes, G))
            pieces = piece_map(held, coeffs)
            now, pieces = lax.optimization_barrier((now, pieces))
        onward = (s * 2, False) if k < 4 else (x, True)
        if k == 3:
            onward = (x, False)
        order = {3: "swap", 4: "swapped"}.get(k, "")
        out = merged(now, m, recv, G, s, x, onward, flip=k < 4, packed_out=k > 0, order=order)
        m, seam, sent = out if k > 0 else (out[0], out[1], out[0])
    other = flipped(seam, *swaps[5])
    recv = flipped(sent, *swaps[5])
    G = inverse(seam, other, 128)
    half_map, seam, reach, edge, W, X = merged(flags(5), m, recv, G, 256, 128, order="swapped", mib=32)
    both = flags(5)
    other = flipped(seam, "slab", 16)
    inner, sent = inner_map(both, half_map, W, X)
    near = flipped(sent, "slab", 16)
    G = inverse(seam, other, 0)
    reach, edge = coupling(both, reach, edge, W, X)
    half = E // 2
    part = lax.dynamic_slice_in_dim(reach, core * half, half, 0)
    near, edge, G, part = lax.optimization_barrier((near, edge, G, part))
    part_recv = flipped(part, "slab", 16)
    S, R, Q = interface(both, inner, near, flipped(near, "slab", 1), edge, G)
    part, Q = lax.optimization_barrier((part_recv, Q))
    Y = solve(S, R, Q)
    rows = last_rows(both, edge, Y, reach, part, flipped(part, "slab", 1))
    return (pieces, rows)


def solution(mesh):
    placed = P(("slab", "col"), None)
    return jax.shard_map(
        local,
        mesh=mesh,
        in_specs=(placed, P(), P()),
        out_specs=(placed, placed),
        check_vma=False,
    )
```

```python
import functools
import jax
import jax.numpy as jnp
from jax import lax
from jax.experimental import pallas as pl
from jax.experimental.pallas import tpu as pltpu
from jax.sharding import PartitionSpec as P

F32 = jnp.float32
BF16 = jnp.bfloat16
PLAIN = (((1,), (0,)), ((), ()))
LEFT_T = (((0,), (0,)), ((), ()))


SCALAR = pl.BlockSpec(memory_space=pltpu.SMEM)
WHOLE = pl.BlockSpec(memory_space=pltpu.VMEM)


def limit(mib):
    return pltpu.CompilerParams(vmem_limit_bytes=mib << 20)


def split(x):
    high = x.astype(BF16)
    return high, (x - high.astype(F32)).astype(BF16)


def dot3(left, right, dims=PLAIN):
    lh, ll = split(left)
    rh, rl = split(right)
    dot = functools.partial(lax.dot_general, dimension_numbers=dims, preferred_element_type=F32)
    return dot(lh, rh) + (dot(lh, rl) + dot(ll, rh))


def total(terms):
    terms = list(terms)
    out = terms[0]
    for term in terms[1:]:
        out = out + term
    return out


def small_inverse(s):
    size = max(i for i, _ in s) + 1
    if size == 1:
        return {(0, 0): 1.0 / s[0, 0]}
    if size == 2:
        a, b, d = s[0, 0], s[0, 1], s[1, 1]
        r = 1.0 / (a * d - b * b)
        return {(0, 0): d * r, (0, 1): -(b * r), (1, 1): a * r}
    h = size // 2
    both = range(h)

    def at(m, i, j):
        return m[min(i, j), max(i, j)]

    A = small_inverse({(i, j): s[i, j] for i in both for j in range(i, h)})
    X = {(i, j): total(at(A, i, k) * s[k, h + j] for k in both) for i in both for j in both}
    S = {(i, j): s[h + i, h + j] - total(s[k, h + i] * X[k, j] for k in both) for i in both for j in range(i, h)}
    S = small_inverse(S)
    Y = {(i, j): -total(X[i, k] * at(S, k, j) for k in both) for i in both for j in both}
    out = {}
    for i in both:
        for j in range(i, h):
            out[i, j] = A[i, j] - total(Y[i, k] * X[j, k] for k in both)
            out[h + i, h + j] = S[i, j]
        for j in both:
            out[i, h + j] = Y[i, j]
    return out


def panel_sweep(tiles, n, spread, lane, size=4):
    shape = tiles[0].shape
    sub = lax.broadcasted_iota(jnp.int32, shape, 0)
    tiles = list(tiles)
    per = n // 8
    groups = len(tiles) // per
    each = range(size)
    upper = [(i, j) for i in each for j in range(i, size)]

    def at(m, i, j):
        return m[min(i, j), max(i, j)]

    def row_of(tile, r):
        return jnp.broadcast_to(tile[r % 8 : r % 8 + 1, :], shape)

    blocks = [None] * groups
    for k in range(0, n, size):
        inside = (lane >= k) & (lane < k + size)
        units = [jnp.where(lane == k + j, 1.0, 0.0) for j in each]
        here, later = k // 8, (k + size) // 8
        for q in range(groups):
            mine = tiles[q * per : (q + 1) * per]
            C = [[spread(t, k + j) for t in mine] for j in each]
            R = [row_of(mine[here], k + j) for j in each]
            if k == 0:
                blocks[q] = {(i, j): row_of(C[j][here], i) for i, j in upper}
            G = small_inverse(blocks[q])
            if k + size < n:
                near = [spread(mine[here], k + size + j) for j in each]
                far = near if here == later else [spread(mine[later], k + size + j) for j in each]
                u = {(i, j): row_of(near[j], k + i) for i in each for j in each}
                v = {(i, j): row_of(far[j], k + size + i) for i, j in upper}
                T = {(i, j): total(at(G, i, m) * u[m, j] for m in each) for i in each for j in each}
                blocks[q] = {(i, j): v[i, j] - total(u[m, i] * T[m, j] for m in each) for i, j in upper}
            R = [jnp.where(inside, units[j], R[j]) for j in each]
            scaled = [total(at(G, i, j) * R[j] for j in each) for i in each]
            for t in range(per):
                new = jnp.where(inside, 0.0, mine[t]) - total(C[j][t] * scaled[j] for j in each)
                if t == here:
                    for j in each:
                        new = jnp.where(sub == (k + j) % 8, scaled[j], new)
                tiles[q * per + t] = new
    return tiles


def inverse_small(A):
    n = A.shape[0]
    lane = lax.broadcasted_iota(jnp.int32, (8, n), 1)
    tiles = [A[i : i + 8, :] for i in range(0, n, 8)]

    def spread(tile, k):
        return jnp.broadcast_to(tile[:, k : k + 1], (8, n))

    return jnp.concatenate(panel_sweep(tiles, n, spread, lane), axis=0)


def inverse_blocks(A_ref, n):
    lane = lax.broadcasted_iota(jnp.int32, (1, n), 1)

    def step(b, carry):
        at = pl.ds(pl.multiple_of(b * 128, 128), 128)
        row = A_ref[at, :]
        col = A_ref[:, at]
        pivot = inverse_small(A_ref[at, at])
        inside = (lane >= b * 128) & (lane < b * 128 + 128)
        scaled = dot3(pivot, row)
        wide = jnp.concatenate([pivot] * (n // 128), axis=1)
        scaled = jnp.where(inside, wide, scaled)
        A_ref[...] = jnp.where(inside, 0.0, A_ref[...]) - dot3(col, scaled)
        A_ref[at, :] = scaled
        return carry

    lax.fori_loop(0, n // 128, step, 0)


def pick(levels, table_ref, which):
    values = jnp.zeros(levels.shape, F32)
    for k in range(table_ref.shape[1]):
        values = jnp.where(levels == k, table_ref[which, k], values)
    return values


def piece_prelude(cls_ref, coeff_ref, rows_ref, cols_ref):
    E = cls_ref.shape[1]
    across = pick(cls_ref[...], coeff_ref, 0)
    along = pick(cls_ref[...], coeff_ref, 1)
    d0, d1 = across[0:1], across[1:2]
    v0, a = along[0:1], along[1:2]
    v0_prev, a_prev = jnp.roll(v0, 1, axis=1), jnp.roll(a, 1, axis=1)
    diag = d0 + d1 + a + a_prev
    down, up = diag, diag
    for _ in range(14):
        down = diag - a_prev * a_prev / jnp.roll(down, 1, axis=1)
        up = diag - a * a / jnp.roll(up, -1, axis=1)
    g = 1.0 / (down + up - diag)
    step_p = jnp.log(down / a)
    step_q = jnp.log(up / a_prev)
    ph = jnp.floor(step_p * 256.0 + 0.5) * (1.0 / 256.0)
    qh = jnp.floor(step_q * 256.0 + 0.5) * (1.0 / 256.0)
    steps = jnp.concatenate([ph, step_p - ph, qh, step_q - qh, d0, d1, d0, d1], axis=0)
    lane8 = lax.broadcasted_iota(jnp.int32, (8, E), 1)
    sums = steps
    width = 1
    while width < E:
        sums = sums + jnp.where(lane8 >= width, jnp.roll(sums, width, axis=1), 0.0)
        width *= 2
    total = sums[:, E - 1 : E]
    ph_before, pl_before = sums[0:1] - steps[0:1], sums[1:2] - steps[1:2]
    rows = jnp.concatenate([ph_before, pl_before, sums[2:4], d0, d1, d0 + v0 + v0_prev, v0], axis=0)
    tall = jnp.concatenate([rows, jnp.zeros((120, E), F32)], axis=0)
    cols_ref[...] = tall.T
    pt_h, pt_l, qt_h, qt_l = total[0:1], total[1:2], total[2:3], total[3:4]
    wrap_p = 1.0 / (1.0 - jnp.exp(-(pt_h + pt_l)))
    wrap_q = 1.0 / (1.0 - jnp.exp(-(qt_h + qt_l)))
    more = [g * wrap_p, g * wrap_q, g, v0_prev]
    more += [jnp.broadcast_to(t, (1, E)) for t in (pt_h, pt_l, qt_h, qt_l)]
    rows_ref[0:8, :] = rows
    rows_ref[8:16, :] = jnp.concatenate(more, axis=0)


def piece_kernel(start, rows_ref, cols_ref, *refs):
    out_ref = refs[-1]
    step = pl.program_id(0) + start
    R, E = out_ref.shape[1], cols_ref.shape[0]
    row = [rows_ref[k : k + 1, :] for k in range(16)]
    c = cols_ref[pl.ds(pl.multiple_of(step * R, R), R), :]
    lane = lax.broadcasted_iota(jnp.int32, (R, E), 1)
    index = lax.broadcasted_iota(jnp.int32, (R, E), 0) + step * R
    later, earlier = lane < index, index < lane
    p = (row[0] - c[:, 0:1]) + jnp.where(later, row[12], 0.0)
    p = p + ((row[1] - c[:, 1:2]) + jnp.where(later, row[13], 0.0))
    q = (c[:, 2:3] - row[2]) + jnp.where(earlier, row[14], 0.0)
    q = q + ((c[:, 3:4] - row[3]) + jnp.where(earlier, row[15], 0.0))
    same = lane == index
    G = row[8] * jnp.exp(-p) + row[9] * jnp.exp(-q) - jnp.where(same, row[10], 0.0)
    d0, d1 = row[4], row[5]
    G0, G1 = G * d0, G * d1
    c0, c1 = c[:, 4:5], c[:, 5:6]
    after = lane == jnp.where(index == E - 1, 0, index + 1)
    before = lane == jnp.where(index == 0, E - 1, index - 1)
    top = jnp.where(same, row[6], 0.0) - jnp.where(after, row[11], 0.0) - jnp.where(before, row[7], 0.0)
    out_ref[0, :, 0:E] = top - c0 * G0
    out_ref[0, :, E : 2 * E] = -(c0 * G1)
    out_ref[1, :, 0:E] = -(c1 * G0)
    out_ref[1, :, E : 2 * E] = jnp.where(same, d1, 0.0) - c1 * G1


def piece_vectors(classes, coeffs):
    E = classes.shape[1]
    return pl.pallas_call(
        piece_prelude,
        out_shape=[jax.ShapeDtypeStruct((16, E), F32), jax.ShapeDtypeStruct((E, 128), F32)],
        in_specs=[WHOLE, SCALAR],
        out_specs=[WHOLE, WHOLE],
        compiler_params=limit(8),
        cost_estimate=pl.CostEstimate(flops=20_000_000, bytes_accessed=6 << 20, transcendentals=0),
        name="piece_vectors",
    )(classes, coeffs)


def piece_part(rows, cols, done, start, count):
    E = cols.shape[0]
    R = E // 8
    old = [] if done is None else [done]
    return pl.pallas_call(
        functools.partial(piece_kernel, start),
        grid=(count,),
        out_shape=jax.ShapeDtypeStruct((2, E, 2 * E), F32),
        in_specs=[WHOLE, WHOLE] + [pl.BlockSpec(memory_space=pl.ANY)] * len(old),
        out_specs=pl.BlockSpec((2, R, 2 * E), lambda i: (0, i + start, 0)),
        input_output_aliases={2: 0} if old else {},
        compiler_params=limit(8),
        cost_estimate=pl.CostEstimate(flops=20_000_000, bytes_accessed=count << 21, transcendentals=0),
        name=f"piece_part_{start}",
    )(rows, cols, *old)


N = 32


def block_kernel(second_ref, cls_ref, coeff_ref, out_ref, seam_ref, maps, vals, packs):
    lane1 = lax.broadcasted_iota(jnp.int32, (1, 128), 1)
    lane = lax.broadcasted_iota(jnp.int32, (128, 128), 1)
    sub = lax.broadcasted_iota(jnp.int32, (128, 128), 0)
    across = pick(cls_ref[...], coeff_ref, 0)
    along = pick(cls_ref[...], coeff_ref, 1)
    vals[0:32, :] = across
    vals[32:64, :] = along
    vals[64:96, :] = jnp.where(lane1 % N == 0, 0.0, jnp.roll(along, 1, axis=1))
    vals[96:128, :] = jnp.broadcast_to(along[:, N - 1 : N], (N, 128))
    low = jnp.where(sub < N, sub, -1000)
    is_diag = low == lane
    is_after = (low + 1 == lane) & (lane < N)
    is_before = (low == lane + 1)
    mid_diag = (sub == lane) & (sub >= N) & (sub < 2 * N)
    cross = ((low + N == lane) & (lane < 2 * N)) | ((lane < N) & (sub == lane + N))

    def first(c, carry):
        ac = vals[pl.ds(c, 1), :]
        al = vals[pl.ds(c + 32, 1), :]
        al_prev = vals[pl.ds(c + 64, 1), :]
        al_last = vals[pl.ds(c + 96, 1), :]
        m = jnp.where(is_diag, ac + al + al_prev, 0.0)
        m = m - jnp.where(is_after, al_prev, 0.0) - jnp.where(is_before, al, 0.0)
        m = m + jnp.where(mid_diag, ac, 0.0) - jnp.where(cross, ac, 0.0)
        slot = 3 * N + c
        ends = ((sub == N - 1) & (lane == slot)) | ((sub == slot) & (lane == N - 1))
        m = m - jnp.where(ends, al_last, 0.0)
        m = m + jnp.where((sub == slot) & (lane == slot), al_last, 0.0)
        maps[c] = m
        return carry

    lax.fori_loop(0, N, first, 0)

    seg1 = lane1 // N
    seg = lane // N
    subN = lax.broadcasted_iota(jnp.int32, (N, 128), 0)
    laneN = lax.broadcasted_iota(jnp.int32, (N, 128), 1)
    row_R = (sub >= N) & (sub < 2 * N)
    row_L = sub < N
    col_R = (lane >= N) & (lane < 2 * N)
    col_L = lane < N
    colR1 = (lane1 >= N) & (lane1 < 2 * N)
    colL1 = lane1 < N
    drop_a = row_R | col_R
    drop_b = row_L | col_L
    edge = (subN == 0) | (laneN % N == 0)
    corner = (subN == 0) & (laneN % N == 0)
    blockdiag = (sub // N) == seg

    lane8 = lax.broadcasted_iota(jnp.int32, (8, 128), 1)
    base8 = lane8 // N * N

    def spread(tile, k):
        return jnp.take_along_axis(tile, base8 + k, axis=1)

    count = N // 2
    span = 1
    while count >= 1:
        quads = max(count // 4, 1)
        live = min(count, 4)

        def gather(q, carry, live=live):
            packed = jnp.zeros((N, 128), F32)
            for i in range(live):
                a_rows = maps[q * 8 + 2 * i, N : 2 * N, :]
                b_rows = maps[q * 8 + 2 * i + 1, 0:N, :]
                piece = jnp.where(colR1, a_rows, 0.0)
                piece = jnp.roll(piece, N * (i - 1), axis=1) if i != 1 else piece
                other = jnp.where(colL1, b_rows, 0.0)
                other = jnp.roll(other, N * i, axis=1) if i else other
                packed = packed + piece + other
            packs[q] = jnp.where(corner, 1.0, jnp.where(edge, 0.0, packed))
            return carry

        lax.fori_loop(0, quads, gather, 0)

        done = panel_sweep(
            [packs[q, 8 * i : 8 * i + 8, :] for q in range(quads) for i in range(N // 8)], N, spread, lane8 % N
        )
        for q in range(quads):
            for i in range(N // 8):
                packs[q, 8 * i : 8 * i + 8, :] = done[q * (N // 8) + i]

        def merge(q, carry, live=live, span=span):
            G = packs[q]
            G4 = jnp.where(blockdiag, jnp.concatenate([G] * 4, axis=0), 0.0)
            sides = []
            fronts = []
            for i in range(4):
                if i >= live:
                    sides.append(jnp.zeros((N, 128), F32))
                    continue
                a = maps[q * 8 + 2 * i]
                b = maps[q * 8 + 2 * i + 1]
                t = 2 * N + (q * 8 + 2 * i + 1) * span
                a_rows, b_rows = a[N : 2 * N], b[0:N]
                W = jnp.where(colR1, 0.0, a_rows) + jnp.where(colL1, 0.0, b_rows)
                a_col, b_col = a[:, N : N + 1], b[:, 0:1]
                at_lane = lane1 == t
                into = a_col[N : 2 * N] + b_col[0:N]
                w_row = W[0:1]
                W = W + jnp.where(at_lane, into, 0.0)
                W = jnp.where(subN == 0, 0.0, W)
                F = jnp.where(drop_a, 0.0, a) + jnp.where(drop_b, 0.0, b)
                kept_col = jnp.where(row_R[:, :1], 0.0, a_col) + jnp.where(row_L[:, :1], 0.0, b_col)
                F = F + jnp.where(at_lane, kept_col, 0.0)
                F = F + jnp.where(sub == t, w_row + jnp.where(at_lane, into[0:1], 0.0), 0.0)
                sides.append(W)
                fronts.append(F)
            stack = jnp.concatenate(sides, axis=0)
            X = dot3(G4, stack)
            for i in range(live):
                part = dot3(sides[i], X[i * N : (i + 1) * N], LEFT_T)
                maps[q * 4 + i] = fronts[i] - part
            return carry

        lax.fori_loop(0, quads, merge, 0)
        count //= 2
        span *= 2
    out_ref[...] = maps[0]
    hand_on(out_ref, seam_ref, second_ref[0] == 1, N, False)


def block_map(second, cells, coeffs):
    return pl.pallas_call(
        block_kernel,
        out_shape=[jax.ShapeDtypeStruct((128, 128), F32), jax.ShapeDtypeStruct((N, N), F32)],
        in_specs=[SCALAR, WHOLE, SCALAR],
        out_specs=[WHOLE, WHOLE],
        scratch_shapes=[
            pltpu.VMEM((N, 128, 128), F32),
            pltpu.VMEM((128, 128), F32),
            pltpu.VMEM((4, N, 128), F32),
        ],
        compiler_params=pltpu.CompilerParams(vmem_limit_bytes=8 << 20),
        name="block_map",
    )(second, cells, coeffs)


def packing(n):
    count = n // 128
    above = [(i, j) for i in range(count) for j in range(i + 1, count)]
    return above, [(i, i + 1 if i + 1 < count else None) for i in range(0, count, 2)]


def packed_rows(n):
    above, twos = packing(n)
    return 128 * (len(above) + len(twos)) + 8


def diagonal_masks():
    row = lax.broadcasted_iota(jnp.int32, (128, 128), 0)
    lane = lax.broadcasted_iota(jnp.int32, (128, 128), 1)
    return row < lane, row == lane


def pack(full_ref, packed_ref):
    above, twos = packing(full_ref.shape[0])
    upper, diagonal = diagonal_masks()

    def block(i, j):
        return full_ref[128 * i : 128 * i + 128, 128 * j : 128 * j + 128]

    for k, (i, j) in enumerate(above):
        packed_ref[128 * k : 128 * k + 128, :] = block(i, j)
    last = 128 * (len(above) + len(twos))
    packed_ref[last : last + 8, :] = jnp.zeros((8, 128), F32)
    for m, (i, j) in enumerate(twos):
        at = 128 * (len(above) + m)
        if j is None:
            packed_ref[at : at + 128, :] = block(i, i)
        else:
            lower = block(j, j)
            packed_ref[at : at + 128, :] = jnp.where(upper | diagonal, block(i, i), lower)
            packed_ref[last + m : last + m + 1, :] = jnp.sum(jnp.where(diagonal, lower, 0.0), axis=0, keepdims=True)


def unpack(packed_ref, full_ref):
    above, twos = packing(full_ref.shape[0])
    upper, diagonal = diagonal_masks()

    def put(i, j, value):
        full_ref[128 * i : 128 * i + 128, 128 * j : 128 * j + 128] = value

    for k, (i, j) in enumerate(above):
        block = packed_ref[128 * k : 128 * k + 128, :]
        put(i, j, block)
        put(j, i, block.T)
    last = 128 * (len(above) + len(twos))
    for m, (i, j) in enumerate(twos):
        at = 128 * (len(above) + m)
        block = packed_ref[at : at + 128, :]
        if j is None:
            put(i, i, block)
        else:
            turned = block.T
            put(i, i, jnp.where(upper | diagonal, block, turned))
            entries = packed_ref[last + m : last + m + 1, :]
            put(j, j, jnp.where(upper, turned, jnp.where(diagonal, entries, block)))


def hand_on(map_ref, seam_ref, second, x, closing):
    n = map_ref.shape[0]
    X, Y = (n - 2 * x, n - x), (n - x, n)
    if not closing:
        first, other = map_ref[Y[0] : Y[1], Y[0] : Y[1]], map_ref[X[0] : X[1], X[0] : X[1]]
        seam_ref[...] = jnp.where(second, other, first)
        return
    for i, rows in enumerate((Y, X)):
        for j, cols in enumerate((Y, X)):
            flip_rows, flip_cols = (X, Y)[i], (X, Y)[j]
            first = map_ref[rows[0] : rows[1], cols[0] : cols[1]]
            other = map_ref[flip_rows[0] : flip_rows[1], flip_cols[0] : flip_cols[1]]
            seam_ref[i * x : i * x + x, j * x : j * x + x] = jnp.where(second, other, first)


def seam_matrix(A, x):
    E = A.shape[0]
    row = lax.broadcasted_iota(jnp.int32, (E, 1), 0)
    lane = lax.broadcasted_iota(jnp.int32, (1, E), 1)
    return jnp.where((row % x == 0) | (lane % x == 0), jnp.where(row == lane, 1.0, 0.0), A)


def seam_inverse(A, x):
    return inverse_small(seam_matrix(A, x))


def inverse_kernel(x, own_ref, recv_ref, out_ref):
    A = own_ref[...] + recv_ref[...]
    if A.shape[0] <= 128:
        out_ref[...] = seam_inverse(A, x) if x else inverse_small(A)
    else:
        out_ref[...] = seam_matrix(A, x)
        inverse_blocks(out_ref, A.shape[0])


def inverse(own, recv, x):
    E = own.shape[0]
    return pl.pallas_call(
        functools.partial(inverse_kernel, x),
        out_shape=jax.ShapeDtypeStruct((E, E), F32),
        in_specs=[WHOLE, WHOLE],
        out_specs=WHOLE,
        compiler_params=limit(8),
        cost_estimate=pl.CostEstimate(flops=40_000_000 * E, bytes_accessed=E * E * 12, transcendentals=0),
        name=f"inverse_{E}",
    )(own, recv)


def merge_kernel(s, x, flip, closing, fused, packed_in, packed_out, order, onward, *refs):
    flags_ref, own_ref, recv_ref = refs[:3]
    refs = list(refs[3:])
    G_ref = None if fused else refs.pop(0)
    if closing:
        inner_ref, first_ref, coupling_ref, edge_ref, W_ref, X_ref, out_ref = refs[:7]
        rest = refs[7:]
    else:
        out_ref = refs.pop(0)
        seam_ref = refs.pop(0)
        packed_ref = refs.pop(0) if packed_out else None
        W_ref, X_ref = refs[:2]
        rest = refs[2:]
    if packed_in:
        full_ref = rest[0]
        unpack(recv_ref, full_ref)
        recv_ref = full_ref
    second = flags_ref[0] == 1
    offsets = {"S1": (0, s), "S2": (s, s), "X": (2 * s, x), "Y": (2 * s + x, x)}

    def block(which, rows, cols, width=0):
        (r, nr), (c, nc) = offsets[rows], offsets[cols]
        nc = width or nc
        own = own_ref[r : r + nr, c : c + nc]
        recv = recv_ref[r : r + nr, c : c + nc]
        if which == "a":
            return jnp.where(second, recv, own)
        return jnp.where(second, own, recv)

    K = out_ref.shape[0]
    if closing:
        kept = {"a": {"S1": 0, "S2": 2 * s}, "b": {"S1": s, "S2": 3 * s}}
        gone = {"a": {"Y": 0, "X": x}, "b": {"X": 0, "Y": x}}
    else:
        sides, ends = (2 * x, 0) if flip else (0, 4 * s)
        kept = {
            "a": {"S1": sides, "S2": sides + 2 * s, "X": ends},
            "b": {"S1": sides + s, "S2": sides + 3 * s, "Y": ends + x},
        }
        gone = {"a": {"Y": 0}, "b": {"X": 0}}

    for which in "ab":
        for rows, r in kept[which].items():
            nr = offsets[rows][1]
            for cols, c in kept[which].items():
                out_ref[r : r + nr, c : c + offsets[cols][1]] = block(which, rows, cols)
            for cols, c in kept["b" if which == "a" else "a"].items():
                nc = offsets[cols][1]
                out_ref[r : r + nr, c : c + nc] = jnp.zeros((nr, nc), F32)
        for rows, r in gone[which].items():
            for cols, c in kept[which].items():
                W_ref[r : r + x, c : c + offsets[cols][1]] = block(which, rows, cols)

    def fold(side):
        targets = [(0, kept["b"][side])]
        if closing:
            targets.append((x, kept["a"][side]))
        for e, t in targets:
            tb = t // 128 * 128
            tw = min(128, K - tb)
            lane = lax.broadcasted_iota(jnp.int32, (1, tw), 1)
            hit = lane == t - tb
            out_ref[t : t + 1, :] += W_ref[e : e + 1, :]
            for which in "ab":
                for cols, c in gone[which].items():
                    if c != e:
                        continue
                    for rows, r in kept[which].items():
                        nr = offsets[rows][1]
                        vec = block(which, rows, cols, 1)
                        out_ref[r : r + nr, tb : tb + tw] += jnp.where(hit, vec, 0.0)
                    for rows, r in gone[which].items():
                        vec = block(which, rows, cols, 1)
                        W_ref[r : r + x, tb : tb + tw] += jnp.where(hit, vec, 0.0)
                        if r == e:
                            out_ref[t : t + 1, tb : tb + tw] += jnp.where(hit, vec[0:1], 0.0)

    if order == "swapped":
        swapped = flags_ref[1] == 1
        pl.when(swapped)(lambda: fold("S2"))
        pl.when(jnp.logical_not(swapped))(lambda: fold("S1"))
    else:
        fold("S1")
    for e in (0, x) if closing else (0,):
        W_ref[e : e + 1, :] = jnp.zeros((1, K), F32)
    G = seam_inverse(block("a", "Y", "Y") + block("b", "X", "X"), x) if fused else G_ref[...]
    X_ref[...] = dot3(G, W_ref[...])
    if closing:
        h = K // 2
        first_ref[...] = out_ref[0:128, 0:128] - dot3(W_ref[:, 0:128], X_ref[:, 0:128], LEFT_T)
        inner_ref[...] = out_ref[0:h, 0:h]
        coupling_ref[...] = out_ref[0:h, h:K]
        edge_ref[...] = out_ref[pl.ds(pl.multiple_of(h + flags_ref[2], 8), 8), :]
        return
    R = min(K, 256) if K % 256 == 0 else min(K, 128) if K % 128 == 0 else K
    for i in range(0, K, R):
        out_ref[i : i + R, :] = out_ref[i : i + R, :] - dot3(W_ref[:, i : i + R], X_ref[...], LEFT_T)
    if order == "swap":

        @pl.when(flags_ref[1] == 1)
        def _():
            first, other = out_ref[0:x, :], out_ref[x : 2 * x, :]
            out_ref[0:x, :] = other
            out_ref[x : 2 * x, :] = first
            first, other = out_ref[:, 0:x], out_ref[:, x : 2 * x]
            out_ref[:, 0:x] = other
            out_ref[:, x : 2 * x] = first

    if packed_out:
        pack(out_ref, packed_ref)
    hand_on(out_ref, seam_ref, flags_ref[3] == 1, *onward)


def merged(flags, own, recv, G, s, x, onward=None, flip=False, packed_out=False, order="", mib=16):
    n = 2 * s + 2 * x
    closing = onward is None
    fused = G is None
    E = 2 * x if closing else x
    K = 4 * s if closing else 4 * s + 2 * x
    packed_in = recv.shape != (n, n)
    if closing:
        h = K // 2
        shapes = [(h, h), (128, 128), (h, h), (8, K), (E, K), (E, K)]
        scratch = [pltpu.VMEM((K, K), F32)]
    else:
        seam = onward[0] * (2 if onward[1] else 1)
        shapes = [(K, K), (seam, seam)]
        if packed_out:
            shapes.append((packed_rows(K), 128))
        scratch = [pltpu.VMEM((E, K), F32), pltpu.VMEM((E, K), F32)]
    if packed_in:
        scratch.append(pltpu.VMEM((n, n), F32))
    return pl.pallas_call(
        functools.partial(merge_kernel, s, x, flip, closing, fused, packed_in, packed_out, order, onward),
        out_shape=[jax.ShapeDtypeStruct(shape, F32) for shape in shapes],
        in_specs=[SCALAR] + [WHOLE] * (2 if fused else 3),
        out_specs=[WHOLE] * len(shapes),
        scratch_shapes=scratch,
        compiler_params=limit(mib),
        name=f"merge_{E}_{K}",
    )(*((flags, own, recv) if fused else (flags, own, recv, G)))


def inner_kernel(flags_ref, map_ref, W_ref, X_ref, inner_ref, send_ref, packed_ref):
    h = map_ref.shape[0]
    for i in range(0, h, 256):
        inner_ref[i : i + 256, :] = map_ref[i : i + 256, :] - dot3(W_ref[:, i : i + 256], X_ref[:, 0:h], LEFT_T)
    pack(inner_ref, packed_ref)
    half = send_ref.shape[0] - 8
    send_ref[0:half, :] = packed_ref[pl.ds(pl.multiple_of(flags_ref[0] * half, half), half), :]
    send_ref[half : half + 8, :] = packed_ref[2 * half : 2 * half + 8, :]


def inner_map(flags, half_map, W, X):
    rows = packed_rows(half_map.shape[0])
    return pl.pallas_call(
        inner_kernel,
        out_shape=[jax.ShapeDtypeStruct(half_map.shape, F32), jax.ShapeDtypeStruct(((rows + 8) // 2, 128), F32)],
        in_specs=[SCALAR] + [WHOLE] * 3,
        out_specs=[WHOLE] * 2,
        scratch_shapes=[pltpu.VMEM((rows, 128), F32)],
        compiler_params=limit(16),
        cost_estimate=pl.CostEstimate(flops=2_000_000_000, bytes_accessed=6 << 20, transcendentals=0),
        name="inner",
    )(flags, half_map, W, X)


def coupling_kernel(flags_ref, reach_ref, edge_ref, W_ref, X_ref, reach_out, edge_out, wide_ref):
    h = reach_ref.shape[0]
    for i in range(0, h, 256):
        reach_out[i : i + 256, :] = reach_ref[i : i + 256, :] - dot3(W_ref[:, i : i + 256], X_ref[:, h : 2 * h], LEFT_T)
    row = flags_ref[2]
    at = pl.ds(pl.multiple_of(h + row // 128 * 128, 128), 128)
    wide_ref[...] = dot3(W_ref[:, at], X_ref[...], LEFT_T)
    edge_out[...] = edge_ref[...] - wide_ref[pl.ds(pl.multiple_of(row % 128, 8), 8), :]


def coupling(flags, reach, edge, W, X):
    return pl.pallas_call(
        coupling_kernel,
        out_shape=[jax.ShapeDtypeStruct(reach.shape, F32), jax.ShapeDtypeStruct(edge.shape, F32)],
        in_specs=[SCALAR] + [WHOLE] * 4,
        out_specs=[WHOLE] * 2,
        scratch_shapes=[pltpu.VMEM((128, edge.shape[1]), F32)],
        compiler_params=limit(16),
        cost_estimate=pl.CostEstimate(flops=3_000_000_000, bytes_accessed=8 << 20, transcendentals=0),
        name="coupling",
    )(flags, reach, edge, W, X)


RIGHT_T = (((1,), (1,)), ((), ()))


def eliminate(S_ref, R_ref, Q_ref, b, pivot):
    n = S_ref.shape[0]
    at, rest = slice(128 * b, 128 * b + 128), slice(128 * b + 128, n)
    Z = dot3(Q_ref[:, at], pivot)
    Q_ref[:, at] = Z
    if rest.start < n:
        row = S_ref[at, rest]
        R = dot3(pivot, row)
        R_ref[at, rest] = R
        S_ref[rest, rest] = S_ref[rest, rest] - dot3(row, R, LEFT_T)
        Q_ref[:, rest] = Q_ref[:, rest] - dot3(Z, row)


def interface_kernel(flags_ref, own_ref, near_ref, cross_ref, edge_ref, pivot_ref, S_out, R_out, Q_out, S_ref, packed_ref):
    n = own_ref.shape[0]
    half = near_ref.shape[0] - 8
    first = flags_ref[0] == 0
    near, cross = near_ref[...], cross_ref[...]
    packed_ref[0:half, :] = jnp.where(first, near, cross)[0:half]
    packed_ref[half : 2 * half, :] = jnp.where(first, cross, near)[0:half]
    packed_ref[2 * half : 2 * half + 8, :] = near[half : half + 8]
    unpack(packed_ref, S_ref)
    S_ref[...] += own_ref[...]
    Q_out[...] = edge_ref[:, 0:n]
    eliminate(S_ref, R_out, Q_out, 0, pivot_ref[...])
    for b in range(1, n // 128 - 1):
        at = slice(128 * b, 128 * b + 128)
        eliminate(S_ref, R_out, Q_out, b, inverse_small(S_ref[at, at]))
    S_out[...] = S_ref[n - 128 : n, n - 128 : n]


def interface(flags, own, near, cross, edge, pivot):
    E = own.shape[0]
    return pl.pallas_call(
        interface_kernel,
        out_shape=[jax.ShapeDtypeStruct(shape, F32) for shape in ((128, 128), (E - 128, E), (8, E))],
        in_specs=[SCALAR] + [WHOLE] * 5,
        out_specs=[WHOLE] * 3,
        scratch_shapes=[pltpu.VMEM((E, E), F32), pltpu.VMEM((packed_rows(E), 128), F32)],
        compiler_params=limit(16),
        cost_estimate=pl.CostEstimate(flops=1_000_000_000, bytes_accessed=4 << 20, transcendentals=0),
        name="interface",
    )(flags, own, near, cross, edge, pivot)


def solve_kernel(S_ref, R_ref, Q_ref, Y_ref):
    n = Q_ref.shape[1]
    last = slice(n - 128, n)
    Y_ref[:, last] = dot3(Q_ref[:, last], inverse_small(S_ref[...]))
    for b in range(n // 128 - 2, -1, -1):
        at, rest = slice(128 * b, 128 * b + 128), slice(128 * b + 128, n)
        Y_ref[:, at] = Q_ref[:, at] - dot3(Y_ref[:, rest], R_ref[at, rest], RIGHT_T)


def solve(S, R, Q):
    return pl.pallas_call(
        solve_kernel,
        out_shape=jax.ShapeDtypeStruct(Q.shape, F32),
        in_specs=[WHOLE] * 3,
        out_specs=WHOLE,
        compiler_params=limit(16),
        cost_estimate=pl.CostEstimate(flops=5_000_000_000, bytes_accessed=4 << 20, transcendentals=0),
        name="solve",
    )(S, R, Q)


def last_kernel(flags_ref, edge_ref, Y_ref, own_ref, near_ref, cross_ref, out_ref):
    E = own_ref.shape[0]
    h = E // 2
    Y = Y_ref[...]
    mine = edge_ref[:, E : 2 * E] - dot3(Y, own_ref[...])
    first = flags_ref[0] == 0
    near, cross = near_ref[...], cross_ref[...]
    low, high = jnp.where(first, near, cross), jnp.where(first, cross, near)
    other = -(dot3(Y[:, 0:h], low) + dot3(Y[:, h:E], high))
    left = flags_ref[1] == 1
    out_ref[:, 0:E] = jnp.where(left, mine, other)
    out_ref[:, E : 2 * E] = jnp.where(left, other, mine)


def last_rows(flags, edge, Y, own, near, cross):
    return pl.pallas_call(
        last_kernel,
        out_shape=jax.ShapeDtypeStruct((Y.shape[0], 2 * own.shape[0]), F32),
        in_specs=[SCALAR] + [WHOLE] * 5,
        out_specs=WHOLE,
        compiler_params=limit(16),
        name="last_rows",
    )(flags, edge, Y, own, near, cross)


def flipped(block, axis, mask):
    return lax.ppermute(block, axis, [(i, i ^ mask) for i in range(lax.axis_size(axis))])


def ordered(parts, index):
    low = (index & 1) == 1
    p0, p1 = jnp.where(low, parts[1], parts[0]), jnp.where(low, parts[0], parts[1])
    p2, p3 = jnp.where(low, parts[3], parts[2]), jnp.where(low, parts[2], parts[3])
    high = (index & 2) == 2
    return [jnp.where(high, p2, p0), jnp.where(high, p3, p1), jnp.where(high, p0, p2), jnp.where(high, p1, p3)]


def gathered_cells(classes):
    E = classes.shape[1]
    x = lax.axis_index("col")
    slab = lax.axis_index("slab")
    core, quarter = slab & 1, slab >> 1 & 1
    parts = [classes] + [flipped(classes, "col", k) for k in (1, 2, 3)]
    strip = jnp.concatenate(ordered(parts, x), axis=0)

    def pair(low, high, second):
        return jnp.concatenate([jnp.where(second, high, low), jnp.where(second, low, high)], axis=0)

    def share(block, index, length):
        return lax.dynamic_slice_in_dim(block, index * length, length, axis=1)

    upper = core == 1
    strip = pair(share(strip, core, E // 2), flipped(share(strip, 1 - core, E // 2), "slab", 1), upper)
    place = 2 * (x >> 1) + ((x ^ (x >> 1)) & 1)
    strip = jnp.stack([share(strip, k * 4 + place, N) for k in (0, 1)])
    mine = lax.dynamic_index_in_dim(strip, quarter, 0, keepdims=False)
    other = lax.dynamic_index_in_dim(strip, 1 - quarter, 0, keepdims=False)
    return pair(mine, flipped(other, "slab", 2), quarter == 1)


def local(classes, across_coeff, along_coeff):
    E = classes.shape[1]
    slab, col = lax.axis_index("slab"), lax.axis_index("col")
    core = slab & 1

    def bit(index, mask):
        return jnp.where((index & mask) != 0, 1, 0).astype(jnp.int32).reshape(1)

    left = bit(slab ^ 16, 16)
    share = 2 * E // (lax.axis_size("slab") * lax.axis_size("col"))
    row = (((slab & 15) * lax.axis_size("col") + col) * share).astype(jnp.int32).reshape(1)
    seconds = [bit(col ^ (col >> 1), 1), bit(slab, 4), bit(col, 2), bit(slab, 8), bit(slab, 2), bit(slab, 1)]

    def flags(k):
        return jnp.concatenate([seconds[k], left, row, seconds[min(k + 1, 5)]])

    swaps = [("col", 1), ("slab", 4), ("col", 3), ("slab", 8), ("slab", 2), ("slab", 1)]
    coeffs = jnp.stack([across_coeff, along_coeff])
    cells = gathered_cells(classes)
    pieces = None
    m, seam = block_map(seconds[0], jnp.concatenate([cells] * 4, axis=1), coeffs)
    sent = m
    sizes = [(32, 32), (32, 64), (64, 64), (64, 128), (128, 128)]
    for k, (s, x) in enumerate(sizes):
        G = None
        if k >= 2:
            other = flipped(seam, *swaps[k])
            if k == 4:
                sent, other = lax.optimization_barrier((sent, other))
            G = inverse(seam, other, x)
        recv = flipped(sent, *swaps[k])
        now = flags(k)
        if k == 0:
            held, m = lax.optimization_barrier((classes, m))
            rows, cols = piece_vectors(held, coeffs)
            now, rows = lax.optimization_barrier((now, rows))
        if k in (1, 4):
            rows, _ = lax.optimization_barrier((rows, G if k == 4 else seam))
            pieces = piece_part(rows, cols, pieces, 0 if k == 1 else 4, 4)
            now, pieces = lax.optimization_barrier((now, pieces))
        onward = (s * 2, False) if k < 4 else (x, True)
        if k == 3:
            onward = (x, False)
        order = {3: "swap", 4: "swapped"}.get(k, "")
        out = merged(now, m, recv, G, s, x, onward, flip=k < 4, packed_out=k > 0, order=order)
        m, seam, sent = out if k > 0 else (out[0], out[1], out[0])
    other = flipped(seam, *swaps[5])
    recv = flipped(sent, *swaps[5])
    G = inverse(seam, other, 128)
    half_map, seam, reach, edge, W, X = merged(flags(5), m, recv, G, 256, 128, order="swapped", mib=32)
    both = flags(5)
    other = flipped(seam, "slab", 16)
    inner, sent = inner_map(both, half_map, W, X)
    near = flipped(sent, "slab", 16)
    G = inverse(seam, other, 0)
    reach, edge = coupling(both, reach, edge, W, X)
    half = E // 2
    part = lax.dynamic_slice_in_dim(reach, core * half, half, 0)
    near, edge, G, part = lax.optimization_barrier((near, edge, G, part))
    part_recv = flipped(part, "slab", 16)
    S, R, Q = interface(both, inner, near, flipped(near, "slab", 1), edge, G)
    part, Q = lax.optimization_barrier((part_recv, Q))
    Y = solve(S, R, Q)
    root_rows = last_rows(both, edge, Y, reach, part, flipped(part, "slab", 1))
    return (pieces.reshape(2 * E, 2 * E), root_rows)


def solution(mesh):
    placed = P(("slab", "col"), None)
    return jax.shard_map(
        local,
        mesh=mesh,
        in_specs=(placed, P(), P()),
        out_specs=(placed, placed),
        check_vma=False,
    )
```

```python
import functools
import jax
import jax.numpy as jnp
from jax import lax
from jax.experimental import pallas as pl
from jax.experimental.pallas import tpu as pltpu
from jax.sharding import PartitionSpec as P

F32 = jnp.float32
BF16 = jnp.bfloat16
PLAIN = (((1,), (0,)), ((), ()))
LEFT_T = (((0,), (0,)), ((), ()))


SCALAR = pl.BlockSpec(memory_space=pltpu.SMEM)
WHOLE = pl.BlockSpec(memory_space=pltpu.VMEM)


def limit(mib):
    return pltpu.CompilerParams(vmem_limit_bytes=mib << 20)


def split(x):
    high = x.astype(BF16)
    return high, (x - high.astype(F32)).astype(BF16)


def dot3(left, right, dims=PLAIN):
    lh, ll = split(left)
    rh, rl = split(right)
    dot = functools.partial(lax.dot_general, dimension_numbers=dims, preferred_element_type=F32)
    return dot(lh, rh) + (dot(lh, rl) + dot(ll, rh))


def total(terms):
    terms = list(terms)
    out = terms[0]
    for term in terms[1:]:
        out = out + term
    return out


def small_inverse(s):
    size = max(i for i, _ in s) + 1
    if size == 1:
        return {(0, 0): 1.0 / s[0, 0]}
    if size == 2:
        a, b, d = s[0, 0], s[0, 1], s[1, 1]
        r = 1.0 / (a * d - b * b)
        return {(0, 0): d * r, (0, 1): -(b * r), (1, 1): a * r}
    h = size // 2
    both = range(h)

    def at(m, i, j):
        return m[min(i, j), max(i, j)]

    A = small_inverse({(i, j): s[i, j] for i in both for j in range(i, h)})
    X = {(i, j): total(at(A, i, k) * s[k, h + j] for k in both) for i in both for j in both}
    S = {(i, j): s[h + i, h + j] - total(s[k, h + i] * X[k, j] for k in both) for i in both for j in range(i, h)}
    S = small_inverse(S)
    Y = {(i, j): -total(X[i, k] * at(S, k, j) for k in both) for i in both for j in both}
    out = {}
    for i in both:
        for j in range(i, h):
            out[i, j] = A[i, j] - total(Y[i, k] * X[j, k] for k in both)
            out[h + i, h + j] = S[i, j]
        for j in both:
            out[i, h + j] = Y[i, j]
    return out


def panel_sweep(tiles, n, spread, lane, size=4):
    shape = tiles[0].shape
    sub = lax.broadcasted_iota(jnp.int32, shape, 0)
    tiles = list(tiles)
    per = n // 8
    groups = len(tiles) // per
    each = range(size)
    upper = [(i, j) for i in each for j in range(i, size)]

    def at(m, i, j):
        return m[min(i, j), max(i, j)]

    def row_of(tile, r):
        return jnp.broadcast_to(tile[r % 8 : r % 8 + 1, :], shape)

    blocks = [None] * groups
    for k in range(0, n, size):
        inside = (lane >= k) & (lane < k + size)
        units = [jnp.where(lane == k + j, 1.0, 0.0) for j in each]
        here, later = k // 8, (k + size) // 8
        for q in range(groups):
            mine = tiles[q * per : (q + 1) * per]
            C = [[spread(t, k + j) for t in mine] for j in each]
            R = [row_of(mine[here], k + j) for j in each]
            if k == 0:
                blocks[q] = {(i, j): row_of(C[j][here], i) for i, j in upper}
            G = small_inverse(blocks[q])
            if k + size < n:
                near = [spread(mine[here], k + size + j) for j in each]
                far = near if here == later else [spread(mine[later], k + size + j) for j in each]
                u = {(i, j): row_of(near[j], k + i) for i in each for j in each}
                v = {(i, j): row_of(far[j], k + size + i) for i, j in upper}
                T = {(i, j): total(at(G, i, m) * u[m, j] for m in each) for i in each for j in each}
                blocks[q] = {(i, j): v[i, j] - total(u[m, i] * T[m, j] for m in each) for i, j in upper}
            R = [jnp.where(inside, units[j], R[j]) for j in each]
            scaled = [total(at(G, i, j) * R[j] for j in each) for i in each]
            for t in range(per):
                new = jnp.where(inside, 0.0, mine[t]) - total(C[j][t] * scaled[j] for j in each)
                if t == here:
                    for j in each:
                        new = jnp.where(sub == (k + j) % 8, scaled[j], new)
                tiles[q * per + t] = new
    return tiles


def inverse_small(A):
    n = A.shape[0]
    lane = lax.broadcasted_iota(jnp.int32, (8, n), 1)
    tiles = [A[i : i + 8, :] for i in range(0, n, 8)]

    def spread(tile, k):
        return jnp.broadcast_to(tile[:, k : k + 1], (8, n))

    return jnp.concatenate(panel_sweep(tiles, n, spread, lane), axis=0)


def inverse_blocks(A_ref, n):
    lane = lax.broadcasted_iota(jnp.int32, (1, n), 1)

    def step(b, carry):
        at = pl.ds(pl.multiple_of(b * 128, 128), 128)
        row = A_ref[at, :]
        col = A_ref[:, at]
        pivot = inverse_small(A_ref[at, at])
        inside = (lane >= b * 128) & (lane < b * 128 + 128)
        scaled = dot3(pivot, row)
        wide = jnp.concatenate([pivot] * (n // 128), axis=1)
        scaled = jnp.where(inside, wide, scaled)
        A_ref[...] = jnp.where(inside, 0.0, A_ref[...]) - dot3(col, scaled)
        A_ref[at, :] = scaled
        return carry

    lax.fori_loop(0, n // 128, step, 0)


def pick(levels, table_ref, which):
    values = jnp.zeros(levels.shape, F32)
    for k in range(table_ref.shape[1]):
        values = jnp.where(levels == k, table_ref[which, k], values)
    return values


def piece_prelude(cls_ref, coeff_ref, rows_ref, cols_ref):
    E = cls_ref.shape[1]
    across = pick(cls_ref[...], coeff_ref, 0)
    along = pick(cls_ref[...], coeff_ref, 1)
    d0, d1 = across[0:1], across[1:2]
    v0, a = along[0:1], along[1:2]
    v0_prev, a_prev = jnp.roll(v0, 1, axis=1), jnp.roll(a, 1, axis=1)
    diag = d0 + d1 + a + a_prev
    down, up = diag, diag
    for _ in range(14):
        down = diag - a_prev * a_prev / jnp.roll(down, 1, axis=1)
        up = diag - a * a / jnp.roll(up, -1, axis=1)
    g = 1.0 / (down + up - diag)
    step_p = jnp.log(down / a)
    step_q = jnp.log(up / a_prev)
    ph = jnp.floor(step_p * 256.0 + 0.5) * (1.0 / 256.0)
    qh = jnp.floor(step_q * 256.0 + 0.5) * (1.0 / 256.0)
    steps = jnp.concatenate([ph, step_p - ph, qh, step_q - qh, d0, d1, d0, d1], axis=0)
    lane8 = lax.broadcasted_iota(jnp.int32, (8, E), 1)
    sums = steps
    width = 1
    while width < E:
        sums = sums + jnp.where(lane8 >= width, jnp.roll(sums, width, axis=1), 0.0)
        width *= 2
    total = sums[:, E - 1 : E]
    ph_before, pl_before = sums[0:1] - steps[0:1], sums[1:2] - steps[1:2]
    rows = jnp.concatenate([ph_before, pl_before, sums[2:4], d0, d1, d0 + v0 + v0_prev, v0], axis=0)
    tall = jnp.concatenate([rows, jnp.zeros((120, E), F32)], axis=0)
    cols_ref[...] = tall.T
    pt_h, pt_l, qt_h, qt_l = total[0:1], total[1:2], total[2:3], total[3:4]
    wrap_p = 1.0 / (1.0 - jnp.exp(-(pt_h + pt_l)))
    wrap_q = 1.0 / (1.0 - jnp.exp(-(qt_h + qt_l)))
    more = [g * wrap_p, g * wrap_q, g, v0_prev]
    more += [jnp.broadcast_to(t, (1, E)) for t in (pt_h, pt_l, qt_h, qt_l)]
    rows_ref[0:8, :] = rows
    rows_ref[8:16, :] = jnp.concatenate(more, axis=0)


def piece_kernel(start, rows_ref, cols_ref, *refs):
    out_ref = refs[-1]
    step = pl.program_id(0) + start
    R, E = out_ref.shape[1], cols_ref.shape[0]
    row = [rows_ref[k : k + 1, :] for k in range(16)]
    c = cols_ref[pl.ds(pl.multiple_of(step * R, R), R), :]
    lane = lax.broadcasted_iota(jnp.int32, (R, E), 1)
    index = lax.broadcasted_iota(jnp.int32, (R, E), 0) + step * R
    later, earlier = lane < index, index < lane
    p = (row[0] - c[:, 0:1]) + jnp.where(later, row[12], 0.0)
    p = p + ((row[1] - c[:, 1:2]) + jnp.where(later, row[13], 0.0))
    q = (c[:, 2:3] - row[2]) + jnp.where(earlier, row[14], 0.0)
    q = q + ((c[:, 3:4] - row[3]) + jnp.where(earlier, row[15], 0.0))
    same = lane == index
    G = row[8] * jnp.exp(-p) + row[9] * jnp.exp(-q) - jnp.where(same, row[10], 0.0)
    d0, d1 = row[4], row[5]
    G0, G1 = G * d0, G * d1
    c0, c1 = c[:, 4:5], c[:, 5:6]
    after = lane == jnp.where(index == E - 1, 0, index + 1)
    before = lane == jnp.where(index == 0, E - 1, index - 1)
    top = jnp.where(same, row[6], 0.0) - jnp.where(after, row[11], 0.0) - jnp.where(before, row[7], 0.0)
    out_ref[0, :, 0:E] = top - c0 * G0
    out_ref[0, :, E : 2 * E] = -(c0 * G1)
    out_ref[1, :, 0:E] = -(c1 * G0)
    out_ref[1, :, E : 2 * E] = jnp.where(same, d1, 0.0) - c1 * G1


def piece_vectors(classes, coeffs):
    E = classes.shape[1]
    return pl.pallas_call(
        piece_prelude,
        out_shape=[jax.ShapeDtypeStruct((16, E), F32), jax.ShapeDtypeStruct((E, 128), F32)],
        in_specs=[WHOLE, SCALAR],
        out_specs=[WHOLE, WHOLE],
        compiler_params=limit(8),
        cost_estimate=pl.CostEstimate(flops=20_000_000, bytes_accessed=6 << 20, transcendentals=0),
        name="piece_vectors",
    )(classes, coeffs)


def piece_part(rows, cols, done, start, count):
    E = cols.shape[0]
    R = E // 8
    old = [] if done is None else [done]
    return pl.pallas_call(
        functools.partial(piece_kernel, start),
        grid=(count,),
        out_shape=jax.ShapeDtypeStruct((2, E, 2 * E), F32),
        in_specs=[WHOLE, WHOLE] + [pl.BlockSpec(memory_space=pl.ANY)] * len(old),
        out_specs=pl.BlockSpec((2, R, 2 * E), lambda i: (0, i + start, 0)),
        input_output_aliases={2: 0} if old else {},
        compiler_params=limit(8),
        cost_estimate=pl.CostEstimate(flops=20_000_000, bytes_accessed=count << 21, transcendentals=0),
        name=f"piece_part_{start}",
    )(rows, cols, *old)


N = 32


def block_kernel(second_ref, cls_ref, coeff_ref, out_ref, seam_ref, maps, vals, packs):
    lane1 = lax.broadcasted_iota(jnp.int32, (1, 128), 1)
    lane = lax.broadcasted_iota(jnp.int32, (128, 128), 1)
    sub = lax.broadcasted_iota(jnp.int32, (128, 128), 0)
    across = pick(cls_ref[...], coeff_ref, 0)
    along = pick(cls_ref[...], coeff_ref, 1)
    vals[0:32, :] = across
    vals[32:64, :] = along
    vals[64:96, :] = jnp.where(lane1 % N == 0, 0.0, jnp.roll(along, 1, axis=1))
    vals[96:128, :] = jnp.broadcast_to(along[:, N - 1 : N], (N, 128))
    low = jnp.where(sub < N, sub, -1000)
    is_diag = low == lane
    is_after = (low + 1 == lane) & (lane < N)
    is_before = (low == lane + 1)
    mid_diag = (sub == lane) & (sub >= N) & (sub < 2 * N)
    cross = ((low + N == lane) & (lane < 2 * N)) | ((lane < N) & (sub == lane + N))

    def first(c, carry):
        ac = vals[pl.ds(c, 1), :]
        al = vals[pl.ds(c + 32, 1), :]
        al_prev = vals[pl.ds(c + 64, 1), :]
        al_last = vals[pl.ds(c + 96, 1), :]
        m = jnp.where(is_diag, ac + al + al_prev, 0.0)
        m = m - jnp.where(is_after, al_prev, 0.0) - jnp.where(is_before, al, 0.0)
        m = m + jnp.where(mid_diag, ac, 0.0) - jnp.where(cross, ac, 0.0)
        slot = 3 * N + c
        ends = ((sub == N - 1) & (lane == slot)) | ((sub == slot) & (lane == N - 1))
        m = m - jnp.where(ends, al_last, 0.0)
        m = m + jnp.where((sub == slot) & (lane == slot), al_last, 0.0)
        maps[c] = m
        return carry

    lax.fori_loop(0, N, first, 0)

    seg1 = lane1 // N
    seg = lane // N
    subN = lax.broadcasted_iota(jnp.int32, (N, 128), 0)
    laneN = lax.broadcasted_iota(jnp.int32, (N, 128), 1)
    row_R = (sub >= N) & (sub < 2 * N)
    row_L = sub < N
    col_R = (lane >= N) & (lane < 2 * N)
    col_L = lane < N
    colR1 = (lane1 >= N) & (lane1 < 2 * N)
    colL1 = lane1 < N
    drop_a = row_R | col_R
    drop_b = row_L | col_L
    edge = (subN == 0) | (laneN % N == 0)
    corner = (subN == 0) & (laneN % N == 0)
    blockdiag = (sub // N) == seg

    lane8 = lax.broadcasted_iota(jnp.int32, (8, 128), 1)
    base8 = lane8 // N * N

    def spread(tile, k):
        return jnp.take_along_axis(tile, base8 + k, axis=1)

    count = N // 2
    span = 1
    while count >= 1:
        quads = max(count // 4, 1)
        live = min(count, 4)

        def gather(q, carry, live=live):
            packed = jnp.zeros((N, 128), F32)
            for i in range(live):
                a_rows = maps[q * 8 + 2 * i, N : 2 * N, :]
                b_rows = maps[q * 8 + 2 * i + 1, 0:N, :]
                piece = jnp.where(colR1, a_rows, 0.0)
                piece = jnp.roll(piece, N * (i - 1), axis=1) if i != 1 else piece
                other = jnp.where(colL1, b_rows, 0.0)
                other = jnp.roll(other, N * i, axis=1) if i else other
                packed = packed + piece + other
            packs[q] = jnp.where(corner, 1.0, jnp.where(edge, 0.0, packed))
            return carry

        lax.fori_loop(0, quads, gather, 0)

        done = panel_sweep(
            [packs[q, 8 * i : 8 * i + 8, :] for q in range(quads) for i in range(N // 8)], N, spread, lane8 % N
        )
        for q in range(quads):
            for i in range(N // 8):
                packs[q, 8 * i : 8 * i + 8, :] = done[q * (N // 8) + i]

        def merge(q, carry, live=live, span=span):
            G = packs[q]
            G4 = jnp.where(blockdiag, jnp.concatenate([G] * 4, axis=0), 0.0)
            sides = []
            fronts = []
            for i in range(4):
                if i >= live:
                    sides.append(jnp.zeros((N, 128), F32))
                    continue
                a = maps[q * 8 + 2 * i]
                b = maps[q * 8 + 2 * i + 1]
                t = 2 * N + (q * 8 + 2 * i + 1) * span
                a_rows, b_rows = a[N : 2 * N], b[0:N]
                W = jnp.where(colR1, 0.0, a_rows) + jnp.where(colL1, 0.0, b_rows)
                a_col, b_col = a[:, N : N + 1], b[:, 0:1]
                at_lane = lane1 == t
                into = a_col[N : 2 * N] + b_col[0:N]
                w_row = W[0:1]
                W = W + jnp.where(at_lane, into, 0.0)
                W = jnp.where(subN == 0, 0.0, W)
                F = jnp.where(drop_a, 0.0, a) + jnp.where(drop_b, 0.0, b)
                kept_col = jnp.where(row_R[:, :1], 0.0, a_col) + jnp.where(row_L[:, :1], 0.0, b_col)
                F = F + jnp.where(at_lane, kept_col, 0.0)
                F = F + jnp.where(sub == t, w_row + jnp.where(at_lane, into[0:1], 0.0), 0.0)
                sides.append(W)
                fronts.append(F)
            stack = jnp.concatenate(sides, axis=0)
            X = dot3(G4, stack)
            for i in range(live):
                part = dot3(sides[i], X[i * N : (i + 1) * N], LEFT_T)
                maps[q * 4 + i] = fronts[i] - part
            return carry

        lax.fori_loop(0, quads, merge, 0)
        count //= 2
        span *= 2
    out_ref[...] = maps[0]
    hand_on(out_ref, seam_ref, second_ref[0] == 1, N, False)


def block_map(second, cells, coeffs):
    return pl.pallas_call(
        block_kernel,
        out_shape=[jax.ShapeDtypeStruct((128, 128), F32), jax.ShapeDtypeStruct((N, N), F32)],
        in_specs=[SCALAR, WHOLE, SCALAR],
        out_specs=[WHOLE, WHOLE],
        scratch_shapes=[
            pltpu.VMEM((N, 128, 128), F32),
            pltpu.VMEM((128, 128), F32),
            pltpu.VMEM((4, N, 128), F32),
        ],
        compiler_params=pltpu.CompilerParams(vmem_limit_bytes=8 << 20),
        name="block_map",
    )(second, cells, coeffs)


def packing(n):
    count = n // 128
    above = [(i, j) for i in range(count) for j in range(i + 1, count)]
    return above, [(i, i + 1 if i + 1 < count else None) for i in range(0, count, 2)]


def packed_rows(n):
    above, twos = packing(n)
    return 128 * (len(above) + len(twos)) + 8


def diagonal_masks():
    row = lax.broadcasted_iota(jnp.int32, (128, 128), 0)
    lane = lax.broadcasted_iota(jnp.int32, (128, 128), 1)
    return row < lane, row == lane


def pack(full_ref, packed_ref):
    above, twos = packing(full_ref.shape[0])
    upper, diagonal = diagonal_masks()

    def block(i, j):
        return full_ref[128 * i : 128 * i + 128, 128 * j : 128 * j + 128]

    for k, (i, j) in enumerate(above):
        packed_ref[128 * k : 128 * k + 128, :] = block(i, j)
    last = 128 * (len(above) + len(twos))
    packed_ref[last : last + 8, :] = jnp.zeros((8, 128), F32)
    for m, (i, j) in enumerate(twos):
        at = 128 * (len(above) + m)
        if j is None:
            packed_ref[at : at + 128, :] = block(i, i)
        else:
            lower = block(j, j)
            packed_ref[at : at + 128, :] = jnp.where(upper | diagonal, block(i, i), lower)
            packed_ref[last + m : last + m + 1, :] = jnp.sum(jnp.where(diagonal, lower, 0.0), axis=0, keepdims=True)


def unpack(packed_ref, full_ref):
    above, twos = packing(full_ref.shape[0])
    upper, diagonal = diagonal_masks()

    def put(i, j, value):
        full_ref[128 * i : 128 * i + 128, 128 * j : 128 * j + 128] = value

    for k, (i, j) in enumerate(above):
        block = packed_ref[128 * k : 128 * k + 128, :]
        put(i, j, block)
        put(j, i, block.T)
    last = 128 * (len(above) + len(twos))
    for m, (i, j) in enumerate(twos):
        at = 128 * (len(above) + m)
        block = packed_ref[at : at + 128, :]
        if j is None:
            put(i, i, block)
        else:
            turned = block.T
            put(i, i, jnp.where(upper | diagonal, block, turned))
            entries = packed_ref[last + m : last + m + 1, :]
            put(j, j, jnp.where(upper, turned, jnp.where(diagonal, entries, block)))


def hand_on(map_ref, seam_ref, second, x, closing):
    n = map_ref.shape[0]
    X, Y = (n - 2 * x, n - x), (n - x, n)
    if not closing:
        first, other = map_ref[Y[0] : Y[1], Y[0] : Y[1]], map_ref[X[0] : X[1], X[0] : X[1]]
        seam_ref[...] = jnp.where(second, other, first)
        return
    for i, rows in enumerate((Y, X)):
        for j, cols in enumerate((Y, X)):
            flip_rows, flip_cols = (X, Y)[i], (X, Y)[j]
            first = map_ref[rows[0] : rows[1], cols[0] : cols[1]]
            other = map_ref[flip_rows[0] : flip_rows[1], flip_cols[0] : flip_cols[1]]
            seam_ref[i * x : i * x + x, j * x : j * x + x] = jnp.where(second, other, first)


def seam_matrix(A, x):
    E = A.shape[0]
    row = lax.broadcasted_iota(jnp.int32, (E, 1), 0)
    lane = lax.broadcasted_iota(jnp.int32, (1, E), 1)
    return jnp.where((row % x == 0) | (lane % x == 0), jnp.where(row == lane, 1.0, 0.0), A)


def seam_inverse(A, x):
    return inverse_small(seam_matrix(A, x))


def inverse_kernel(x, own_ref, recv_ref, out_ref):
    A = own_ref[...] + recv_ref[...]
    if A.shape[0] <= 128:
        out_ref[...] = seam_inverse(A, x) if x else inverse_small(A)
    else:
        out_ref[...] = seam_matrix(A, x)
        inverse_blocks(out_ref, A.shape[0])


def inverse(own, recv, x):
    E = own.shape[0]
    return pl.pallas_call(
        functools.partial(inverse_kernel, x),
        out_shape=jax.ShapeDtypeStruct((E, E), F32),
        in_specs=[WHOLE, WHOLE],
        out_specs=WHOLE,
        compiler_params=limit(8),
        cost_estimate=pl.CostEstimate(flops=40_000_000 * E, bytes_accessed=E * E * 12, transcendentals=0),
        name=f"inverse_{E}",
    )(own, recv)


def merge_kernel(s, x, flip, closing, fused, packed_in, packed_out, order, onward, *refs):
    flags_ref, own_ref, recv_ref = refs[:3]
    refs = list(refs[3:])
    G_ref = None if fused else refs.pop(0)
    if closing:
        inner_ref, first_ref, coupling_ref, edge_ref, W_ref, X_ref, out_ref = refs[:7]
        rest = refs[7:]
    else:
        out_ref = refs.pop(0)
        seam_ref = refs.pop(0)
        packed_ref = refs.pop(0) if packed_out else None
        W_ref, X_ref = refs[:2]
        rest = refs[2:]
    if packed_in:
        full_ref = rest[0]
        unpack(recv_ref, full_ref)
        recv_ref = full_ref
    second = flags_ref[0] == 1
    offsets = {"S1": (0, s), "S2": (s, s), "X": (2 * s, x), "Y": (2 * s + x, x)}

    def block(which, rows, cols, width=0):
        (r, nr), (c, nc) = offsets[rows], offsets[cols]
        nc = width or nc
        own = own_ref[r : r + nr, c : c + nc]
        recv = recv_ref[r : r + nr, c : c + nc]
        if which == "a":
            return jnp.where(second, recv, own)
        return jnp.where(second, own, recv)

    K = out_ref.shape[0]
    if closing:
        kept = {"a": {"S1": 0, "S2": 2 * s}, "b": {"S1": s, "S2": 3 * s}}
        gone = {"a": {"Y": 0, "X": x}, "b": {"X": 0, "Y": x}}
    else:
        sides, ends = (2 * x, 0) if flip else (0, 4 * s)
        kept = {
            "a": {"S1": sides, "S2": sides + 2 * s, "X": ends},
            "b": {"S1": sides + s, "S2": sides + 3 * s, "Y": ends + x},
        }
        gone = {"a": {"Y": 0}, "b": {"X": 0}}

    for which in "ab":
        for rows, r in kept[which].items():
            nr = offsets[rows][1]
            for cols, c in kept[which].items():
                out_ref[r : r + nr, c : c + offsets[cols][1]] = block(which, rows, cols)
            for cols, c in kept["b" if which == "a" else "a"].items():
                nc = offsets[cols][1]
                out_ref[r : r + nr, c : c + nc] = jnp.zeros((nr, nc), F32)
        for rows, r in gone[which].items():
            for cols, c in kept[which].items():
                W_ref[r : r + x, c : c + offsets[cols][1]] = block(which, rows, cols)

    def fold(side):
        targets = [(0, kept["b"][side])]
        if closing:
            targets.append((x, kept["a"][side]))
        for e, t in targets:
            tb = t // 128 * 128
            tw = min(128, K - tb)
            lane = lax.broadcasted_iota(jnp.int32, (1, tw), 1)
            hit = lane == t - tb
            out_ref[t : t + 1, :] += W_ref[e : e + 1, :]
            for which in "ab":
                for cols, c in gone[which].items():
                    if c != e:
                        continue
                    for rows, r in kept[which].items():
                        nr = offsets[rows][1]
                        vec = block(which, rows, cols, 1)
                        out_ref[r : r + nr, tb : tb + tw] += jnp.where(hit, vec, 0.0)
                    for rows, r in gone[which].items():
                        vec = block(which, rows, cols, 1)
                        W_ref[r : r + x, tb : tb + tw] += jnp.where(hit, vec, 0.0)
                        if r == e:
                            out_ref[t : t + 1, tb : tb + tw] += jnp.where(hit, vec[0:1], 0.0)

    if order == "swapped":
        swapped = flags_ref[1] == 1
        pl.when(swapped)(lambda: fold("S2"))
        pl.when(jnp.logical_not(swapped))(lambda: fold("S1"))
    else:
        fold("S1")
    for e in (0, x) if closing else (0,):
        W_ref[e : e + 1, :] = jnp.zeros((1, K), F32)
    G = seam_inverse(block("a", "Y", "Y") + block("b", "X", "X"), x) if fused else G_ref[...]
    X_ref[...] = dot3(G, W_ref[...])
    if closing:
        h = K // 2
        first_ref[...] = out_ref[0:128, 0:128] - dot3(W_ref[:, 0:128], X_ref[:, 0:128], LEFT_T)
        inner_ref[...] = out_ref[0:h, 0:h]
        coupling_ref[...] = out_ref[0:h, h:K]
        edge_ref[...] = out_ref[pl.ds(pl.multiple_of(h + flags_ref[2], 8), 8), :]
        return
    R = min(K, 256) if K % 256 == 0 else min(K, 128) if K % 128 == 0 else K
    for i in range(0, K, R):
        out_ref[i : i + R, :] = out_ref[i : i + R, :] - dot3(W_ref[:, i : i + R], X_ref[...], LEFT_T)
    if order == "swap":

        @pl.when(flags_ref[1] == 1)
        def _():
            first, other = out_ref[0:x, :], out_ref[x : 2 * x, :]
            out_ref[0:x, :] = other
            out_ref[x : 2 * x, :] = first
            first, other = out_ref[:, 0:x], out_ref[:, x : 2 * x]
            out_ref[:, 0:x] = other
            out_ref[:, x : 2 * x] = first

    if packed_out:
        pack(out_ref, packed_ref)
    hand_on(out_ref, seam_ref, flags_ref[3] == 1, *onward)


def merged(flags, own, recv, G, s, x, onward=None, flip=False, packed_out=False, order="", mib=16):
    n = 2 * s + 2 * x
    closing = onward is None
    fused = G is None
    E = 2 * x if closing else x
    K = 4 * s if closing else 4 * s + 2 * x
    packed_in = recv.shape != (n, n)
    if closing:
        h = K // 2
        shapes = [(h, h), (128, 128), (h, h), (8, K), (E, K), (E, K)]
        scratch = [pltpu.VMEM((K, K), F32)]
    else:
        seam = onward[0] * (2 if onward[1] else 1)
        shapes = [(K, K), (seam, seam)]
        if packed_out:
            shapes.append((packed_rows(K), 128))
        scratch = [pltpu.VMEM((E, K), F32), pltpu.VMEM((E, K), F32)]
    if packed_in:
        scratch.append(pltpu.VMEM((n, n), F32))
    return pl.pallas_call(
        functools.partial(merge_kernel, s, x, flip, closing, fused, packed_in, packed_out, order, onward),
        out_shape=[jax.ShapeDtypeStruct(shape, F32) for shape in shapes],
        in_specs=[SCALAR] + [WHOLE] * (2 if fused else 3),
        out_specs=[WHOLE] * len(shapes),
        scratch_shapes=scratch,
        compiler_params=limit(mib),
        name=f"merge_{E}_{K}",
    )(*((flags, own, recv) if fused else (flags, own, recv, G)))


def inner_kernel(flags_ref, map_ref, W_ref, X_ref, inner_ref, send_ref, packed_ref):
    h = map_ref.shape[0]
    for i in range(0, h, 256):
        inner_ref[i : i + 256, :] = map_ref[i : i + 256, :] - dot3(W_ref[:, i : i + 256], X_ref[:, 0:h], LEFT_T)
    pack(inner_ref, packed_ref)
    half = send_ref.shape[0] - 8
    send_ref[0:half, :] = packed_ref[pl.ds(pl.multiple_of(flags_ref[0] * half, half), half), :]
    send_ref[half : half + 8, :] = packed_ref[2 * half : 2 * half + 8, :]


def inner_map(flags, half_map, W, X):
    rows = packed_rows(half_map.shape[0])
    return pl.pallas_call(
        inner_kernel,
        out_shape=[jax.ShapeDtypeStruct(half_map.shape, F32), jax.ShapeDtypeStruct(((rows + 8) // 2, 128), F32)],
        in_specs=[SCALAR] + [WHOLE] * 3,
        out_specs=[WHOLE] * 2,
        scratch_shapes=[pltpu.VMEM((rows, 128), F32)],
        compiler_params=limit(16),
        cost_estimate=pl.CostEstimate(flops=2_000_000_000, bytes_accessed=6 << 20, transcendentals=0),
        name="inner",
    )(flags, half_map, W, X)


def coupling_kernel(flags_ref, reach_ref, edge_ref, W_ref, X_ref, reach_out, edge_out, wide_ref):
    h = reach_ref.shape[0]
    for i in range(0, h, 256):
        reach_out[i : i + 256, :] = reach_ref[i : i + 256, :] - dot3(W_ref[:, i : i + 256], X_ref[:, h : 2 * h], LEFT_T)
    row = flags_ref[2]
    at = pl.ds(pl.multiple_of(h + row // 128 * 128, 128), 128)
    wide_ref[...] = dot3(W_ref[:, at], X_ref[...], LEFT_T)
    edge_out[...] = edge_ref[...] - wide_ref[pl.ds(pl.multiple_of(row % 128, 8), 8), :]


def coupling(flags, reach, edge, W, X):
    return pl.pallas_call(
        coupling_kernel,
        out_shape=[jax.ShapeDtypeStruct(reach.shape, F32), jax.ShapeDtypeStruct(edge.shape, F32)],
        in_specs=[SCALAR] + [WHOLE] * 4,
        out_specs=[WHOLE] * 2,
        scratch_shapes=[pltpu.VMEM((128, edge.shape[1]), F32)],
        compiler_params=limit(16),
        cost_estimate=pl.CostEstimate(flops=3_000_000_000, bytes_accessed=8 << 20, transcendentals=0),
        name="coupling",
    )(flags, reach, edge, W, X)


RIGHT_T = (((1,), (1,)), ((), ()))


def eliminate(S_ref, R_ref, Q_ref, b, pivot):
    n = S_ref.shape[0]
    at, rest = slice(128 * b, 128 * b + 128), slice(128 * b + 128, n)
    Z = dot3(Q_ref[:, at], pivot)
    Q_ref[:, at] = Z
    if rest.start < n:
        row = S_ref[at, rest]
        R = dot3(pivot, row)
        R_ref[at, rest] = R
        S_ref[rest, rest] = S_ref[rest, rest] - dot3(row, R, LEFT_T)
        Q_ref[:, rest] = Q_ref[:, rest] - dot3(Z, row)


def interface_kernel(flags_ref, own_ref, near_ref, cross_ref, edge_ref, pivot_ref, S_out, R_out, Q_out, S_ref, packed_ref):
    n = own_ref.shape[0]
    half = near_ref.shape[0] - 8
    first = flags_ref[0] == 0
    near, cross = near_ref[...], cross_ref[...]
    packed_ref[0:half, :] = jnp.where(first, near, cross)[0:half]
    packed_ref[half : 2 * half, :] = jnp.where(first, cross, near)[0:half]
    packed_ref[2 * half : 2 * half + 8, :] = near[half : half + 8]
    unpack(packed_ref, S_ref)
    S_ref[...] += own_ref[...]
    Q_out[...] = edge_ref[:, 0:n]
    eliminate(S_ref, R_out, Q_out, 0, pivot_ref[...])
    for b in range(1, n // 128 - 1):
        at = slice(128 * b, 128 * b + 128)
        eliminate(S_ref, R_out, Q_out, b, inverse_small(S_ref[at, at]))
    S_out[...] = S_ref[n - 128 : n, n - 128 : n]


def interface(flags, own, near, cross, edge, pivot):
    E = own.shape[0]
    return pl.pallas_call(
        interface_kernel,
        out_shape=[jax.ShapeDtypeStruct(shape, F32) for shape in ((128, 128), (E - 128, E), (8, E))],
        in_specs=[SCALAR] + [WHOLE] * 5,
        out_specs=[WHOLE] * 3,
        scratch_shapes=[pltpu.VMEM((E, E), F32), pltpu.VMEM((packed_rows(E), 128), F32)],
        compiler_params=limit(16),
        cost_estimate=pl.CostEstimate(flops=1_000_000_000, bytes_accessed=4 << 20, transcendentals=0),
        name="interface",
    )(flags, own, near, cross, edge, pivot)


def solve_kernel(S_ref, R_ref, Q_ref, Y_ref):
    n = Q_ref.shape[1]
    last = slice(n - 128, n)
    Y_ref[:, last] = dot3(Q_ref[:, last], inverse_small(S_ref[...]))
    for b in range(n // 128 - 2, -1, -1):
        at, rest = slice(128 * b, 128 * b + 128), slice(128 * b + 128, n)
        Y_ref[:, at] = Q_ref[:, at] - dot3(Y_ref[:, rest], R_ref[at, rest], RIGHT_T)


def solve(S, R, Q):
    return pl.pallas_call(
        solve_kernel,
        out_shape=jax.ShapeDtypeStruct(Q.shape, F32),
        in_specs=[WHOLE] * 3,
        out_specs=WHOLE,
        compiler_params=limit(16),
        cost_estimate=pl.CostEstimate(flops=5_000_000_000, bytes_accessed=4 << 20, transcendentals=0),
        name="solve",
    )(S, R, Q)


def last_kernel(flags_ref, edge_ref, Y_ref, own_ref, near_ref, cross_ref, out_ref):
    E = own_ref.shape[0]
    h = E // 2
    Y = Y_ref[...]
    mine = edge_ref[:, E : 2 * E] - dot3(Y, own_ref[...])
    first = flags_ref[0] == 0
    near, cross = near_ref[...], cross_ref[...]
    low, high = jnp.where(first, near, cross), jnp.where(first, cross, near)
    other = -(dot3(Y[:, 0:h], low) + dot3(Y[:, h:E], high))
    left = flags_ref[1] == 1
    out_ref[:, 0:E] = jnp.where(left, mine, other)
    out_ref[:, E : 2 * E] = jnp.where(left, other, mine)


def last_rows(flags, edge, Y, own, near, cross):
    return pl.pallas_call(
        last_kernel,
        out_shape=jax.ShapeDtypeStruct((Y.shape[0], 2 * own.shape[0]), F32),
        in_specs=[SCALAR] + [WHOLE] * 5,
        out_specs=WHOLE,
        compiler_params=limit(16),
        name="last_rows",
    )(flags, edge, Y, own, near, cross)


def flipped(block, axis, mask):
    return lax.ppermute(block, axis, [(i, i ^ mask) for i in range(lax.axis_size(axis))])


def ordered(parts, index):
    low = (index & 1) == 1
    p0, p1 = jnp.where(low, parts[1], parts[0]), jnp.where(low, parts[0], parts[1])
    p2, p3 = jnp.where(low, parts[3], parts[2]), jnp.where(low, parts[2], parts[3])
    high = (index & 2) == 2
    return [jnp.where(high, p2, p0), jnp.where(high, p3, p1), jnp.where(high, p0, p2), jnp.where(high, p1, p3)]


def gathered_cells(classes):
    E = classes.shape[1]
    x = lax.axis_index("col")
    slab = lax.axis_index("slab")
    core, quarter = slab & 1, slab >> 1 & 1
    parts = [classes] + [flipped(classes, "col", k) for k in (1, 2, 3)]
    strip = jnp.concatenate(ordered(parts, x), axis=0)

    def pair(low, high, second):
        return jnp.concatenate([jnp.where(second, high, low), jnp.where(second, low, high)], axis=0)

    def share(block, index, length):
        return lax.dynamic_slice_in_dim(block, index * length, length, axis=1)

    upper = core == 1
    strip = pair(share(strip, core, E // 2), flipped(share(strip, 1 - core, E // 2), "slab", 1), upper)
    place = 2 * (x >> 1) + ((x ^ (x >> 1)) & 1)
    strip = jnp.stack([share(strip, k * 4 + place, N) for k in (0, 1)])
    mine = lax.dynamic_index_in_dim(strip, quarter, 0, keepdims=False)
    other = lax.dynamic_index_in_dim(strip, 1 - quarter, 0, keepdims=False)
    return pair(mine, flipped(other, "slab", 2), quarter == 1)


def local(classes, across_coeff, along_coeff):
    E = classes.shape[1]
    slab, col = lax.axis_index("slab"), lax.axis_index("col")
    core = slab & 1

    def bit(index, mask):
        return jnp.where((index & mask) != 0, 1, 0).astype(jnp.int32).reshape(1)

    left = bit(slab ^ 16, 16)
    share = 2 * E // (lax.axis_size("slab") * lax.axis_size("col"))
    row = (((slab & 15) * lax.axis_size("col") + col) * share).astype(jnp.int32).reshape(1)
    seconds = [bit(col ^ (col >> 1), 1), bit(slab, 4), bit(col, 2), bit(slab, 8), bit(slab, 2), bit(slab, 1)]

    def flags(k):
        return jnp.concatenate([seconds[k], left, row, seconds[min(k + 1, 5)]])

    swaps = [("col", 1), ("slab", 4), ("col", 3), ("slab", 8), ("slab", 2), ("slab", 1)]
    coeffs = jnp.stack([across_coeff, along_coeff])
    cells = gathered_cells(classes)
    pieces = None
    m, seam = block_map(seconds[0], jnp.concatenate([cells] * 4, axis=1), coeffs)
    sent = m
    sizes = [(32, 32), (32, 64), (64, 64), (64, 128), (128, 128)]
    for k, (s, x) in enumerate(sizes):
        G = None
        if k >= 3:
            other = flipped(seam, *swaps[k])
            if k == 4:
                sent, other = lax.optimization_barrier((sent, other))
            G = inverse(seam, other, x)
        recv = flipped(sent, *swaps[k])
        now = flags(k)
        if k == 0:
            held, m = lax.optimization_barrier((classes, m))
            rows, cols = piece_vectors(held, coeffs)
            now, rows = lax.optimization_barrier((now, rows))
        if k in (1, 4):
            rows, _ = lax.optimization_barrier((rows, G if k == 4 else seam))
            pieces = piece_part(rows, cols, pieces, 0 if k == 1 else 4, 4)
            now, pieces = lax.optimization_barrier((now, pieces))
        onward = (s * 2, False) if k < 4 else (x, True)
        if k == 3:
            onward = (x, False)
        order = {3: "swap", 4: "swapped"}.get(k, "")
        out = merged(now, m, recv, G, s, x, onward, flip=k < 4, packed_out=k > 0, order=order)
        m, seam, sent = out if k > 0 else (out[0], out[1], out[0])
    other = flipped(seam, *swaps[5])
    recv = flipped(sent, *swaps[5])
    G = inverse(seam, other, 128)
    half_map, seam, reach, edge, W, X = merged(flags(5), m, recv, G, 256, 128, order="swapped", mib=32)
    both = flags(5)
    other = flipped(seam, "slab", 16)
    inner, sent = inner_map(both, half_map, W, X)
    near = flipped(sent, "slab", 16)
    G = inverse(seam, other, 0)
    reach, edge = coupling(both, reach, edge, W, X)
    half = E // 2
    part = lax.dynamic_slice_in_dim(reach, core * half, half, 0)
    near, edge, G, part = lax.optimization_barrier((near, edge, G, part))
    part_recv = flipped(part, "slab", 16)
    S, R, Q = interface(both, inner, near, flipped(near, "slab", 1), edge, G)
    part, Q = lax.optimization_barrier((part_recv, Q))
    Y = solve(S, R, Q)
    root_rows = last_rows(both, edge, Y, reach, part, flipped(part, "slab", 1))
    return (pieces.reshape(2 * E, 2 * E), root_rows)


def solution(mesh):
    placed = P(("slab", "col"), None)
    return jax.shard_map(
        local,
        mesh=mesh,
        in_specs=(placed, P(), P()),
        out_specs=(placed, placed),
        check_vma=False,
    )
```
